32 devices in a mesh: blk: 4 (over y, x), shard: 8 (over z, core).
Axes of the slice: x: 2, y: 2, z: 4, core: 2. Of those that a mesh axis runs over, the one named last changes fastest.
Arguments:
- activations: bfloat16 [12288, 8192], P(('blk', 'shard')), may hold values from -6 to 6
- cotangent: bfloat16 [12288, 1024], P(('blk', 'shard')), may hold values from -6 to 6
- kv_weight: bfloat16 [8192, 1024], P('shard', 'blk'), may hold values from -0.0625 to 0.0625
Outputs:
- key_values: bfloat16 [12288, 1024], P(('blk', 'shard'))
- grad_input: bfloat16 [12288, 8192], P(('blk', 'shard'))
- grad_weight: bfloat16 [8192, 1024], P('shard', 'blk')
The draws below stay inside these ranges and needn't reach their ends.
All inputs are finite; a program needn't handle non-finite values.
Results may differ from the reference program's by a relative error of at most 0.014.
Values may be sent and summed in bfloat16 or wider, within the bound.
No kernel may reach another device: no remote copies, remote signals or barrier semaphores. Data moves between devices by JAX's collectives and lax.ppermute only.
A program may use at most 256 MiB of HBM per device.

```python
import jax
import jax.numpy as jnp
from jax import lax

D = 8192
TOK_DEV = 384
KV = 1024
TOKENS = 12288


def raised(drawn, own_key, source, target, parts, factor):
    def block_of(dim):
        return (jnp.arange(drawn.shape[dim]) // (drawn.shape[dim] // parts)).reshape((-1,) + (1,) * (drawn.ndim - 1 - dim))

    one_side = jax.random.permutation(own_key, parts)[block_of(target)]
    far = (block_of(target) + parts // 2) % parts
    return jnp.where((block_of(source) == one_side) | (block_of(source) == far), factor * drawn, drawn)


def level_of(own_key, extent, shards, smallest, top_value):
    loudness, own = 1.0, jax.random.fold_in(own_key, 6)
    for axis_at, shards_of in shards:
        heights = jnp.exp(jax.random.uniform(jax.random.fold_in(own, axis_at), (shards_of,), jnp.float32, smallest / len(shards), top_value / len(shards)))
        loudness = loudness * jnp.repeat(heights, extent[axis_at] // shards_of).reshape([-1 if axis == axis_at else 1 for axis in range(len(extent))])
    return loudness


def scatter_about(own_key, dims, spread, limit, pieces=(), kind=jnp.bfloat16):
    array = jax.random.normal(own_key, dims, jnp.float32) * spread
    if len(pieces) > 0:
        array = level_of(own_key, dims, pieces, -0.22, 0.18) * array
    return jnp.clip(array, min=-limit, max=limit).astype(kind)


def heavy_noise(rng, dims, deviation, most, pieces, heavy, kind=jnp.bfloat16):
    array = deviation * jax.random.normal(rng, dims, jnp.float32)
    if pieces:
        array = array * level_of(rng, dims, pieces, -0.22, 0.18)
    return jnp.clip(raised(array, jax.random.fold_in(rng, 3), *heavy), -most, most).astype(kind)


def setup_inputs(seed: int = 0) -> dict:
    key_of = jax.random.split(jax.random.key(seed), 4)
    return {
        "activations": heavy_noise(key_of[0], (TOKENS, D), 1.0, 6.0, ((0, 32),), (0, 1, 32, 2.75)),
        "cotangent": scatter_about(key_of[1], (TOKENS, KV), 1.0, 6.0, ((0, 32),)),
        "kv_weight": scatter_about(key_of[2], (D, KV), D ** -0.5, 0.0625, ((0, 8), (1, 4))),
    }


def reference(activations, cotangent, kv_weight):
    weight32 = kv_weight.astype(jnp.float32)
    groups = activations.shape[0] // TOK_DEV
    act_groups = activations.reshape(groups, TOK_DEV, activations.shape[1])
    cot_groups = cotangent.reshape(groups, TOK_DEV, cotangent.shape[1])

    def one_group(total, pair):
        inputs, grads = pair
        inputs32 = inputs.astype(jnp.float32)
        grads32 = grads.astype(jnp.float32)
        projected = jnp.dot(inputs32, weight32, precision=lax.Precision.HIGHEST).astype(jnp.bfloat16)
        back_part = jnp.dot(grads32, weight32.T, precision=lax.Precision.HIGHEST).astype(jnp.bfloat16)
        partial_sum = jnp.dot(inputs32.T, grads32, precision=lax.Precision.HIGHEST)
        rounded = lax.optimization_barrier(partial_sum.astype(jnp.bfloat16))
        return (total + rounded.astype(jnp.float32), (projected, back_part))
    start = jnp.zeros(kv_weight.shape, jnp.float32)
    total, (projected, back_part) = lax.scan(one_group, start, (act_groups, cot_groups))
    key_values = projected.reshape(cotangent.shape)
    grad_input = back_part.reshape(activations.shape)
    grad_weight = (total / jnp.sqrt(jnp.float32(TOKENS))).astype(jnp.bfloat16)
    return (key_values, grad_input, grad_weight)
```

```python
import math

import jax
import jax.numpy as jnp
from jax import lax
from jax.sharding import Mesh, PartitionSpec as P


def swapped(array):
    return lax.ppermute(array, "core", [(0, 1), (1, 0)])


def local(activations, cotangent, kv_weight):
    blocks, chips = lax.axis_size("blk"), lax.axis_size("chip")
    core = lax.axis_index("core")
    tokens, features = activations.shape
    rows, cols = kv_weight.shape
    columns = cotangent.shape[1]
    by_core = activations.reshape(tokens, chips, 2, rows)
    mine = lax.dynamic_index_in_dim(by_core, core, 2, keepdims=False)
    other = lax.dynamic_index_in_dim(by_core, 1 - core, 2, keepdims=False)
    acts = jnp.concatenate([mine, swapped(other)], 0)
    cots = jnp.concatenate([cotangent, swapped(cotangent)], 0)
    weight = lax.all_gather(kv_weight, ("blk", "chip"), axis=0, tiled=False)
    weight = weight.reshape(blocks, chips, rows, cols)
    terms = jnp.einsum(
        "tzr,tbc->bzrc", acts, cots.reshape(2 * tokens, blocks, cols),
        preferred_element_type=jnp.float32,
    ).astype(jnp.bfloat16).reshape(blocks * chips, rows, cols)
    total = lax.psum_scatter(terms, ("blk", "chip"), scatter_dimension=0, tiled=False)
    count = tokens * blocks * chips * 2
    grad_weight = (total.astype(jnp.float32) * (1.0 / math.sqrt(count))).astype(jnp.bfloat16)

    full = weight.transpose(1, 2, 0, 3).reshape(chips * rows, columns)
    keys = jnp.dot(acts.reshape(2 * tokens, chips * rows), full, preferred_element_type=jnp.float32)
    key_values = (keys[:tokens] + swapped(keys[tokens:])).astype(jnp.bfloat16)
    inputs = lax.dot_general(
        cots, full, (((1,), (1,)), ((), ())), preferred_element_type=jnp.float32
    ).astype(jnp.bfloat16).reshape(2 * tokens, chips, rows)
    near, far = inputs[:tokens], swapped(inputs[tokens:])
    low = jnp.where(core == 0, near, far)
    high = jnp.where(core == 0, far, near)
    grad_input = jnp.stack([low, high], 2).reshape(tokens, features)
    return (key_values, grad_input, grad_weight)


def solution(mesh):
    blocks, shards = mesh.shape["blk"], mesh.shape["shard"]
    split = Mesh(mesh.devices.reshape(blocks, shards // 2, 2), ("blk", "chip", "core"))
    by_token = P(("blk", "chip", "core"), None)
    by_piece = P(("chip", "core"), "blk")
    return jax.shard_map(
        local,
        mesh=split,
        in_specs=(by_token, by_token, by_piece),
        out_specs=(by_token, by_token, by_piece),
        check_vma=False,
    )
```

```python
import math

import jax
import jax.numpy as jnp
from jax import lax
from jax.experimental import pallas as pl
from jax.experimental.pallas import tpu as pltpu
from jax.sharding import Mesh, PartitionSpec as P

F32, BF16 = jnp.float32, jnp.bfloat16
AXES = ("blk", "chip", "core")
HALVES = 2


def hops(move):
    pairs = []
    for blk in range(4):
        for z in range(4):
            for core in range(2):
                to = move(blk, z, core)
                if to is not None:
                    pairs.append(((blk * 4 + z) * 2 + core, (to[0] * 4 + to[1]) * 2 + to[2]))
    return pairs


def middle(z):
    return z in (1, 2)


SWAP = hops(lambda b, z, c: (b, z, 1 - c))
FLIP_A = hops(lambda b, z, c: (b ^ (1 + c), z, c))
FLIP_B = hops(lambda b, z, c: (b ^ (2 - c), z, c))
FLIP_B_MID = hops(lambda b, z, c: (b ^ (2 - c), z, c) if middle(z) else None)
FLIP_B_END = hops(lambda b, z, c: (b ^ (2 - c), z, c) if not middle(z) else None)
PAIR = hops(lambda b, z, c: (b, z ^ 1, c))
MID = hops(lambda b, z, c: (b, z ^ 3, c) if middle(z) else None)
OUT = hops(lambda b, z, c: (b, z ^ 1, c) if middle(z) else None)
IN = hops(lambda b, z, c: (b, z ^ 1, c) if not middle(z) else None)


def sent(array, pairs):
    return lax.ppermute(array, AXES, pairs)


def column_block(place, a, b):
    core = place[1]
    return place[2] ^ (a * (1 + core)) ^ (b * (2 - core))


def pack_kernel(place, acts, *outs):
    rows = acts.shape[1] // HALVES
    for half in range(HALVES):
        outs[half][...] = acts[:, half * rows : (half + 1) * rows]


def packed(place, activations, rows):
    tokens = activations.shape[0]
    return pl.pallas_call(
        pack_kernel,
        grid_spec=pltpu.PrefetchScalarGridSpec(
            num_scalar_prefetch=1,
            grid=(4,),
            in_specs=[pl.BlockSpec((tokens, rows), lambda k, s: (0, 2 * (s[0] ^ k) + 1 - s[1]))],
            out_specs=[pl.BlockSpec((tokens, rows // HALVES), lambda k, s: (0, k))] * HALVES,
        ),
        out_shape=[jax.ShapeDtypeStruct((tokens, 4 * rows // HALVES), BF16)] * HALVES,
        cost_estimate=pl.CostEstimate(flops=0, bytes_accessed=16 * tokens * rows, transcendentals=0),
        name="pack",
    )(place, activations)


def term_kernel(place, mine, other, cot_mine, cot_other, send, keep):
    tall = jnp.concatenate([mine[...], other[...]], 0).T
    cols = cot_mine.shape[1] // 4
    for b, out in ((1, send), (0, keep)):
        for a in (0, 1):
            at = pl.ds(pl.multiple_of(column_block(place, a, b) * cols, cols), cols)
            cot = jnp.concatenate([cot_mine[:, at], cot_other[:, at]], 0)
            out[0, a] = jnp.dot(tall, cot, preferred_element_type=F32).astype(BF16)


def terms(place, half, activations, other, cot_mine, cot_other, rows):
    tokens, columns = cot_mine.shape
    part, cols = rows // HALVES, columns // 4
    whole = pl.BlockSpec((tokens, columns), lambda k, s: (0, 0))
    piece = pl.BlockSpec((1, 2, part, cols), lambda k, s: (k, 0, 0, 0))
    return pl.pallas_call(
        term_kernel,
        grid_spec=pltpu.PrefetchScalarGridSpec(
            num_scalar_prefetch=1,
            grid=(4,),
            in_specs=[
                pl.BlockSpec(
                    (tokens, part), lambda k, s: (0, HALVES * (2 * (s[0] ^ k) + s[1]) + half)
                ),
                pl.BlockSpec((tokens, part), lambda k, s: (0, k)),
                whole,
                whole,
            ],
            out_specs=[piece, piece],
        ),
        out_shape=[jax.ShapeDtypeStruct((4, 2, part, cols), BF16)] * 2,
        cost_estimate=pl.CostEstimate(
            flops=16 * tokens * part * columns,
            bytes_accessed=16 * tokens * part + 8 * part * columns,
            transcendentals=0,
        ),
        name="terms",
    )(place, activations, other, cot_mine, cot_other)


def project_kernel(place, *refs):
    acts, cot_mine, cot_other = refs[:1 + HALVES], refs[1 + HALVES], refs[2 + HALVES]
    pieces, outs = refs[3 + HALVES : -4], refs[-4:]
    near, far, keys_near, keys_far = outs
    cols = cot_mine.shape[1] // 4
    tokens = cot_mine.shape[0]
    tall = jnp.concatenate(
        [acts[0][...], jnp.concatenate([act[...] for act in acts[1:]], 1)], 0
    )
    count = len(pieces) // 2
    total = None
    for b in (0, 1):
        for a in (0, 1):
            weight = pieces[b * count][a]
            for extra in pieces[b * count + 1 : (b + 1) * count]:
                weight = weight + extra[a]
            at = pl.ds(pl.multiple_of(column_block(place, a, b) * cols, cols), cols)
            cot = jnp.concatenate([cot_mine[:, at], cot_other[:, at]], 0)
            term = lax.dot_general(
                cot, weight, (((1,), (1,)), ((), ())), preferred_element_type=F32
            )
            total = term if total is None else total + term
            keys = jnp.dot(tall, weight, preferred_element_type=F32)
            keys_near[:, at] = keys[:tokens]
            keys_far[:, at] = keys[tokens:]
    near[...] = total[:tokens].astype(BF16)
    far[...] = total[tokens:].astype(BF16)


def projected(place, k, activations, others, cot_mine, cot_other, pieces):
    tokens, columns = cot_mine.shape
    rows, cols = pieces[0].shape[1:]
    whole = pl.BlockSpec((tokens, columns), lambda i, s: (0, 0))
    wide = pl.BlockSpec((tokens, rows), lambda i, s: (0, 0))
    return pl.pallas_call(
        project_kernel,
        grid_spec=pltpu.PrefetchScalarGridSpec(
            num_scalar_prefetch=1,
            grid=(1,),
            in_specs=[
                pl.BlockSpec((tokens, rows), lambda i, s: (0, 2 * (s[0] ^ k) + s[1])),
                *[pl.BlockSpec((tokens, rows // HALVES), lambda i, s: (0, k))] * HALVES,
                whole,
                whole,
                *[pl.BlockSpec((2, rows, cols), lambda i, s: (0, 0, 0))] * len(pieces),
            ],
            out_specs=[wide, wide, whole, whole],
        ),
        out_shape=[jax.ShapeDtypeStruct((tokens, rows), BF16)] * 2
        + [jax.ShapeDtypeStruct((tokens, columns), F32)] * 2,
        compiler_params=pltpu.CompilerParams(vmem_limit_bytes=56 * 2**20),
        cost_estimate=pl.CostEstimate(
            flops=8 * tokens * rows * columns,
            bytes_accessed=8 * tokens * rows + 2 * rows * columns + 8 * tokens * columns,
            transcendentals=0,
        ),
        name="project",
    )(place, activations, *others, cot_mine, cot_other, *pieces)


def lay_kernel(place, *refs):
    out = refs[-1]
    at = pl.program_id(0)
    z, core = lax.div(at, 2), lax.rem(at, 2)
    for k in range(4):
        for side in range(2):

            @pl.when(((z ^ place[0]) == k) & ((core ^ place[1]) == side))
            def _():
                out[...] = refs[4 * side + k][...]


def laid(place, near, far):
    tokens, rows = near[0].shape
    whole = pl.BlockSpec((tokens, rows), lambda i, s: (0, 0))
    return pl.pallas_call(
        lay_kernel,
        grid_spec=pltpu.PrefetchScalarGridSpec(
            num_scalar_prefetch=1,
            grid=(8,),
            in_specs=[whole] * 8,
            out_specs=pl.BlockSpec((tokens, rows), lambda i, s: (0, i)),
        ),
        out_shape=jax.ShapeDtypeStruct((tokens, 8 * rows), BF16),
        cost_estimate=pl.CostEstimate(flops=0, bytes_accessed=32 * tokens * rows, transcendentals=0),
        compiler_params=pltpu.CompilerParams(vmem_limit_bytes=40 * 2**20),
        name="lay",
    )(place, *near, *far)


def added(*arrays):
    total = arrays[0].astype(F32)
    for array in arrays[1:]:
        total = total + array.astype(F32)
    return total


def gathered(weight):
    base = jnp.stack([weight, sent(weight, FLIP_A)])
    one = sent(base, PAIR)
    mid = sent(base, MID)
    mid_far = sent(one, MID)
    end = sent(mid, OUT)
    end_far = sent(mid_far, OUT)
    return (
        (base, sent(base, FLIP_B)),
        (one, sent(one, FLIP_B)),
        (mid_far, end, sent(mid_far, FLIP_B_MID), sent(end, FLIP_B_END)),
        (mid, end_far, sent(mid, FLIP_B_MID), sent(end_far, FLIP_B_END)),
    )


def scattered(send, keep):
    got = sent(send, FLIP_B)
    sums = [added(keep[k], got[k]) for k in range(4)]
    far = sent(sums[3].astype(BF16), IN)
    near = sent(sums[2].astype(BF16), IN)
    mid_far = sent(added(sums[2], far).astype(BF16), MID)
    mid = sent(added(sums[3], near).astype(BF16), MID)
    one = sent(added(sums[1], mid_far).astype(BF16), PAIR)
    last = added(sums[0], mid, one)
    return last[0] + sent(last[1].astype(BF16), FLIP_A).astype(F32)


def by_hops(activations, cotangent, kv_weight):
    rows = kv_weight.shape[0]
    tokens = activations.shape[0]
    place = jnp.stack([lax.axis_index(name) for name in ("chip", "core", "blk")]).astype(jnp.int32)
    others = [sent(part, SWAP) for part in packed(place, activations, rows)]
    cot_other = sent(cotangent, SWAP)
    weights = gathered(kv_weight)
    halves = []
    for half in range(HALVES):
        send, keep = terms(place, half, activations, others[half], cotangent, cot_other, rows)
        halves.append(scattered(send, keep))
    grad_weight = (jnp.concatenate(halves, 0) * (1.0 / math.sqrt(32 * tokens))).astype(BF16)
    near, far, keys_near, keys_far = zip(
        *[
            projected(place, k, activations, others, cotangent, cot_other, weights[k])
            for k in range(4)
        ]
    )
    grad_input = laid(place, near, [sent(part, SWAP) for part in far])
    key_values = (added(*keys_near) + sent(added(*keys_far), SWAP)).astype(BF16)
    return (key_values, grad_input, grad_weight)


def swapped(array):
    return lax.ppermute(array, "core", [(0, 1), (1, 0)])


def by_collectives(activations, cotangent, kv_weight):
    blocks, chips = lax.axis_size("blk"), lax.axis_size("chip")
    core = lax.axis_index("core")
    tokens, features = activations.shape
    rows, cols = kv_weight.shape
    columns = cotangent.shape[1]
    by_core = activations.reshape(tokens, chips, 2, rows)
    mine = lax.dynamic_index_in_dim(by_core, core, 2, keepdims=False)
    other = lax.dynamic_index_in_dim(by_core, 1 - core, 2, keepdims=False)
    acts = jnp.concatenate([mine, swapped(other)], 0)
    cots = jnp.concatenate([cotangent, swapped(cotangent)], 0)
    weight = lax.all_gather(kv_weight, ("blk", "chip"), axis=0, tiled=False)
    weight = weight.reshape(blocks, chips, rows, cols)
    parts = jnp.einsum(
        "tzr,tbc->bzrc", acts, cots.reshape(2 * tokens, blocks, cols), preferred_element_type=F32
    ).astype(BF16).reshape(blocks * chips, rows, cols)
    total = lax.psum_scatter(parts, ("blk", "chip"), scatter_dimension=0, tiled=False)
    count = tokens * blocks * chips * 2
    grad_weight = (total.astype(F32) * (1.0 / math.sqrt(count))).astype(BF16)
    full = weight.transpose(1, 2, 0, 3).reshape(chips * rows, columns)
    keys = jnp.dot(acts.reshape(2 * tokens, chips * rows), full, preferred_element_type=F32)
    key_values = (keys[:tokens] + swapped(keys[tokens:])).astype(BF16)
    inputs = lax.dot_general(
        cots, full, (((1,), (1,)), ((), ())), preferred_element_type=F32
    ).astype(BF16).reshape(2 * tokens, chips, rows)
    near, far = inputs[:tokens], swapped(inputs[tokens:])
    low = jnp.where(core == 0, near, far)
    high = jnp.where(core == 0, far, near)
    grad_input = jnp.stack([low, high], 2).reshape(tokens, features)
    return (key_values, grad_input, grad_weight)


def solution(mesh):
    blocks, shards = mesh.shape["blk"], mesh.shape["shard"]
    split = Mesh(mesh.devices.reshape(blocks, shards // 2, 2), AXES)
    by_token = P(AXES, None)
    by_piece = P(("chip", "core"), "blk")
    return jax.shard_map(
        by_hops if (blocks, shards) == (4, 8) else by_collectives,
        mesh=split,
        in_specs=(by_token, by_token, by_piece),
        out_specs=(by_token, by_token, by_piece),
        check_vma=False,
    )
```

```python
import math

import jax
import jax.numpy as jnp
from jax import lax
from jax.experimental import pallas as pl
from jax.experimental.pallas import tpu as pltpu
from jax.sharding import Mesh, PartitionSpec as P

F32, BF16 = jnp.float32, jnp.bfloat16
AXES = ("blk", "chip", "core")
HALVES = 2
SHRINK = 1000


def hops(move):
    pairs = []
    for blk in range(4):
        for z in range(4):
            for core in range(2):
                to = move(blk, z, core)
                if to is not None:
                    pairs.append(((blk * 4 + z) * 2 + core, (to[0] * 4 + to[1]) * 2 + to[2]))
    return pairs


def middle(z):
    return z in (1, 2)


SWAP = hops(lambda b, z, c: (b, z, 1 - c))
FLIP_A = hops(lambda b, z, c: (b ^ (1 + c), z, c))
FLIP_B = hops(lambda b, z, c: (b ^ (2 - c), z, c))
FLIP_B_MID = hops(lambda b, z, c: (b ^ (2 - c), z, c) if middle(z) else None)
FLIP_B_END = hops(lambda b, z, c: (b ^ (2 - c), z, c) if not middle(z) else None)
PAIR = hops(lambda b, z, c: (b, z ^ 1, c))
MID = hops(lambda b, z, c: (b, z ^ 3, c) if middle(z) else None)
OUT = hops(lambda b, z, c: (b, z ^ 1, c) if middle(z) else None)
IN = hops(lambda b, z, c: (b, z ^ 1, c) if not middle(z) else None)


def sent(array, pairs):
    return lax.ppermute(array, AXES, pairs)


def column_block(place, a, b):
    core = place[1]
    return place[2] ^ (a * (1 + core)) ^ (b * (2 - core))


def cost(flops, moved):
    return pl.CostEstimate(flops=flops // SHRINK, bytes_accessed=moved // SHRINK, transcendentals=0)


def pack_kernel(place, acts, *outs):
    rows = acts.shape[1] // HALVES
    for half in range(HALVES):
        outs[half][...] = acts[:, half * rows : (half + 1) * rows]


def packed(place, activations, rows):
    tokens = activations.shape[0]
    return pl.pallas_call(
        pack_kernel,
        grid_spec=pltpu.PrefetchScalarGridSpec(
            num_scalar_prefetch=1,
            grid=(4,),
            in_specs=[pl.BlockSpec((tokens, rows), lambda k, s: (0, 2 * (s[0] ^ k) + 1 - s[1]))],
            out_specs=[pl.BlockSpec((tokens, rows // HALVES), lambda k, s: (0, k))] * HALVES,
        ),
        out_shape=[jax.ShapeDtypeStruct((tokens, 4 * rows // HALVES), BF16)] * HALVES,
        cost_estimate=cost(0, 16 * tokens * rows),
        name="pack",
    )(place, activations)


def term_kernel(place, mine, other, cot_mine, cot_other, send, keep, turned):
    tokens, cols = cot_mine.shape[0], cot_mine.shape[1] // 4

    @pl.when(pl.program_id(0) == 0)
    def _():
        for b in (0, 1):
            for a in (0, 1):
                at = pl.ds(pl.multiple_of(column_block(place, a, b) * cols, cols), cols)
                to = slice((2 * b + a) * cols, (2 * b + a + 1) * cols)
                turned[to, :tokens] = cot_mine[:, at].T
                turned[to, tokens:] = cot_other[:, at].T

    tall = jnp.concatenate([mine[...], other[...]], 0)
    for b, out in ((1, send), (0, keep)):
        part = jnp.dot(
            turned[2 * b * cols : (2 * b + 2) * cols], tall, preferred_element_type=F32
        ).astype(BF16)
        out[...] = part.reshape(out.shape)


def terms(place, half, activations, other, cot_mine, cot_other, rows):
    tokens, columns = cot_mine.shape
    part, cols = rows // HALVES, columns // 4
    whole = pl.BlockSpec((tokens, columns), lambda k, s: (0, 0))
    piece = pl.BlockSpec((1, 2, cols, part), lambda k, s: (k, 0, 0, 0))
    return pl.pallas_call(
        term_kernel,
        grid_spec=pltpu.PrefetchScalarGridSpec(
            num_scalar_prefetch=1,
            grid=(4,),
            in_specs=[
                pl.BlockSpec(
                    (tokens, part), lambda k, s: (0, HALVES * (2 * (s[0] ^ k) + s[1]) + half)
                ),
                pl.BlockSpec((tokens, part), lambda k, s: (0, k)),
                whole,
                whole,
            ],
            out_specs=[piece, piece],
            scratch_shapes=[pltpu.VMEM((columns, 2 * tokens), BF16)],
        ),
        out_shape=[jax.ShapeDtypeStruct((4, 2, cols, part), BF16)] * 2,
        compiler_params=pltpu.CompilerParams(vmem_limit_bytes=24 * 2**20),
        cost_estimate=cost(16 * tokens * part * columns, 16 * tokens * part + 8 * part * columns),
        name="terms",
    )(place, activations, other, cot_mine, cot_other)


def project_kernel(place, *refs, counts, last):
    near, far, *keys = refs[-6 if last else -5 : -2]
    if last:
        near, far, *keys = refs[-6:-2]
    acc, cots = refs[-2:]
    acts, others, cot_mine, cot_other = refs[0], refs[1 : 1 + HALVES], *refs[1 + HALVES : 3 + HALVES]
    pieces = refs[3 + HALVES : 3 + HALVES + sum(counts)]
    tokens, cols = cot_mine.shape[0], cot_mine.shape[1] // 4
    group, tile = pl.program_id(0), pl.program_id(1)
    blocks = [
        (slice((2 * b + a) * cols, (2 * b + a + 1) * cols),
         pl.ds(pl.multiple_of(column_block(place, a, b) * cols, cols), cols))
        for b in (0, 1) for a in (0, 1)
    ]

    @pl.when((group == 0) & (tile == 0))
    def _():
        for to, at in blocks:
            cots[:tokens, to] = cot_mine[:, at]
            cots[tokens:, to] = cot_other[:, at]
        if last:
            acc[...] = refs[3 + HALVES + sum(counts)][...]
        else:
            acc[...] = jnp.zeros_like(acc)

    for at_group in range(len(counts)):
        start = sum(counts[:at_group])
        mine = pieces[start : start + counts[at_group]]
        for half in range(HALVES):

            @pl.when((group == at_group) & (tile == half))
            def _():
                parts = []
                for b in (0, 1):
                    some = mine[b * len(mine) // 2 : (b + 1) * len(mine) // 2]
                    for a in (0, 1):
                        part = some[0][a]
                        for extra in some[1:]:
                            part = part + extra[a]
                        parts.append(part)
                weight = jnp.concatenate(parts, 1)
                tall = jnp.concatenate([acts[...], others[half][...]], 0)
                acc[...] += jnp.dot(tall, weight, preferred_element_type=F32)
                total = lax.dot_general(
                    cots[...], weight, (((1,), (1,)), ((), ())), preferred_element_type=F32
                ).astype(BF16)
                near[...] = total[:tokens]
                far[...] = total[tokens:]

    @pl.when((group == len(counts) - 1) & (tile == HALVES - 1))
    def _():
        if last:
            for to, at in blocks:
                keys[0][:, at] = acc[:tokens, to]
                keys[1][:, at] = acc[tokens:, to]
        else:
            keys[0][...] = acc[...]


def projected(place, offsets, activations, others, cot_mine, cot_other, pieces, prior=None):
    tokens, columns = cot_mine.shape
    rows, cols = pieces[0][0].shape[1:]
    part = rows // HALVES
    last = prior is not None
    whole = pl.BlockSpec((tokens, columns), lambda i, r, s: (0, 0))
    both = pl.BlockSpec((2 * tokens, columns), lambda i, r, s: (0, 0))
    first, step = offsets[0], offsets[1] - offsets[0]

    def held(at_group):
        return pl.BlockSpec(
            (2, part, cols),
            lambda i, r, s: (0, jnp.clip((i - at_group) * HALVES + r, 0, HALVES - 1), 0),
        )

    out = pl.BlockSpec((tokens, part), lambda i, r, s: (0, HALVES * i + r))
    wide = jax.ShapeDtypeStruct((tokens, len(offsets) * rows), BF16)
    one = jax.ShapeDtypeStruct((tokens, columns), F32)
    return pl.pallas_call(
        lambda *refs: project_kernel(*refs, counts=[len(p) for p in pieces], last=last),
        grid_spec=pltpu.PrefetchScalarGridSpec(
            num_scalar_prefetch=1,
            grid=(len(offsets), HALVES),
            in_specs=[
                pl.BlockSpec(
                    (tokens, part),
                    lambda i, r, s: (0, HALVES * (2 * (s[0] ^ (first + step * i)) + s[1]) + r),
                ),
                *[pl.BlockSpec((tokens, part), lambda i, r, s: (0, first + step * i))] * HALVES,
                whole,
                whole,
                *[held(i) for i in range(len(pieces)) for _ in pieces[i]],
                *([both] if last else []),
            ],
            out_specs=[out, out] + ([whole, whole] if last else [both]),
            scratch_shapes=[
                pltpu.VMEM((2 * tokens, columns), F32),
                pltpu.VMEM((2 * tokens, columns), BF16),
            ],
        ),
        out_shape=[wide, wide]
        + ([one, one] if last else [jax.ShapeDtypeStruct((2 * tokens, columns), F32)]),
        compiler_params=pltpu.CompilerParams(vmem_limit_bytes=48 * 2**20),
        cost_estimate=cost(
            8 * tokens * rows * columns * len(offsets),
            (8 * tokens * rows + 2 * rows * columns) * len(offsets) + 8 * tokens * columns,
        ),
        name="project",
    )(
        place, activations, *others, cot_mine, cot_other,
        *[piece for some in pieces for piece in some], *([prior] if last else []),
    )


def lay_kernel(place, *refs):
    out = refs[-1]
    at = pl.program_id(0)
    z, core = lax.div(at, 2), lax.rem(at, 2)
    for side in range(2):
        for group in range(2):

            @pl.when((((z ^ place[0]) >> 1) == group) & ((core ^ place[1]) == side))
            def _():
                out[...] = refs[2 * side + group][...]


def laid(place, near, far):
    tokens, rows = near[0].shape[0], near[0].shape[1] // 2
    piece = pl.BlockSpec((tokens, rows), lambda i, s: (0, (lax.div(i, 2) ^ s[0]) & 1))
    return pl.pallas_call(
        lay_kernel,
        grid_spec=pltpu.PrefetchScalarGridSpec(
            num_scalar_prefetch=1,
            grid=(8,),
            in_specs=[piece] * 4,
            out_specs=pl.BlockSpec((tokens, rows), lambda i, s: (0, i)),
        ),
        out_shape=jax.ShapeDtypeStruct((tokens, 8 * rows), BF16),
        cost_estimate=cost(0, 32 * tokens * rows),
        compiler_params=pltpu.CompilerParams(vmem_limit_bytes=24 * 2**20),
        name="lay",
    )(place, *near, *far)


def added(*arrays):
    total = arrays[0].astype(F32)
    for array in arrays[1:]:
        total = total + array.astype(F32)
    return total


def gathered(weight):
    base = jnp.stack([weight, sent(weight, FLIP_A)])
    one = sent(base, PAIR)
    mid = sent(base, MID)
    mid_far = sent(one, MID)
    end = sent(mid, OUT)
    end_far = sent(mid_far, OUT)
    return (
        (base, sent(base, FLIP_B)),
        (one, sent(one, FLIP_B)),
        (mid_far, end, sent(mid_far, FLIP_B_MID), sent(end, FLIP_B_END)),
        (mid, end_far, sent(mid, FLIP_B_MID), sent(end_far, FLIP_B_END)),
    )


def scattered(send, keep):
    got = sent(send, FLIP_B)
    sums = [added(keep[k], got[k]) for k in range(4)]
    far = sent(sums[3].astype(BF16), IN)
    near = sent(sums[2].astype(BF16), IN)
    mid_far = sent(added(sums[2], far).astype(BF16), MID)
    mid = sent(added(sums[3], near).astype(BF16), MID)
    one = sent(added(sums[1], mid_far).astype(BF16), PAIR)
    last = added(sums[0], mid, one)
    return last[0] + sent(last[1].astype(BF16), FLIP_A).astype(F32)


def by_hops(activations, cotangent, kv_weight):
    rows = kv_weight.shape[0]
    tokens = activations.shape[0]
    place = jnp.stack([lax.axis_index(name) for name in ("chip", "core", "blk")]).astype(jnp.int32)
    others = [sent(part, SWAP) for part in packed(place, activations, rows)]
    cot_other = sent(cotangent, SWAP)
    weights = gathered(kv_weight)
    halves = []
    for half in range(HALVES):
        send, keep = terms(place, half, activations, others[half], cotangent, cot_other, rows)
        halves.append(scattered(send, keep))
    grad_weight = (jnp.concatenate(halves, 1) * (1.0 / math.sqrt(32 * tokens))).astype(BF16).T
    shared = (activations, others, cotangent, cot_other)
    near, far, keys = projected(place, (0, 1), *shared, weights[:2])
    more, more_far, keys, keys_far = projected(place, (2, 3), *shared, weights[2:], keys)
    grad_input = laid(place, (near, more), (sent(far, SWAP), sent(more_far, SWAP)))
    key_values = (keys + sent(keys_far, SWAP)).astype(BF16)
    return (key_values, grad_input, grad_weight)


def swapped(array):
    return lax.ppermute(array, "core", [(0, 1), (1, 0)])


def by_collectives(activations, cotangent, kv_weight):
    blocks, chips = lax.axis_size("blk"), lax.axis_size("chip")
    core = lax.axis_index("core")
    tokens, features = activations.shape
    rows, cols = kv_weight.shape
    columns = cotangent.shape[1]
    by_core = activations.reshape(tokens, chips, 2, rows)
    mine = lax.dynamic_index_in_dim(by_core, core, 2, keepdims=False)
    other = lax.dynamic_index_in_dim(by_core, 1 - core, 2, keepdims=False)
    acts = jnp.concatenate([mine, swapped(other)], 0)
    cots = jnp.concatenate([cotangent, swapped(cotangent)], 0)
    weight = lax.all_gather(kv_weight, ("blk", "chip"), axis=0, tiled=False)
    weight = weight.reshape(blocks, chips, rows, cols)
    parts = jnp.einsum(
        "tzr,tbc->bzrc", acts, cots.reshape(2 * tokens, blocks, cols), preferred_element_type=F32
    ).astype(BF16).reshape(blocks * chips, rows, cols)
    total = lax.psum_scatter(parts, ("blk", "chip"), scatter_dimension=0, tiled=False)
    count = tokens * blocks * chips * 2
    grad_weight = (total.astype(F32) * (1.0 / math.sqrt(count))).astype(BF16)
    full = weight.transpose(1, 2, 0, 3).reshape(chips * rows, columns)
    keys = jnp.dot(acts.reshape(2 * tokens, chips * rows), full, preferred_element_type=F32)
    key_values = (keys[:tokens] + swapped(keys[tokens:])).astype(BF16)
    inputs = lax.dot_general(
        cots, full, (((1,), (1,)), ((), ())), preferred_element_type=F32
    ).astype(BF16).reshape(2 * tokens, chips, rows)
    near, far = inputs[:tokens], swapped(inputs[tokens:])
    low = jnp.where(core == 0, near, far)
    high = jnp.where(core == 0, far, near)
    grad_input = jnp.stack([low, high], 2).reshape(tokens, features)
    return (key_values, grad_input, grad_weight)


def solution(mesh):
    blocks, shards = mesh.shape["blk"], mesh.shape["shard"]
    split = Mesh(mesh.devices.reshape(blocks, shards // 2, 2), AXES)
    by_token = P(AXES, None)
    by_piece = P(("chip", "core"), "blk")
    return jax.shard_map(
        by_hops if (blocks, shards) == (4, 8) else by_collectives,
        mesh=split,
        in_specs=(by_token, by_token, by_piece),
        out_specs=(by_token, by_token, by_piece),
        check_vma=False,
    )
```

```python
import math

import jax
import jax.numpy as jnp
from jax import lax
from jax.experimental import pallas as pl
from jax.experimental.pallas import tpu as pltpu
from jax.sharding import Mesh, PartitionSpec as P

F32, BF16 = jnp.float32, jnp.bfloat16
AXES = ("blk", "chip", "core")
SHRINK = 1000


def hops(move):
    pairs = []
    for blk in range(4):
        for z in range(4):
            for core in range(2):
                to = move(blk, z, core)
                if to is not None:
                    pairs.append(((blk * 4 + z) * 2 + core, (to[0] * 4 + to[1]) * 2 + to[2]))
    return pairs


def middle(z):
    return z in (1, 2)


SWAP = hops(lambda b, z, c: (b, z, 1 - c))
FLIP_A = hops(lambda b, z, c: (b ^ (1 + c), z, c))
FLIP_B = hops(lambda b, z, c: (b ^ (2 - c), z, c))
PAIR = hops(lambda b, z, c: (b, z ^ 1, c))
MID = hops(lambda b, z, c: (b, z ^ 3, c) if middle(z) else None)
OUT = hops(lambda b, z, c: (b, z ^ 1, c) if middle(z) else None)
IN = hops(lambda b, z, c: (b, z ^ 1, c) if not middle(z) else None)


def after(array, *others):
    return lax.optimization_barrier((array, *others))[0]


def sent(array, pairs):
    return lax.ppermute(array, AXES, pairs)


def column_block(place, a, b):
    core = place[1]
    return place[2] ^ (a * (1 + core)) ^ (b * (2 - core))


def cost(flops, moved):
    return pl.CostEstimate(flops=flops // SHRINK, bytes_accessed=moved // SHRINK, transcendentals=0)


def pack_kernel(place, acts, out):
    out[...] = acts[...]


def packed(place, first, activations, rows):
    tokens = activations.shape[0]
    return pl.pallas_call(
        pack_kernel,
        grid_spec=pltpu.PrefetchScalarGridSpec(
            num_scalar_prefetch=1,
            grid=(2, 2),
            in_specs=[
                pl.BlockSpec(
                    (tokens, rows // 2),
                    lambda k, r, s: (0, 2 * (2 * (s[0] ^ (first + k)) + 1 - s[1]) + r),
                )
            ],
            out_specs=pl.BlockSpec((tokens, rows // 2), lambda k, r, s: (0, 2 * k + r)),
        ),
        out_shape=jax.ShapeDtypeStruct((tokens, 2 * rows), BF16),
        cost_estimate=cost(0, 8 * tokens * rows),
        name="pack",
    )(place, activations)


def term_kernel(place, mine, other, cot_mine, cot_other, *refs):
    tokens, cols = cot_mine.shape[0], cot_mine.shape[1] // 4
    turned = refs[-1]

    @pl.when((pl.program_id(0) == 0) & (pl.program_id(1) == 0))
    def _():
        for b in (0, 1):
            for a in (0, 1):
                at = pl.ds(pl.multiple_of(column_block(place, a, b) * cols, cols), cols)
                to = slice((2 * b + a) * cols, (2 * b + a + 1) * cols)
                turned[to, :tokens] = cot_mine[:, at].T
                turned[to, tokens:] = cot_other[:, at].T

    tall = jnp.concatenate([mine[...], other[...]], 0)
    for b in (0, 1):
        part = jnp.dot(
            turned[2 * b * cols : (2 * b + 2) * cols], tall, preferred_element_type=F32
        ).astype(BF16)
        for k in (0, 1):

            @pl.when(pl.program_id(0) == k)
            def _():
                refs[2 * b + k][...] = part.reshape(2, cols, part.shape[1])


def terms(place, first, activations, other, cot_mine, cot_other, rows):
    tokens, columns = cot_mine.shape
    part, cols = rows // 2, columns // 4
    whole = pl.BlockSpec((tokens, columns), lambda k, r, s: (0, 0))
    pieces = [
        pl.BlockSpec((2, cols, part), lambda k, r, s: (0, 0, jnp.where(k == 0, r, 1))),
        pl.BlockSpec((2, cols, part), lambda k, r, s: (0, 0, jnp.where(k == 0, 0, r))),
    ]
    return pl.pallas_call(
        term_kernel,
        grid_spec=pltpu.PrefetchScalarGridSpec(
            num_scalar_prefetch=1,
            grid=(2, 2),
            in_specs=[
                pl.BlockSpec(
                    (tokens, part),
                    lambda k, r, s: (0, 2 * (2 * (s[0] ^ (first + k)) + s[1]) + r),
                ),
                pl.BlockSpec((tokens, part), lambda k, r, s: (0, 2 * k + r)),
                whole,
                whole,
            ],
            out_specs=pieces * 2,
            scratch_shapes=[pltpu.VMEM((columns, 2 * tokens), BF16)],
        ),
        out_shape=[jax.ShapeDtypeStruct((2, cols, rows), BF16)] * 4,
        compiler_params=pltpu.CompilerParams(vmem_limit_bytes=28 * 2**20),
        cost_estimate=cost(16 * tokens * rows * columns, 8 * tokens * rows + 8 * rows * columns),
        name="terms",
    )(place, activations, other, cot_mine, cot_other)


def project_kernel(place, *refs, first, last):
    acts, other, cot_mine, cot_other, here, there = refs[:6]
    at_out = 6 if first else 8
    near, far, *keys = refs[at_out:-2]
    acc, cots = refs[-2:]
    tokens, cols = cot_mine.shape[0], cot_mine.shape[1] // 4
    tile = pl.program_id(0)
    blocks = [
        (
            slice((2 * b + a) * cols, (2 * b + a + 1) * cols),
            pl.ds(pl.multiple_of(column_block(place, a, b) * cols, cols), cols),
        )
        for b in (0, 1)
        for a in (0, 1)
    ]

    @pl.when(tile == 0)
    def _():
        for to, at in blocks:
            cots[:tokens, to] = cot_mine[:, at]
            cots[tokens:, to] = cot_other[:, at]

    weight = jnp.concatenate([here[0], here[1], there[0], there[1]], 1)
    tall = jnp.concatenate([acts[...], other[...]], 0)
    sums = jnp.dot(tall, weight, preferred_element_type=F32)

    @pl.when(tile == 0)
    def _():
        acc[...] = sums if first else refs[6][...] + sums

    @pl.when(tile > 0)
    def _():
        acc[...] += sums

    total = lax.dot_general(
        cots[...], weight, (((1,), (1,)), ((), ())), preferred_element_type=F32
    ).astype(BF16)
    near[...] = total[:tokens]
    far[...] = total[tokens:]

    @pl.when(tile == pl.num_programs(0) - 1)
    def _():
        if last:
            for to, at in blocks:
                keys[0][:, at] = acc[:tokens, to]
                keys[1][:, at] = acc[tokens:, to]
        else:
            keys[0][...] = acc[...]


def projected(place, k, activations, others, cot_mine, cot_other, here, there, so_far=None):
    tokens, columns = cot_mine.shape
    _, rows, cols = here.shape
    part = rows // 2
    first, last = k == 0, k == 3
    whole = pl.BlockSpec((tokens, columns), lambda r, s: (0, 0))
    both = pl.BlockSpec((2 * tokens, columns), lambda r, s: (0, 0))
    mine = pl.BlockSpec((tokens, part), lambda r, s: (0, 2 * (2 * (s[0] ^ k) + s[1]) + r))
    piece = pl.BlockSpec((2, part, cols), lambda r, s: (0, r, 0))
    one = jax.ShapeDtypeStruct((tokens, columns), F32)
    return pl.pallas_call(
        lambda *refs: project_kernel(*refs, first=first, last=last),
        grid_spec=pltpu.PrefetchScalarGridSpec(
            num_scalar_prefetch=1,
            grid=(2,),
            in_specs=[
                mine,
                pl.BlockSpec((tokens, part), lambda r, s: (0, 2 * (k % 2) + r)),
                whole,
                whole,
                piece,
                piece,
            ]
            + ([] if first else [both, pl.BlockSpec(memory_space=pl.ANY)]),
            out_specs=[mine, pl.BlockSpec((tokens, part), lambda r, s: (0, r))]
            + ([whole, whole] if last else [both]),
            scratch_shapes=[
                pltpu.VMEM((2 * tokens, columns), F32),
                pltpu.VMEM((2 * tokens, columns), BF16),
            ],
        ),
        out_shape=[
            jax.ShapeDtypeStruct(activations.shape, BF16),
            jax.ShapeDtypeStruct((tokens, rows), BF16),
        ]
        + ([one, one] if last else [jax.ShapeDtypeStruct((2 * tokens, columns), F32)]),
        input_output_aliases={} if first else {8: 0},
        compiler_params=pltpu.CompilerParams(vmem_limit_bytes=48 * 2**20),
        cost_estimate=cost(
            8 * tokens * rows * columns, 8 * tokens * rows + 2 * rows * columns + 8 * tokens * columns
        ),
        name="project",
    )(
        place, activations, others, cot_mine, cot_other, here, there,
        *([] if first else [so_far[1], so_far[0]]),
    )


def lay_kernel(place, *refs, count):
    for i in range(count):

        @pl.when(pl.program_id(0) == i)
        def _():
            refs[-1][...] = refs[i][...]


def laid(place, offsets, whole, far):
    tokens, rows = far[0].shape
    count, start = len(offsets), offsets[0]
    return pl.pallas_call(
        lambda *refs: lay_kernel(*refs, count=count),
        grid_spec=pltpu.PrefetchScalarGridSpec(
            num_scalar_prefetch=1,
            grid=(count, 2),
            in_specs=[
                pl.BlockSpec(
                    (tokens, rows // 2),
                    lambda i, r, s, n=n: (0, jnp.clip(2 * (i - n) + r, 0, 1)),
                )
                for n in range(count)
            ]
            + [pl.BlockSpec(memory_space=pl.ANY)],
            out_specs=pl.BlockSpec(
                (tokens, rows // 2),
                lambda i, r, s: (0, 2 * (2 * (s[0] ^ (start + i)) + 1 - s[1]) + r),
            ),
        ),
        out_shape=jax.ShapeDtypeStruct(whole.shape, BF16),
        input_output_aliases={1 + count: 0},
        cost_estimate=cost(0, 4 * count * tokens * rows),
        name="lay",
    )(place, *far, whole)


def added(*arrays):
    total = arrays[0].astype(F32)
    for array in arrays[1:]:
        total = total + array.astype(F32)
    return total


def by_hops(activations, cotangent, kv_weight):
    rows = kv_weight.shape[0]
    tokens = activations.shape[0]
    place = jnp.stack([lax.axis_index(name) for name in ("chip", "core", "blk")]).astype(jnp.int32)

    cot_other = sent(cotangent, SWAP)
    base = jnp.stack([kv_weight, sent(kv_weight, FLIP_A)])
    high = sent(packed(place, 2, after(activations, base), rows), SWAP)
    low = sent(packed(place, 0, after(activations, high), rows), SWAP)
    one, mid = sent(base, PAIR), sent(base, MID)
    base_b = sent(base, FLIP_B)

    shared = (cotangent, cot_other)
    keep2, keep3, send2, send3 = terms(place, 2, activations, high, *shared, rows)
    got3 = sent(after(send3, base), FLIP_B)
    got2 = sent(after(send2, base_b), FLIP_B)
    keep0, keep1, send0, send1 = terms(place, 0, after(activations, keep2), low, *shared, rows)
    so_far = projected(place, 0, after(activations, keep0), low, *shared, base, base_b)
    out0 = sent(so_far[1], SWAP)

    got1 = sent(after(send1, got3), FLIP_B)
    far = sent(after(added(keep3, got3).astype(BF16), one, mid), IN)
    two_mid = sent(one, MID)
    two_end = sent(mid, OUT)
    got0 = sent(after(send0, got2), FLIP_B)
    sum2 = added(keep2, got2)
    two = two_mid + two_end
    near = sent(after(sum2.astype(BF16), far, two), IN)
    mid_far = sent(added(keep2, got2, far).astype(BF16), MID)
    three_end = sent(two_mid, OUT)
    one_b = sent(after(one, got1), FLIP_B)
    two_b = sent(after(two, got0), FLIP_B)

    so_far = projected(place, 1, activations, low, *shared, one, one_b, (so_far[0], so_far[2]))
    out1 = sent(so_far[1], SWAP)
    three = mid + three_end
    sum_mid = sent(after(added(keep3, got3, near).astype(BF16), three), MID)
    sum_one = sent(added(keep1, got1, mid_far).astype(BF16), PAIR)
    three_b = sent(after(three, one_b), FLIP_B)
    so_far = projected(place, 2, activations, high, *shared, two, two_b, (so_far[0], so_far[2]))
    out2 = sent(so_far[1], SWAP)
    last = added(keep0, got0, sum_mid, sum_one)
    final = last[0] + sent(last[1].astype(BF16), FLIP_A).astype(F32)
    grad_weight = (final * (1.0 / math.sqrt(32 * tokens))).astype(BF16).T

    whole = laid(place, (0, 1, 2), so_far[0], (out0, out1, out2))
    whole, out3, keys, keys_far = projected(
        place, 3, activations, high, *shared, three, three_b, (whole, so_far[2])
    )
    grad_input = laid(place, (3,), whole, (sent(out3, SWAP),))
    key_values = (keys + sent(keys_far, SWAP)).astype(BF16)
    return (key_values, grad_input, grad_weight)


def swapped(array):
    return lax.ppermute(array, "core", [(0, 1), (1, 0)])


def by_collectives(activations, cotangent, kv_weight):
    blocks, chips = lax.axis_size("blk"), lax.axis_size("chip")
    core = lax.axis_index("core")
    tokens, features = activations.shape
    rows, cols = kv_weight.shape
    columns = cotangent.shape[1]
    by_core = activations.reshape(tokens, chips, 2, rows)
    mine = lax.dynamic_index_in_dim(by_core, core, 2, keepdims=False)
    other = lax.dynamic_index_in_dim(by_core, 1 - core, 2, keepdims=False)
    acts = jnp.concatenate([mine, swapped(other)], 0)
    cots = jnp.concatenate([cotangent, swapped(cotangent)], 0)
    weight = lax.all_gather(kv_weight, ("blk", "chip"), axis=0, tiled=False)
    weight = weight.reshape(blocks, chips, rows, cols)
    parts = jnp.einsum(
        "tzr,tbc->bzrc", acts, cots.reshape(2 * tokens, blocks, cols), preferred_element_type=F32
    ).astype(BF16).reshape(blocks * chips, rows, cols)
    total = lax.psum_scatter(parts, ("blk", "chip"), scatter_dimension=0, tiled=False)
    count = tokens * blocks * chips * 2
    grad_weight = (total.astype(F32) * (1.0 / math.sqrt(count))).astype(BF16)
    full = weight.transpose(1, 2, 0, 3).reshape(chips * rows, columns)
    keys = jnp.dot(acts.reshape(2 * tokens, chips * rows), full, preferred_element_type=F32)
    key_values = (keys[:tokens] + swapped(keys[tokens:])).astype(BF16)
    inputs = lax.dot_general(
        cots, full, (((1,), (1,)), ((), ())), preferred_element_type=F32
    ).astype(BF16).reshape(2 * tokens, chips, rows)
    near, far = inputs[:tokens], swapped(inputs[tokens:])
    low = jnp.where(core == 0, near, far)
    high = jnp.where(core == 0, far, near)
    grad_input = jnp.stack([low, high], 2).reshape(tokens, features)
    return (key_values, grad_input, grad_weight)


def solution(mesh):
    blocks, shards = mesh.shape["blk"], mesh.shape["shard"]
    split = Mesh(mesh.devices.reshape(blocks, shards // 2, 2), AXES)
    by_token = P(AXES, None)
    by_piece = P(("chip", "core"), "blk")
    return jax.shard_map(
        by_hops if (blocks, shards) == (4, 8) else by_collectives,
        mesh=split,
        in_specs=(by_token, by_token, by_piece),
        out_specs=(by_token, by_token, by_piece),
        check_vma=False,
    )
```

```python
import math

import jax
import jax.numpy as jnp
from jax import lax
from jax.experimental import pallas as pl
from jax.experimental.pallas import tpu as pltpu
from jax.sharding import Mesh, PartitionSpec as P

F32, BF16 = jnp.float32, jnp.bfloat16
AXES = ("blk", "chip", "core")
SHRINK = 1000
VMEM = 60 * 2**20


def hops(move):
    pairs = []
    for blk in range(4):
        for z in range(4):
            for core in range(2):
                to = move(blk, z, core)
                if to is not None:
                    pairs.append(((blk * 4 + z) * 2 + core, (to[0] * 4 + to[1]) * 2 + to[2]))
    return pairs


def middle(z):
    return z in (1, 2)


SWAP = hops(lambda b, z, c: (b, z, 1 - c))
FLIP_A = hops(lambda b, z, c: (b ^ (1 + c), z, c))
FLIP_B = hops(lambda b, z, c: (b ^ (2 - c), z, c))
PAIR = hops(lambda b, z, c: (b, z ^ 1, c))
MID = hops(lambda b, z, c: (b, z ^ 3, c) if middle(z) else None)
OUT = hops(lambda b, z, c: (b, z ^ 1, c) if middle(z) else None)
IN = hops(lambda b, z, c: (b, z ^ 1, c) if not middle(z) else None)


def after(array, *others):
    return lax.optimization_barrier((array, *others))[0]


def sent(array, pairs):
    return lax.ppermute(array, AXES, pairs)


def column_block(place, a, b):
    core = place[1]
    return place[2] ^ (a * (1 + core)) ^ (b * (2 - core))


def cost(flops, moved, shrink=SHRINK):
    return pl.CostEstimate(flops=flops // shrink, bytes_accessed=moved // shrink, transcendentals=0)


def term_kernel(place, mine, other, cot_mine, cot_other, *refs):
    tokens, cols = cot_mine.shape[0], cot_mine.shape[1] // 4
    turned = refs[-1]
    step = pl.program_id(0)

    @pl.when((step == 0) & (pl.program_id(1) == 0))
    def _():
        for b in (0, 1):
            for a in (0, 1):
                at = pl.ds(pl.multiple_of(column_block(place, a, b) * cols, cols), cols)
                to = slice((2 * b + a) * cols, (2 * b + a + 1) * cols)
                turned[to, :tokens] = cot_mine[:, at].T
                turned[to, tokens:] = cot_other[:, at].T

    tall = jnp.concatenate([mine[...], other[...]], 0)
    for b in (0, 1):
        part = jnp.dot(
            turned[2 * b * cols : (2 * b + 2) * cols], tall, preferred_element_type=F32
        ).astype(BF16)
        for i in range(3):

            @pl.when((step >= 2) if i == 2 else (step == i))
            def _():
                out = refs[3 * b + i]
                out[...] = part.reshape(out.shape)


def terms(place, activations, other, cot_mine, cot_other, rows):
    tokens, columns = cot_mine.shape
    part, cols = rows // 2, columns // 4
    whole = pl.BlockSpec((tokens, columns), lambda i, r, s: (0, 0))
    mine = pl.BlockSpec((tokens, part), lambda i, r, s: (0, 2 * (2 * (s[0] ^ (3 - i)) + s[1]) + r))
    pieces = [
        pl.BlockSpec((2, cols, part), lambda i, r, s: (0, 0, jnp.where(i == 0, r, 1))),
        pl.BlockSpec(
            (2, cols, part), lambda i, r, s: (0, 0, jnp.where(i == 1, r, jnp.where(i == 0, 0, 1)))
        ),
        pl.BlockSpec(
            (1, 2, cols, part),
            lambda i, r, s: (jnp.where(i == 3, 0, 1), 0, 0, jnp.where(i < 2, 0, r)),
        ),
    ]
    return pl.pallas_call(
        term_kernel,
        grid_spec=pltpu.PrefetchScalarGridSpec(
            num_scalar_prefetch=1,
            grid=(4, 2),
            in_specs=[mine, mine, whole, whole],
            out_specs=pieces * 2,
            scratch_shapes=[pltpu.VMEM((columns, 2 * tokens), BF16)],
        ),
        out_shape=[
            jax.ShapeDtypeStruct((2, cols, rows), BF16),
            jax.ShapeDtypeStruct((2, cols, rows), BF16),
            jax.ShapeDtypeStruct((2, 2, cols, rows), BF16),
        ]
        * 2,
        compiler_params=pltpu.CompilerParams(vmem_limit_bytes=VMEM),
        cost_estimate=cost(16 * tokens * rows * columns, 16 * tokens * rows + 16 * rows * columns),
        name="terms",
    )(place, activations, other, cot_mine, cot_other)


def project_kernel(place, *refs, count, first, last):
    acts, other, cot_mine, cot_other = refs[:4]
    pieces = refs[4 : 4 + 2 * count]
    at_out = 4 + 2 * count + (0 if first else 2)
    near, far, *keys = refs[at_out:-2]
    acc, cots = refs[-2:]
    tokens, cols = cot_mine.shape[0], cot_mine.shape[1] // 4
    group, tile = pl.program_id(0), pl.program_id(1)
    blocks = [
        (
            slice((2 * b + a) * cols, (2 * b + a + 1) * cols),
            pl.ds(pl.multiple_of(column_block(place, a, b) * cols, cols), cols),
        )
        for b in (0, 1)
        for a in (0, 1)
    ]

    @pl.when((group == 0) & (tile == 0))
    def _():
        for to, at in blocks:
            cots[:tokens, to] = cot_mine[:, at]
            cots[tokens:, to] = cot_other[:, at]

    for n in range(count):

        @pl.when(group == n)
        def _():
            here, there = pieces[2 * n], pieces[2 * n + 1]
            weight = jnp.concatenate([here[0], here[1], there[0], there[1]], 1)
            total = lax.dot_general(
                cots[...], weight, (((1,), (1,)), ((), ())), preferred_element_type=F32
            ).astype(BF16)
            near[...] = total[:tokens]
            far[...] = total[tokens:]
            tall = jnp.concatenate([acts[...], other[...]], 0)
            sums = jnp.dot(tall, weight, preferred_element_type=F32)
            if n > 0:
                acc[...] += sums
            else:

                @pl.when(tile == 0)
                def _():
                    acc[...] = sums if first else refs[4 + 2 * count][...] + sums

                @pl.when(tile > 0)
                def _():
                    acc[...] += sums

    @pl.when((group == count - 1) & (tile == pl.num_programs(1) - 1))
    def _():
        if last:
            for to, at in blocks:
                keys[0][:, at] = acc[:tokens, to]
                keys[1][:, at] = acc[tokens:, to]
        else:
            keys[0][...] = acc[...]


def projected(place, start, activations, other, cot_mine, cot_other, pieces, so_far=None):
    tokens, columns = cot_mine.shape
    _, rows, cols = pieces[0].shape
    part, count = rows // 2, len(pieces) // 2
    first, last = so_far is None, start + count == 4
    whole = pl.BlockSpec((tokens, columns), lambda i, r, s: (0, 0))
    both = pl.BlockSpec((2 * tokens, columns), lambda i, r, s: (0, 0))
    mine = pl.BlockSpec(
        (tokens, part), lambda i, r, s: (0, 2 * (2 * (s[0] ^ (start + i)) + s[1]) + r)
    )
    held = [
        pl.BlockSpec((2, part, cols), lambda i, r, s, n=n: (0, jnp.clip(2 * (i - n) + r, 0, 1), 0))
        for n in range(count)
        for _ in range(2)
    ]
    one = jax.ShapeDtypeStruct((tokens, columns), F32)
    return pl.pallas_call(
        lambda *refs: project_kernel(*refs, count=count, first=first, last=last),
        grid_spec=pltpu.PrefetchScalarGridSpec(
            num_scalar_prefetch=1,
            grid=(count, 2),
            in_specs=[mine, mine, whole, whole, *held]
            + ([] if first else [both, pl.BlockSpec(memory_space=pl.ANY)]),
            out_specs=[mine, pl.BlockSpec((tokens, part), lambda i, r, s: (0, 2 * i + r))]
            + ([whole, whole] if last else [both]),
            scratch_shapes=[
                pltpu.VMEM((2 * tokens, columns), F32),
                pltpu.VMEM((2 * tokens, columns), BF16),
            ],
        ),
        out_shape=[
            jax.ShapeDtypeStruct(activations.shape, BF16),
            jax.ShapeDtypeStruct((tokens, count * rows), BF16),
        ]
        + ([one, one] if last else [jax.ShapeDtypeStruct((2 * tokens, columns), F32)]),
        input_output_aliases={} if first else {6 + 2 * count: 0},
        compiler_params=pltpu.CompilerParams(vmem_limit_bytes=VMEM),
        cost_estimate=cost(
            8 * tokens * rows * columns * count,
            (8 * tokens * rows + 2 * rows * columns) * count + 8 * tokens * columns,
            1 if last else SHRINK,
        ),
        name="project",
    )(
        place, activations, other, cot_mine, cot_other, *pieces,
        *([] if first else [so_far[2], so_far[0]]),
    )


def lay_kernel(place, *refs, rows):
    parts, out, sems = refs[:-3], refs[-2], refs[-1]
    copies, k = [], 0
    for part in parts:
        for i in range(part.shape[1] // rows):
            at = pl.multiple_of((2 * (place[0] ^ k) + 1 - place[1]) * rows, rows)
            copies.append(
                pltpu.make_async_copy(
                    part.at[:, i * rows : (i + 1) * rows], out.at[:, pl.ds(at, rows)], sems.at[k]
                )
            )
            k += 1
    for copy in copies:
        copy.start()
    for copy in copies:
        copy.wait()


def laid(place, whole, parts, rows):
    return pl.pallas_call(
        lambda *refs: lay_kernel(*refs, rows=rows),
        in_specs=[pl.BlockSpec(memory_space=pltpu.SMEM)]
        + [pl.BlockSpec(memory_space=pl.ANY)] * (len(parts) + 1),
        out_specs=pl.BlockSpec(memory_space=pl.ANY),
        out_shape=jax.ShapeDtypeStruct(whole.shape, BF16),
        scratch_shapes=[pltpu.SemaphoreType.DMA((4,))],
        input_output_aliases={1 + len(parts): 0},
        compiler_params=pltpu.CompilerParams(vmem_limit_bytes=VMEM),
        cost_estimate=cost(0, 2 * whole.size),
        name="lay",
    )(place, *parts, whole)


def added(*arrays):
    total = arrays[0].astype(F32)
    for array in arrays[1:]:
        total = total + array.astype(F32)
    return total.astype(BF16)


def by_hops(activations, cotangent, kv_weight):
    rows = kv_weight.shape[0]
    tokens = activations.shape[0]
    place = jnp.stack([lax.axis_index(name) for name in ("chip", "core", "blk")]).astype(jnp.int32)

    other = sent(activations, SWAP)
    base = jnp.stack([kv_weight, sent(kv_weight, FLIP_A)])
    cot_other = sent(after(cotangent, base), SWAP)
    shared = (activations, other, cotangent, cot_other)
    one, mid = sent(base, PAIR), sent(base, MID)
    base_b = sent(base, FLIP_B)

    keep3, keep2, keep10, send3, send2, send10 = terms(
        place, after(activations, base), *shared[1:], rows
    )
    got3 = sent(send3, FLIP_B)
    got2 = sent(after(send2, base_b), FLIP_B)
    got10 = sent(after(send10, got3), FLIP_B)
    so_far = projected(place, 0, after(activations, keep10), *shared[1:], (base, base_b))
    out0 = sent(so_far[1], SWAP)

    sum3 = added(after(keep3, so_far[1]), got3)
    far = sent(after(sum3, one, mid), IN)
    two_mid = sent(one, MID)
    two_end = sent(mid, OUT)
    sum2 = added(keep2, got2)
    two = two_mid + two_end
    near = sent(after(sum2, far, two), IN)
    mid_far = sent(added(sum2, far), MID)
    three_end = sent(two_mid, OUT)
    one_b = sent(after(one, got2), FLIP_B)
    two_b = sent(after(two, got10), FLIP_B)

    three = mid + three_end
    three_b = sent(after(three, one_b), FLIP_B)
    sum_mid = sent(added(sum3, after(near, three)), MID)
    sum_one = sent(added(keep10[1], got10[1], mid_far), PAIR)
    so_far = projected(
        place, 1, after(activations, out0), *shared[1:], (one, one_b, two, two_b), so_far
    )
    out12 = sent(so_far[1], SWAP)
    last = [
        keep10[0, a].astype(F32)
        + got10[0, a].astype(F32)
        + sum_mid[a].astype(F32)
        + sum_one[a].astype(F32)
        for a in (0, 1)
    ]
    over = last[1].astype(BF16)
    final = last[0] + sent(over, FLIP_A).astype(F32)
    grad_weight = (final * (1.0 / math.sqrt(32 * tokens))).astype(BF16).T

    whole, out3, keys, keys_far = projected(
        place, 3, after(activations, over), *shared[1:], (three, three_b), so_far
    )
    grad_input = laid(place, whole, (out0, out12, sent(out3, SWAP)), rows)
    key_values = (keys + sent(keys_far, SWAP)).astype(BF16)
    return (key_values, grad_input, grad_weight)


def swapped(array):
    return lax.ppermute(array, "core", [(0, 1), (1, 0)])


def by_collectives(activations, cotangent, kv_weight):
    blocks, chips = lax.axis_size("blk"), lax.axis_size("chip")
    core = lax.axis_index("core")
    tokens, features = activations.shape
    rows, cols = kv_weight.shape
    columns = cotangent.shape[1]
    by_core = activations.reshape(tokens, chips, 2, rows)
    mine = lax.dynamic_index_in_dim(by_core, core, 2, keepdims=False)
    other = lax.dynamic_index_in_dim(by_core, 1 - core, 2, keepdims=False)
    acts = jnp.concatenate([mine, swapped(other)], 0)
    cots = jnp.concatenate([cotangent, swapped(cotangent)], 0)
    weight = lax.all_gather(kv_weight, ("blk", "chip"), axis=0, tiled=False)
    weight = weight.reshape(blocks, chips, rows, cols)
    parts = jnp.einsum(
        "tzr,tbc->bzrc", acts, cots.reshape(2 * tokens, blocks, cols), preferred_element_type=F32
    ).astype(BF16).reshape(blocks * chips, rows, cols)
    total = lax.psum_scatter(parts, ("blk", "chip"), scatter_dimension=0, tiled=False)
    count = tokens * blocks * chips * 2
    grad_weight = (total.astype(F32) * (1.0 / math.sqrt(count))).astype(BF16)
    full = weight.transpose(1, 2, 0, 3).reshape(chips * rows, columns)
    keys = jnp.dot(acts.reshape(2 * tokens, chips * rows), full, preferred_element_type=F32)
    key_values = (keys[:tokens] + swapped(keys[tokens:])).astype(BF16)
    inputs = lax.dot_general(
        cots, full, (((1,), (1,)), ((), ())), preferred_element_type=F32
    ).astype(BF16).reshape(2 * tokens, chips, rows)
    near, far = inputs[:tokens], swapped(inputs[tokens:])
    low = jnp.where(core == 0, near, far)
    high = jnp.where(core == 0, far, near)
    grad_input = jnp.stack([low, high], 2).reshape(tokens, features)
    return (key_values, grad_input, grad_weight)


def solution(mesh):
    blocks, shards = mesh.shape["blk"], mesh.shape["shard"]
    split = Mesh(mesh.devices.reshape(blocks, shards // 2, 2), AXES)
    by_token = P(AXES, None)
    by_piece = P(("chip", "core"), "blk")
    return jax.shard_map(
        by_hops if (blocks, shards) == (4, 8) else by_collectives,
        mesh=split,
        in_specs=(by_token, by_token, by_piece),
        out_specs=(by_token, by_token, by_piece),
        check_vma=False,
    )
```

```python
import math

import jax
import jax.numpy as jnp
from jax import lax
from jax.experimental import pallas as pl
from jax.experimental.pallas import tpu as pltpu
from jax.sharding import Mesh, PartitionSpec as P

F32, BF16 = jnp.float32, jnp.bfloat16
AXES = ("blk", "chip", "core")
SHRINK = 1000
VMEM = 63 * 2**20


def hops(move):
    pairs = []
    for blk in range(4):
        for z in range(4):
            for core in range(2):
                to = move(blk, z, core)
                if to is not None:
                    pairs.append(((blk * 4 + z) * 2 + core, (to[0] * 4 + to[1]) * 2 + to[2]))
    return pairs


def middle(z):
    return z in (1, 2)


SWAP = hops(lambda b, z, c: (b, z, 1 - c))
FLIP_A = hops(lambda b, z, c: (b ^ (1 + c), z, c))
FLIP_B = hops(lambda b, z, c: (b ^ (2 - c), z, c))
PAIR = hops(lambda b, z, c: (b, z ^ 1, c))
MID = hops(lambda b, z, c: (b, z ^ 3, c) if middle(z) else None)
OUT = hops(lambda b, z, c: (b, z ^ 1, c) if middle(z) else None)
IN = hops(lambda b, z, c: (b, z ^ 1, c) if not middle(z) else None)


def after(array, *others):
    return lax.optimization_barrier((array, *others))[0]


def sent(array, pairs):
    return lax.ppermute(array, AXES, pairs)


def column_block(place, a, b):
    core = place[1]
    return place[2] ^ (a * (1 + core)) ^ (b * (2 - core))


def cost(flops, moved, shrink=SHRINK):
    return pl.CostEstimate(flops=flops // shrink, bytes_accessed=moved // shrink, transcendentals=0)


def first_term_kernel(place, mine, other, cot_mine, cot_other, keep, send, cots, turned):
    tokens, cols = cot_mine.shape[0], cot_mine.shape[1] // 4

    @pl.when(pl.program_id(0) == 0)
    def _():
        for b in (0, 1):
            for a in (0, 1):
                at = pl.ds(pl.multiple_of(column_block(place, a, b) * cols, cols), cols)
                to = slice((2 * b + a) * cols, (2 * b + a + 1) * cols)
                for array, half in ((cot_mine, slice(0, tokens)), (cot_other, slice(tokens, None))):
                    piece = array[:, at]
                    cots[half, to] = piece
                    turned[to, half] = piece.T

    tall = jnp.concatenate([mine[...], other[...]], 0)
    for b, out in ((1, send), (0, keep)):
        part = turned[2 * b * cols : (2 * b + 2) * cols]
        out[...] = jnp.dot(part, tall, preferred_element_type=F32).astype(BF16).reshape(out.shape)


def first_terms(place, activations, other, cot_mine, cot_other, rows):
    tokens, columns = cot_mine.shape
    part, cols = rows // 2, columns // 4
    mine = pl.BlockSpec((tokens, part), lambda r, s: (0, 2 * (2 * (s[0] ^ 3) + s[1]) + r))
    piece = pl.BlockSpec((2, cols, part), lambda r, s: (0, 0, r))

    def whole(*shape):
        return pl.BlockSpec(shape, lambda r, s: (0, 0))

    return pl.pallas_call(
        first_term_kernel,
        grid_spec=pltpu.PrefetchScalarGridSpec(
            num_scalar_prefetch=1,
            grid=(2,),
            in_specs=[mine, mine, whole(tokens, columns), whole(tokens, columns)],
            out_specs=[piece, piece, whole(2 * tokens, columns), whole(columns, 2 * tokens)],
        ),
        out_shape=[jax.ShapeDtypeStruct((2, cols, rows), BF16)] * 2
        + [
            jax.ShapeDtypeStruct((2 * tokens, columns), BF16),
            jax.ShapeDtypeStruct((columns, 2 * tokens), BF16),
        ],
        compiler_params=pltpu.CompilerParams(vmem_limit_bytes=VMEM),
        cost_estimate=cost(4 * tokens * rows * columns, 4 * tokens * rows + 4 * rows * columns),
        name="terms",
    )(place, activations, other, cot_mine, cot_other)


def term_kernel(place, mine, other, turned, keep2, keep10, send2, send10):
    rows = turned.shape[0] // 2
    for first in (True, False):

        @pl.when((pl.program_id(0) == 0) == first)
        def _():
            tall = jnp.concatenate([mine[...], other[...]], 0)
            for b, out in ((1, send2 if first else send10), (0, keep2 if first else keep10)):
                part = turned[b * rows : (b + 1) * rows]
                out[...] = (
                    jnp.dot(part, tall, preferred_element_type=F32).astype(BF16).reshape(out.shape)
                )


def terms(place, activations, other, turned, rows):
    columns, tokens = turned.shape[0], activations.shape[0]
    part, cols = rows // 2, columns // 4
    mine = pl.BlockSpec((tokens, part), lambda i, r, s: (0, 2 * (2 * (s[0] ^ (2 - i)) + s[1]) + r))
    pieces = [
        pl.BlockSpec((2, cols, part), lambda i, r, s: (0, 0, jnp.where(i == 0, r, 1))),
        pl.BlockSpec(
            (1, 2, cols, part),
            lambda i, r, s: (jnp.where(i == 2, 0, 1), 0, 0, jnp.where(i == 0, 0, r)),
        ),
    ]
    return pl.pallas_call(
        term_kernel,
        grid_spec=pltpu.PrefetchScalarGridSpec(
            num_scalar_prefetch=1,
            grid=(3, 2),
            in_specs=[mine, mine, pl.BlockSpec(turned.shape, lambda i, r, s: (0, 0))],
            out_specs=pieces * 2,
        ),
        out_shape=[
            jax.ShapeDtypeStruct((2, cols, rows), BF16),
            jax.ShapeDtypeStruct((2, 2, cols, rows), BF16),
        ]
        * 2,
        compiler_params=pltpu.CompilerParams(vmem_limit_bytes=VMEM),
        cost_estimate=cost(12 * tokens * rows * columns, 12 * tokens * rows + 12 * rows * columns),
        name="terms",
    )(place, activations, other, turned)


def project_kernel(place, acts, other, cots, here, there, *refs, first, last):
    near, far, *keys = refs[0 if first else 3 : -1]
    acc = refs[-1]
    tokens, cols = acts.shape[0], here.shape[2]
    step = pl.program_id(0)

    @pl.when(step < 2)
    def _():
        weight = jnp.concatenate([here[0], here[1], there[0], there[1]], 1)
        total = lax.dot_general(
            cots[...], weight, (((1,), (1,)), ((), ())), preferred_element_type=F32
        ).astype(BF16)
        near[...] = total[:tokens]
        far[...] = total[tokens:]
        tall = jnp.concatenate([acts[...], other[...]], 0)
        sums = jnp.dot(tall, weight, preferred_element_type=F32)

        @pl.when(step == 0)
        def _():
            acc[...] = sums if first else refs[0][...] + sums

        @pl.when(step == 1)
        def _():
            if last:
                for b in (0, 1):
                    for a in (0, 1):
                        at = pl.ds(pl.multiple_of(column_block(place, a, b) * cols, cols), cols)
                        to = slice((2 * b + a) * cols, (2 * b + a + 1) * cols)
                        keys[0][:, at] = acc[:tokens, to] + sums[:tokens, to]
                        keys[1][:, at] = acc[tokens:, to] + sums[tokens:, to]
            else:
                keys[0][...] = acc[...] + sums

    if not first:

        @pl.when(step >= 2)
        def _():
            near[...] = refs[1][...]


def projected(place, k, activations, other, cots, here, there, so_far=None, got=None):
    tokens, columns = activations.shape[0], cots.shape[1]
    _, rows, cols = here.shape
    part = rows // 2
    first, last = k == 0, k == 3

    def whole(*shape):
        return pl.BlockSpec(shape, lambda r, s: (0, 0))

    def out_at(r, s):
        own = 2 * (2 * (s[0] ^ k) + s[1]) + r
        received = 2 * (2 * (s[0] ^ (k - 1)) + 1 - s[1]) + r - 2
        return (0, own if first else jnp.where(r < 2, own, received))

    mine = pl.BlockSpec(
        (tokens, part), lambda r, s: (0, 2 * (2 * (s[0] ^ k) + s[1]) + jnp.minimum(r, 1))
    )
    piece = pl.BlockSpec((2, part, cols), lambda r, s: (0, jnp.minimum(r, 1), 0))
    one = jax.ShapeDtypeStruct((tokens, columns), F32)
    return pl.pallas_call(
        lambda *refs: project_kernel(*refs, first=first, last=last),
        grid_spec=pltpu.PrefetchScalarGridSpec(
            num_scalar_prefetch=1,
            grid=(2 if first else 4,),
            in_specs=[mine, mine, whole(2 * tokens, columns), piece, piece]
            + (
                []
                if first
                else [
                    whole(2 * tokens, columns),
                    pl.BlockSpec((tokens, part), lambda r, s: (0, jnp.maximum(r - 2, 0))),
                    pl.BlockSpec(memory_space=pl.ANY),
                ]
            ),
            out_specs=[
                pl.BlockSpec((tokens, part), out_at),
                pl.BlockSpec((tokens, part), lambda r, s: (0, jnp.minimum(r, 1))),
            ]
            + ([whole(tokens, columns)] * 2 if last else [whole(2 * tokens, columns)]),
            scratch_shapes=[pltpu.VMEM((2 * tokens, columns), F32)],
        ),
        out_shape=[
            jax.ShapeDtypeStruct(activations.shape, BF16),
            jax.ShapeDtypeStruct((tokens, rows), BF16),
        ]
        + ([one, one] if last else [jax.ShapeDtypeStruct((2 * tokens, columns), F32)]),
        input_output_aliases={} if first else {8: 0},
        compiler_params=pltpu.CompilerParams(vmem_limit_bytes=VMEM),
        cost_estimate=cost(
            8 * tokens * rows * columns,
            8 * tokens * rows + 2 * rows * columns + 8 * tokens * columns,
            1 if last else SHRINK,
        ),
        name="project",
    )(
        place, activations, other, cots, here, there,
        *([] if first else [so_far[2], got, so_far[0]]),
    )


def finish_kernel(place, got, near, far, whole, out, keys):
    out[...] = got[...]
    keys[...] = (near[...] + far[...]).astype(BF16)


def finished(place, whole, got, keys_near, keys_far):
    tokens, rows = got.shape
    columns = keys_near.shape[1]
    part, some = rows // 2, columns // 2
    wide = pl.BlockSpec((tokens, some), lambda r, s: (0, r))
    return pl.pallas_call(
        finish_kernel,
        grid_spec=pltpu.PrefetchScalarGridSpec(
            num_scalar_prefetch=1,
            grid=(2,),
            in_specs=[
                pl.BlockSpec((tokens, part), lambda r, s: (0, r)),
                wide,
                wide,
                pl.BlockSpec(memory_space=pl.ANY),
            ],
            out_specs=[
                pl.BlockSpec((tokens, part), lambda r, s: (0, 2 * (2 * (s[0] ^ 3) + 1 - s[1]) + r)),
                wide,
            ],
        ),
        out_shape=[
            jax.ShapeDtypeStruct(whole.shape, BF16),
            jax.ShapeDtypeStruct((tokens, columns), BF16),
        ],
        input_output_aliases={4: 0},
        compiler_params=pltpu.CompilerParams(vmem_limit_bytes=VMEM),
        cost_estimate=cost(0, 4 * tokens * rows + 10 * tokens * columns),
        name="finish",
    )(place, got, keys_near, keys_far, whole)


def added(*arrays):
    total = arrays[0].astype(F32)
    for array in arrays[1:]:
        total = total + array.astype(F32)
    return total.astype(BF16)


def by_hops(activations, cotangent, kv_weight):
    rows = kv_weight.shape[0]
    tokens = activations.shape[0]
    place = jnp.stack([lax.axis_index(name) for name in ("chip", "core", "blk")]).astype(jnp.int32)

    other, cot_other = sent(activations, SWAP), sent(cotangent, SWAP)
    base = jnp.stack([kv_weight, sent(kv_weight, FLIP_A)])
    one, mid = sent(base, PAIR), sent(base, MID)
    base_b = sent(base, FLIP_B)

    keep3, send3, cots, turned = first_terms(
        place, after(activations, base), other, cotangent, cot_other, rows
    )
    got3 = sent(send3, FLIP_B)
    keep2, keep10, send2, send10 = terms(place, activations, other, turned, rows)
    got2 = sent(after(send2, got3, base_b), FLIP_B)

    sum3 = added(keep3, got3)
    far = sent(after(sum3, one, mid), IN)
    two_mid = sent(after(one, mid), MID)
    two_end = sent(mid, OUT)
    one_b = sent(after(one, got2), FLIP_B)
    got10 = sent(after(send10, got2), FLIP_B)
    whole, out, keys = projected(
        place, 0, after(activations, keep10), other, cots, base, base_b
    )
    got = sent(out, SWAP)
    sum2 = added(keep2, got2)
    two = two_mid + two_end
    near = sent(after(sum2, far, two, out), IN)
    mid_far = sent(added(sum2, far), MID)
    three_end = sent(two_mid, OUT)
    two_b = sent(after(two, one_b), FLIP_B)
    whole, out, keys = projected(
        place, 1, after(activations, out), other, cots, one, one_b, (whole, None, keys), got
    )
    got = sent(out, SWAP)

    three = mid + three_end
    three_b = sent(after(three, got10), FLIP_B)
    sum_mid = sent(added(sum3, after(near, three, out)), MID)
    sum_one = sent(added(keep10[1], got10[1], mid_far), PAIR)
    whole, out, keys = projected(
        place, 2, after(activations, out), other, cots, two, two_b, (whole, None, keys), got
    )
    got = sent(out, SWAP)
    sum_mid, sum_one = after(sum_mid, out), after(sum_one, out)
    last = [
        keep10[0, a].astype(F32)
        + got10[0, a].astype(F32)
        + sum_mid[a].astype(F32)
        + sum_one[a].astype(F32)
        for a in (0, 1)
    ]
    over = last[1].astype(BF16)
    arrived = sent(over, FLIP_A)
    final = last[0] + arrived.astype(F32)
    grad_weight = (final * (1.0 / math.sqrt(32 * tokens))).astype(BF16).T

    whole, out, keys, keys_far = projected(
        place, 3, after(activations, over), other, cots, three, three_b, (whole, None, keys), got
    )
    grad_input, key_values = finished(
        place, whole, sent(out, SWAP), keys, sent(after(keys_far, arrived), SWAP)
    )
    return (key_values, grad_input, grad_weight)


def swapped(array):
    return lax.ppermute(array, "core", [(0, 1), (1, 0)])


def by_collectives(activations, cotangent, kv_weight):
    blocks, chips = lax.axis_size("blk"), lax.axis_size("chip")
    core = lax.axis_index("core")
    tokens, features = activations.shape
    rows, cols = kv_weight.shape
    columns = cotangent.shape[1]
    by_core = activations.reshape(tokens, chips, 2, rows)
    mine = lax.dynamic_index_in_dim(by_core, core, 2, keepdims=False)
    other = lax.dynamic_index_in_dim(by_core, 1 - core, 2, keepdims=False)
    acts = jnp.concatenate([mine, swapped(other)], 0)
    cots = jnp.concatenate([cotangent, swapped(cotangent)], 0)
    weight = lax.all_gather(kv_weight, ("blk", "chip"), axis=0, tiled=False)
    weight = weight.reshape(blocks, chips, rows, cols)
    parts = jnp.einsum(
        "tzr,tbc->bzrc", acts, cots.reshape(2 * tokens, blocks, cols), preferred_element_type=F32
    ).astype(BF16).reshape(blocks * chips, rows, cols)
    total = lax.psum_scatter(parts, ("blk", "chip"), scatter_dimension=0, tiled=False)
    count = tokens * blocks * chips * 2
    grad_weight = (total.astype(F32) * (1.0 / math.sqrt(count))).astype(BF16)
    full = weight.transpose(1, 2, 0, 3).reshape(chips * rows, columns)
    keys = jnp.dot(acts.reshape(2 * tokens, chips * rows), full, preferred_element_type=F32)
    key_values = (keys[:tokens] + swapped(keys[tokens:])).astype(BF16)
    inputs = lax.dot_general(
        cots, full, (((1,), (1,)), ((), ())), preferred_element_type=F32
    ).astype(BF16).reshape(2 * tokens, chips, rows)
    near, far = inputs[:tokens], swapped(inputs[tokens:])
    low = jnp.where(core == 0, near, far)
    high = jnp.where(core == 0, far, near)
    grad_input = jnp.stack([low, high], 2).reshape(tokens, features)
    return (key_values, grad_input, grad_weight)


def solution(mesh):
    blocks, shards = mesh.shape["blk"], mesh.shape["shard"]
    split = Mesh(mesh.devices.reshape(blocks, shards // 2, 2), AXES)
    by_token = P(AXES, None)
    by_piece = P(("chip", "core"), "blk")
    return jax.shard_map(
        by_hops if (blocks, shards) == (4, 8) else by_collectives,
        mesh=split,
        in_specs=(by_token, by_token, by_piece),
        out_specs=(by_token, by_token, by_piece),
        check_vma=False,
    )
```

```python
import math

import jax
import jax.numpy as jnp
from jax import lax
from jax.experimental import pallas as pl
from jax.experimental.pallas import tpu as pltpu
from jax.sharding import Mesh, PartitionSpec as P

F32, BF16 = jnp.float32, jnp.bfloat16
AXES = ("blk", "chip", "core")
SHRINK = 1000
MIB = 2**20
ONCE = pl.Buffered(1)


def hops(move):
    pairs = []
    for blk in range(4):
        for z in range(4):
            for core in range(2):
                to = move(blk, z, core)
                if to is not None:
                    pairs.append(((blk * 4 + z) * 2 + core, (to[0] * 4 + to[1]) * 2 + to[2]))
    return pairs


def middle(z):
    return z in (1, 2)


SWAP = hops(lambda b, z, c: (b, z, 1 - c))
FLIP_A = hops(lambda b, z, c: (b ^ (1 + c), z, c))
FLIP_B = hops(lambda b, z, c: (b ^ (2 - c), z, c))
PAIR = hops(lambda b, z, c: (b, z ^ 1, c))
MID = hops(lambda b, z, c: (b, z ^ 3, c) if middle(z) else None)
OUT = hops(lambda b, z, c: (b, z ^ 1, c) if middle(z) else None)
IN = hops(lambda b, z, c: (b, z ^ 1, c) if not middle(z) else None)


def after(array, *others):
    return lax.optimization_barrier((array, *others))[0]


def sent(array, pairs):
    return lax.ppermute(array, AXES, pairs)


def column_block(place, a, b):
    core = place[1]
    return place[2] ^ (a * (1 + core)) ^ (b * (2 - core))


def cost(flops, moved, shrink=SHRINK):
    return pl.CostEstimate(flops=flops // shrink, bytes_accessed=moved // shrink, transcendentals=0)


def first_term_kernel(place, mine, other, cot_mine, cot_other, keep, send, cots, turned):
    tokens, cols = cot_mine.shape[0], cot_mine.shape[1] // 4

    @pl.when(pl.program_id(0) == 0)
    def _():
        for b in (0, 1):
            for a in (0, 1):
                at = pl.ds(pl.multiple_of(column_block(place, a, b) * cols, cols), cols)
                to = slice((2 * b + a) * cols, (2 * b + a + 1) * cols)
                for array, half in ((cot_mine, slice(0, tokens)), (cot_other, slice(tokens, None))):
                    piece = array[:, at]
                    cots[half, to] = piece
                    turned[to, half] = piece.T

    tall = jnp.concatenate([mine[...], other[...]], 0)
    for b, out in ((1, send), (0, keep)):
        part = turned[2 * b * cols : (2 * b + 2) * cols]
        out[...] = jnp.dot(part, tall, preferred_element_type=F32).astype(BF16).reshape(out.shape)


def first_terms(place, activations, other, cot_mine, cot_other, rows):
    tokens, columns = cot_mine.shape
    part, cols = rows // 2, columns // 4
    mine = pl.BlockSpec((tokens, part), lambda r, s: (0, 2 * (2 * (s[0] ^ 3) + s[1]) + r))
    piece = pl.BlockSpec((2, cols, part), lambda r, s: (0, 0, r))

    held = pl.BlockSpec((tokens, columns), lambda r, s: (0, 0), pipeline_mode=ONCE)

    def whole(*shape):
        return pl.BlockSpec(shape, lambda r, s: (0, 0))

    return pl.pallas_call(
        first_term_kernel,
        grid_spec=pltpu.PrefetchScalarGridSpec(
            num_scalar_prefetch=1,
            grid=(2,),
            in_specs=[mine, mine, held, held],
            out_specs=[piece, piece, whole(2 * tokens, columns), whole(columns, 2 * tokens)],
        ),
        out_shape=[jax.ShapeDtypeStruct((2, cols, rows), BF16)] * 2
        + [
            jax.ShapeDtypeStruct((2 * tokens, columns), BF16),
            jax.ShapeDtypeStruct((columns, 2 * tokens), BF16),
        ],
        compiler_params=pltpu.CompilerParams(vmem_limit_bytes=22 * MIB),
        cost_estimate=cost(4 * tokens * rows * columns, 4 * tokens * rows + 4 * rows * columns),
        name="terms",
    )(place, activations, other, cot_mine, cot_other)


def term_kernel(place, mine, other, turned, keep2, keep10, send2, send10):
    rows = turned.shape[0] // 2
    for first in (True, False):

        @pl.when((pl.program_id(0) == 0) == first)
        def _():
            tall = jnp.concatenate([mine[...], other[...]], 0)
            for b, out in ((1, send2 if first else send10), (0, keep2 if first else keep10)):
                part = turned[b * rows : (b + 1) * rows]
                out[...] = (
                    jnp.dot(part, tall, preferred_element_type=F32).astype(BF16).reshape(out.shape)
                )


def terms(place, activations, other, turned, rows):
    columns, tokens = turned.shape[0], activations.shape[0]
    part, cols = rows // 2, columns // 4
    mine = pl.BlockSpec((tokens, part), lambda i, r, s: (0, 2 * (2 * (s[0] ^ (2 - i)) + s[1]) + r))
    pieces = [
        pl.BlockSpec((2, cols, part), lambda i, r, s: (0, 0, jnp.where(i == 0, r, 1))),
        pl.BlockSpec(
            (1, 2, cols, part),
            lambda i, r, s: (jnp.where(i == 2, 0, 1), 0, 0, jnp.where(i == 0, 0, r)),
        ),
    ]
    return pl.pallas_call(
        term_kernel,
        grid_spec=pltpu.PrefetchScalarGridSpec(
            num_scalar_prefetch=1,
            grid=(3, 2),
            in_specs=[mine, mine, pl.BlockSpec(turned.shape, lambda i, r, s: (0, 0), pipeline_mode=ONCE)],
            out_specs=pieces * 2,
        ),
        out_shape=[
            jax.ShapeDtypeStruct((2, cols, rows), BF16),
            jax.ShapeDtypeStruct((2, 2, cols, rows), BF16),
        ]
        * 2,
        compiler_params=pltpu.CompilerParams(vmem_limit_bytes=16 * MIB),
        cost_estimate=cost(12 * tokens * rows * columns, 12 * tokens * rows + 12 * rows * columns),
        name="terms",
    )(place, activations, other, turned)


def project_kernel(place, acts, other, cots, here, there, *refs, first, last):
    near, far, *keys = refs[0 if first else 3 : -1]
    acc = refs[-1]
    tokens, cols = acts.shape[0], here.shape[2]
    step = pl.program_id(0)

    @pl.when(step < 2)
    def _():
        weight = jnp.concatenate([here[0], here[1], there[0], there[1]], 1)
        total = lax.dot_general(
            cots[...], weight, (((1,), (1,)), ((), ())), preferred_element_type=F32
        ).astype(BF16)
        near[...] = total[:tokens]
        far[...] = total[tokens:]
        tall = jnp.concatenate([acts[...], other[...]], 0)
        sums = jnp.dot(tall, weight, preferred_element_type=F32)

        @pl.when(step == 0)
        def _():
            acc[...] = sums if first else refs[0][...] + sums

        @pl.when(step == 1)
        def _():
            if last:
                for b in (0, 1):
                    for a in (0, 1):
                        at = pl.ds(pl.multiple_of(column_block(place, a, b) * cols, cols), cols)
                        to = slice((2 * b + a) * cols, (2 * b + a + 1) * cols)
                        keys[0][:, at] = acc[:tokens, to] + sums[:tokens, to]
                        keys[1][:, at] = acc[tokens:, to] + sums[tokens:, to]
            else:
                keys[0][...] = acc[...] + sums

    if not first:

        @pl.when(step >= 2)
        def _():
            near[...] = refs[1][...]


def projected(place, k, activations, other, cots, here, there, so_far=None, got=None):
    tokens, columns = activations.shape[0], cots.shape[1]
    _, rows, cols = here.shape
    part = rows // 2
    first, last = k == 0, k == 3

    def whole(*shape):
        return pl.BlockSpec(shape, lambda r, s: (0, 0))

    held = pl.BlockSpec((2 * tokens, columns), lambda r, s: (0, 0), pipeline_mode=ONCE)

    def out_at(r, s):
        own = 2 * (2 * (s[0] ^ k) + s[1]) + r
        received = 2 * (2 * (s[0] ^ (k - 1)) + 1 - s[1]) + r - 2
        return (0, own if first else jnp.where(r < 2, own, received))

    mine = pl.BlockSpec(
        (tokens, part), lambda r, s: (0, 2 * (2 * (s[0] ^ k) + s[1]) + jnp.minimum(r, 1))
    )
    piece = pl.BlockSpec((2, part, cols), lambda r, s: (0, jnp.minimum(r, 1), 0))
    one = jax.ShapeDtypeStruct((tokens, columns), F32)
    return pl.pallas_call(
        lambda *refs: project_kernel(*refs, first=first, last=last),
        grid_spec=pltpu.PrefetchScalarGridSpec(
            num_scalar_prefetch=1,
            grid=(2 if first else 4,),
            in_specs=[mine, mine, held, piece, piece]
            + (
                []
                if first
                else [
                    held,
                    pl.BlockSpec((tokens, part), lambda r, s: (0, jnp.maximum(r - 2, 0))),
                    pl.BlockSpec(memory_space=pl.ANY),
                ]
            ),
            out_specs=[
                pl.BlockSpec((tokens, part), out_at),
                pl.BlockSpec((tokens, part), lambda r, s: (0, jnp.minimum(r, 1))),
            ]
            + ([whole(tokens, columns)] * 2 if last else [whole(2 * tokens, columns)]),
            scratch_shapes=[pltpu.VMEM((2 * tokens, columns), F32)],
        ),
        out_shape=[
            jax.ShapeDtypeStruct(activations.shape, BF16),
            jax.ShapeDtypeStruct((tokens, rows), BF16),
        ]
        + ([one, one] if last else [jax.ShapeDtypeStruct((2 * tokens, columns), F32)]),
        input_output_aliases={} if first else {8: 0},
        compiler_params=pltpu.CompilerParams(vmem_limit_bytes=28 * MIB),
        cost_estimate=cost(
            8 * tokens * rows * columns,
            8 * tokens * rows + 2 * rows * columns + 8 * tokens * columns,
            1 if last else SHRINK,
        ),
        name="project",
    )(
        place, activations, other, cots, here, there,
        *([] if first else [so_far[2], got, so_far[0]]),
    )


def finish_kernel(place, got, near, far, whole, out, keys):
    out[...] = got[...]
    keys[...] = (near[...] + far[...]).astype(BF16)


def finished(place, whole, got, keys_near, keys_far):
    tokens, rows = got.shape
    columns = keys_near.shape[1]
    part, some = rows // 2, columns // 2
    wide = pl.BlockSpec((tokens, some), lambda r, s: (0, r))
    return pl.pallas_call(
        finish_kernel,
        grid_spec=pltpu.PrefetchScalarGridSpec(
            num_scalar_prefetch=1,
            grid=(2,),
            in_specs=[
                pl.BlockSpec((tokens, part), lambda r, s: (0, r)),
                wide,
                wide,
                pl.BlockSpec(memory_space=pl.ANY),
            ],
            out_specs=[
                pl.BlockSpec((tokens, part), lambda r, s: (0, 2 * (2 * (s[0] ^ 3) + 1 - s[1]) + r)),
                wide,
            ],
        ),
        out_shape=[
            jax.ShapeDtypeStruct(whole.shape, BF16),
            jax.ShapeDtypeStruct((tokens, columns), BF16),
        ],
        input_output_aliases={4: 0},
        compiler_params=pltpu.CompilerParams(vmem_limit_bytes=10 * MIB),
        cost_estimate=cost(0, 4 * tokens * rows + 10 * tokens * columns),
        name="finish",
    )(place, got, keys_near, keys_far, whole)


def added(*arrays):
    total = arrays[0].astype(F32)
    for array in arrays[1:]:
        total = total + array.astype(F32)
    return total.astype(BF16)


def by_hops(activations, cotangent, kv_weight):
    rows = kv_weight.shape[0]
    tokens = activations.shape[0]
    place = jnp.stack([lax.axis_index(name) for name in ("chip", "core", "blk")]).astype(jnp.int32)

    other, cot_other = sent(activations, SWAP), sent(cotangent, SWAP)
    base = jnp.stack([kv_weight, sent(kv_weight, FLIP_A)])
    one, mid = sent(base, PAIR), sent(base, MID)
    base_b = sent(base, FLIP_B)

    keep3, send3, cots, turned = first_terms(
        place, activations, other, cotangent, cot_other, rows
    )
    got3 = sent(send3, FLIP_B)
    keep2, keep10, send2, send10 = terms(place, activations, other, turned, rows)
    got2 = sent(after(send2, got3, base_b), FLIP_B)

    sum3 = added(keep3, got3)
    far = sent(after(sum3, one, mid), IN)
    two_mid = sent(after(one, mid), MID)
    two_end = sent(mid, OUT)
    one_b = sent(after(one, got2), FLIP_B)
    got10 = sent(after(send10, got2), FLIP_B)
    whole, out, keys = projected(
        place, 0, after(activations, keep10), other, cots, base, base_b
    )
    got = sent(out, SWAP)
    sum2 = added(keep2, got2)
    two = two_mid + two_end
    near = sent(after(sum2, far, two, out), IN)
    mid_far = sent(added(sum2, far), MID)
    three_end = sent(two_mid, OUT)
    two_b = sent(after(two, one_b), FLIP_B)
    whole, out, keys = projected(
        place, 1, after(activations, out), other, cots, one, one_b, (whole, None, keys), got
    )
    got = sent(out, SWAP)

    three = mid + three_end
    three_b = sent(after(three, got10), FLIP_B)
    sum_mid = sent(added(sum3, after(near, three, out)), MID)
    sum_one = sent(added(keep10[1], got10[1], mid_far), PAIR)
    whole, out, keys = projected(
        place, 2, after(activations, out), other, cots, two, two_b, (whole, None, keys), got
    )
    got = sent(out, SWAP)
    sum_mid, sum_one = after(sum_mid, out), after(sum_one, out)
    last = [
        keep10[0, a].astype(F32)
        + got10[0, a].astype(F32)
        + sum_mid[a].astype(F32)
        + sum_one[a].astype(F32)
        for a in (0, 1)
    ]
    over = last[1].astype(BF16)
    arrived = sent(over, FLIP_A)
    final = last[0] + arrived.astype(F32)
    grad_weight = (final * (1.0 / math.sqrt(32 * tokens))).astype(BF16).T

    whole, out, keys, keys_far = projected(
        place, 3, after(activations, over), other, cots, three, three_b, (whole, None, keys), got
    )
    grad_input, key_values = finished(
        place, whole, sent(out, SWAP), keys, sent(after(keys_far, arrived), SWAP)
    )
    return (key_values, grad_input, grad_weight)


def swapped(array):
    return lax.ppermute(array, "core", [(0, 1), (1, 0)])


def by_collectives(activations, cotangent, kv_weight):
    blocks, chips = lax.axis_size("blk"), lax.axis_size("chip")
    core = lax.axis_index("core")
    tokens, features = activations.shape
    rows, cols = kv_weight.shape
    columns = cotangent.shape[1]
    by_core = activations.reshape(tokens, chips, 2, rows)
    mine = lax.dynamic_index_in_dim(by_core, core, 2, keepdims=False)
    other = lax.dynamic_index_in_dim(by_core, 1 - core, 2, keepdims=False)
    acts = jnp.concatenate([mine, swapped(other)], 0)
    cots = jnp.concatenate([cotangent, swapped(cotangent)], 0)
    weight = lax.all_gather(kv_weight, ("blk", "chip"), axis=0, tiled=False)
    weight = weight.reshape(blocks, chips, rows, cols)
    parts = jnp.einsum(
        "tzr,tbc->bzrc", acts, cots.reshape(2 * tokens, blocks, cols), preferred_element_type=F32
    ).astype(BF16).reshape(blocks * chips, rows, cols)
    total = lax.psum_scatter(parts, ("blk", "chip"), scatter_dimension=0, tiled=False)
    count = tokens * blocks * chips * 2
    grad_weight = (total.astype(F32) * (1.0 / math.sqrt(count))).astype(BF16)
    full = weight.transpose(1, 2, 0, 3).reshape(chips * rows, columns)
    keys = jnp.dot(acts.reshape(2 * tokens, chips * rows), full, preferred_element_type=F32)
    key_values = (keys[:tokens] + swapped(keys[tokens:])).astype(BF16)
    inputs = lax.dot_general(
        cots, full, (((1,), (1,)), ((), ())), preferred_element_type=F32
    ).astype(BF16).reshape(2 * tokens, chips, rows)
    near, far = inputs[:tokens], swapped(inputs[tokens:])
    low = jnp.where(core == 0, near, far)
    high = jnp.where(core == 0, far, near)
    grad_input = jnp.stack([low, high], 2).reshape(tokens, features)
    return (key_values, grad_input, grad_weight)


def solution(mesh):
    blocks, shards = mesh.shape["blk"], mesh.shape["shard"]
    split = Mesh(mesh.devices.reshape(blocks, shards // 2, 2), AXES)
    by_token = P(AXES, None)
    by_piece = P(("chip", "core"), "blk")
    return jax.shard_map(
        by_hops if (blocks, shards) == (4, 8) else by_collectives,
        mesh=split,
        in_specs=(by_token, by_token, by_piece),
        out_specs=(by_token, by_token, by_piece),
        check_vma=False,
    )
```

```python
import math

import jax
import jax.numpy as jnp
from jax import lax
from jax.experimental import pallas as pl
from jax.experimental.pallas import tpu as pltpu
from jax.sharding import Mesh, PartitionSpec as P

F32, BF16 = jnp.float32, jnp.bfloat16
AXES = ("blk", "chip", "core")
SHRINK = 1000
MIB = 2**20
GATE = 10**7
ONCE = pl.Buffered(1)


def hops(move):
    pairs = []
    for blk in range(4):
        for z in range(4):
            for core in range(2):
                to = move(blk, z, core)
                if to is not None:
                    pairs.append(((blk * 4 + z) * 2 + core, (to[0] * 4 + to[1]) * 2 + to[2]))
    return pairs


def middle(z):
    return z in (1, 2)


SWAP = hops(lambda b, z, c: (b, z, 1 - c))
FLIP_A = hops(lambda b, z, c: (b ^ (1 + c), z, c))
FLIP_B = hops(lambda b, z, c: (b ^ (2 - c), z, c))
PAIR = hops(lambda b, z, c: (b, z ^ 1, c))
MID = hops(lambda b, z, c: (b, z ^ 3, c) if middle(z) else None)
OUT = hops(lambda b, z, c: (b, z ^ 1, c) if middle(z) else None)
IN = hops(lambda b, z, c: (b, z ^ 1, c) if not middle(z) else None)


def after(array, *others):
    return lax.optimization_barrier((array, *others))[0]


def sent(array, pairs):
    return lax.ppermute(array, AXES, pairs)


def column_block(place, a, b):
    core = place[1]
    return place[2] ^ (a * (1 + core)) ^ (b * (2 - core))


def cost(flops, moved, shrink=SHRINK):
    return pl.CostEstimate(flops=flops // shrink, bytes_accessed=moved // shrink, transcendentals=0)


def gate(place, *arrays):
    def kernel(*refs):
        for i in range(3):
            refs[-1][i] = refs[0][i]

    return pl.pallas_call(
        kernel,
        in_specs=[pl.BlockSpec(memory_space=pltpu.SMEM)]
        + [pl.BlockSpec(memory_space=pl.ANY)] * len(arrays),
        out_specs=pl.BlockSpec(memory_space=pltpu.SMEM),
        out_shape=jax.ShapeDtypeStruct(place.shape, place.dtype),
        compiler_params=pltpu.CompilerParams(vmem_limit_bytes=MIB),
        cost_estimate=cost(0, GATE, 1),
        name="gate",
    )(place, *arrays)


def first_term_kernel(place, mine, other, cot_mine, cot_other, keep, send, cots, turned):
    tokens, cols = cot_mine.shape[0], cot_mine.shape[1] // 4

    @pl.when(pl.program_id(0) == 0)
    def _():
        for b in (0, 1):
            for a in (0, 1):
                at = pl.ds(pl.multiple_of(column_block(place, a, b) * cols, cols), cols)
                to = slice((2 * b + a) * cols, (2 * b + a + 1) * cols)
                for array, half in ((cot_mine, slice(0, tokens)), (cot_other, slice(tokens, None))):
                    piece = array[:, at]
                    cots[half, to] = piece
                    turned[to, half] = piece.T

    tall = jnp.concatenate([mine[...], other[...]], 0)
    for b, out in ((1, send), (0, keep)):
        part = turned[2 * b * cols : (2 * b + 2) * cols]
        out[...] = jnp.dot(part, tall, preferred_element_type=F32).astype(BF16).reshape(out.shape)


def first_terms(place, activations, other, cot_mine, cot_other, rows):
    tokens, columns = cot_mine.shape
    part, cols = rows // 2, columns // 4
    mine = pl.BlockSpec((tokens, part), lambda r, s: (0, 2 * (2 * (s[0] ^ 3) + s[1]) + r))
    piece = pl.BlockSpec((2, cols, part), lambda r, s: (0, 0, r))

    held = pl.BlockSpec((tokens, columns), lambda r, s: (0, 0), pipeline_mode=ONCE)

    def whole(*shape):
        return pl.BlockSpec(shape, lambda r, s: (0, 0))

    return pl.pallas_call(
        first_term_kernel,
        grid_spec=pltpu.PrefetchScalarGridSpec(
            num_scalar_prefetch=1,
            grid=(2,),
            in_specs=[mine, mine, held, held],
            out_specs=[piece, piece, whole(2 * tokens, columns), whole(columns, 2 * tokens)],
        ),
        out_shape=[jax.ShapeDtypeStruct((2, cols, rows), BF16)] * 2
        + [
            jax.ShapeDtypeStruct((2 * tokens, columns), BF16),
            jax.ShapeDtypeStruct((columns, 2 * tokens), BF16),
        ],
        compiler_params=pltpu.CompilerParams(vmem_limit_bytes=22 * MIB),
        cost_estimate=cost(4 * tokens * rows * columns, 4 * tokens * rows + 4 * rows * columns),
        name="terms",
    )(place, activations, other, cot_mine, cot_other)


def term_kernel(place, mine, other, turned, keep2, keep10, send2, send10):
    rows = turned.shape[0] // 2
    for first in (True, False):

        @pl.when((pl.program_id(0) == 0) == first)
        def _():
            tall = jnp.concatenate([mine[...], other[...]], 0)
            for b, out in ((1, send2 if first else send10), (0, keep2 if first else keep10)):
                part = turned[b * rows : (b + 1) * rows]
                out[...] = (
                    jnp.dot(part, tall, preferred_element_type=F32).astype(BF16).reshape(out.shape)
                )


def terms(place, activations, other, turned, rows):
    columns, tokens = turned.shape[0], activations.shape[0]
    part, cols = rows // 2, columns // 4
    mine = pl.BlockSpec((tokens, part), lambda i, r, s: (0, 2 * (2 * (s[0] ^ (2 - i)) + s[1]) + r))
    pieces = [
        pl.BlockSpec((2, cols, part), lambda i, r, s: (0, 0, jnp.where(i == 0, r, 1))),
        pl.BlockSpec(
            (1, 2, cols, part),
            lambda i, r, s: (jnp.where(i == 2, 0, 1), 0, 0, jnp.where(i == 0, 0, r)),
        ),
    ]
    return pl.pallas_call(
        term_kernel,
        grid_spec=pltpu.PrefetchScalarGridSpec(
            num_scalar_prefetch=1,
            grid=(3, 2),
            in_specs=[mine, mine, pl.BlockSpec(turned.shape, lambda i, r, s: (0, 0), pipeline_mode=ONCE)],
            out_specs=pieces * 2,
        ),
        out_shape=[
            jax.ShapeDtypeStruct((2, cols, rows), BF16),
            jax.ShapeDtypeStruct((2, 2, cols, rows), BF16),
        ]
        * 2,
        compiler_params=pltpu.CompilerParams(vmem_limit_bytes=16 * MIB),
        cost_estimate=cost(12 * tokens * rows * columns, 12 * tokens * rows + 12 * rows * columns),
        name="terms",
    )(place, activations, other, turned)


def project_kernel(place, acts, other, cots, here, there, *refs, first, last):
    near, far, *keys = refs[0 if first else 3 : -1]
    acc = refs[-1]
    tokens, cols = acts.shape[0], here.shape[2]
    step = pl.program_id(0)

    @pl.when(step < 2)
    def _():
        weight = jnp.concatenate([here[0], here[1], there[0], there[1]], 1)
        total = lax.dot_general(
            cots[...], weight, (((1,), (1,)), ((), ())), preferred_element_type=F32
        ).astype(BF16)
        near[...] = total[:tokens]
        far[...] = total[tokens:]
        tall = jnp.concatenate([acts[...], other[...]], 0)
        sums = jnp.dot(tall, weight, preferred_element_type=F32)

        @pl.when(step == 0)
        def _():
            acc[...] = sums if first else refs[0][...] + sums

        @pl.when(step == 1)
        def _():
            if last:
                for b in (0, 1):
                    for a in (0, 1):
                        at = pl.ds(pl.multiple_of(column_block(place, a, b) * cols, cols), cols)
                        to = slice((2 * b + a) * cols, (2 * b + a + 1) * cols)
                        keys[0][:, at] = acc[:tokens, to] + sums[:tokens, to]
                        keys[1][:, at] = acc[tokens:, to] + sums[tokens:, to]
            else:
                keys[0][...] = acc[...] + sums

    if not first:

        @pl.when(step >= 2)
        def _():
            near[...] = refs[1][...]


def projected(place, k, activations, other, cots, here, there, so_far=None, got=None):
    tokens, columns = activations.shape[0], cots.shape[1]
    _, rows, cols = here.shape
    part = rows // 2
    first, last = k == 0, k == 3

    def whole(*shape):
        return pl.BlockSpec(shape, lambda r, s: (0, 0))

    held = pl.BlockSpec((2 * tokens, columns), lambda r, s: (0, 0), pipeline_mode=ONCE)

    def out_at(r, s):
        own = 2 * (2 * (s[0] ^ k) + s[1]) + r
        received = 2 * (2 * (s[0] ^ (k - 1)) + 1 - s[1]) + r - 2
        return (0, own if first else jnp.where(r < 2, own, received))

    mine = pl.BlockSpec(
        (tokens, part), lambda r, s: (0, 2 * (2 * (s[0] ^ k) + s[1]) + jnp.minimum(r, 1))
    )
    piece = pl.BlockSpec((2, part, cols), lambda r, s: (0, jnp.minimum(r, 1), 0))
    one = jax.ShapeDtypeStruct((tokens, columns), F32)
    return pl.pallas_call(
        lambda *refs: project_kernel(*refs, first=first, last=last),
        grid_spec=pltpu.PrefetchScalarGridSpec(
            num_scalar_prefetch=1,
            grid=(2 if first else 4,),
            in_specs=[mine, mine, held, piece, piece]
            + (
                []
                if first
                else [
                    held,
                    pl.BlockSpec((tokens, part), lambda r, s: (0, jnp.maximum(r - 2, 0))),
                    pl.BlockSpec(memory_space=pl.ANY),
                ]
            ),
            out_specs=[
                pl.BlockSpec((tokens, part), out_at),
                pl.BlockSpec((tokens, part), lambda r, s: (0, jnp.minimum(r, 1))),
            ]
            + ([whole(tokens, columns)] * 2 if last else [whole(2 * tokens, columns)]),
            scratch_shapes=[pltpu.VMEM((2 * tokens, columns), F32)],
        ),
        out_shape=[
            jax.ShapeDtypeStruct(activations.shape, BF16),
            jax.ShapeDtypeStruct((tokens, rows), BF16),
        ]
        + ([one, one] if last else [jax.ShapeDtypeStruct((2 * tokens, columns), F32)]),
        input_output_aliases={} if first else {8: 0},
        compiler_params=pltpu.CompilerParams(vmem_limit_bytes=28 * MIB),
        cost_estimate=cost(
            8 * tokens * rows * columns,
            8 * tokens * rows + 2 * rows * columns + 8 * tokens * columns,
            1 if last else SHRINK,
        ),
        name="project",
    )(
        place, activations, other, cots, here, there,
        *([] if first else [so_far[2], got, so_far[0]]),
    )


def finish_kernel(place, got, near, far, last, arrived, whole, out, keys, weight, *, scale):
    out[...] = got[...]
    keys[...] = (near[...] + far[...]).astype(BF16)
    weight[...] = ((last[...] + arrived[...].astype(F32)) * scale).T.astype(BF16)


def finished(place, whole, got, keys_near, keys_far, last, arrived, scale):
    tokens, rows = got.shape
    cols, columns = last.shape[0], keys_near.shape[1]
    part, some = rows // 2, columns // 2
    wide = pl.BlockSpec((tokens, some), lambda r, s: (0, r))
    flat = pl.BlockSpec((cols, part), lambda r, s: (0, r))
    return pl.pallas_call(
        lambda *refs: finish_kernel(*refs, scale=scale),
        grid_spec=pltpu.PrefetchScalarGridSpec(
            num_scalar_prefetch=1,
            grid=(2,),
            in_specs=[
                pl.BlockSpec((tokens, part), lambda r, s: (0, r)),
                wide,
                wide,
                flat,
                flat,
                pl.BlockSpec(memory_space=pl.ANY),
            ],
            out_specs=[
                pl.BlockSpec((tokens, part), lambda r, s: (0, 2 * (2 * (s[0] ^ 3) + 1 - s[1]) + r)),
                wide,
                pl.BlockSpec((part, cols), lambda r, s: (r, 0)),
            ],
        ),
        out_shape=[
            jax.ShapeDtypeStruct(whole.shape, BF16),
            jax.ShapeDtypeStruct((tokens, columns), BF16),
            jax.ShapeDtypeStruct((rows, cols), BF16),
        ],
        input_output_aliases={6: 0},
        compiler_params=pltpu.CompilerParams(vmem_limit_bytes=12 * MIB),
        cost_estimate=cost(0, 4 * tokens * rows + 10 * tokens * columns),
        name="finish",
    )(place, got, keys_near, keys_far, last, arrived, whole)


def added(*arrays):
    total = arrays[0].astype(F32)
    for array in arrays[1:]:
        total = total + array.astype(F32)
    return total.astype(BF16)


def by_hops(activations, cotangent, kv_weight):
    rows = kv_weight.shape[0]
    tokens = activations.shape[0]
    place = jnp.stack([lax.axis_index(name) for name in ("chip", "core", "blk")]).astype(jnp.int32)

    other, cot_other = sent(activations, SWAP), sent(cotangent, SWAP)
    base = jnp.stack([kv_weight, sent(kv_weight, FLIP_A)])
    one, mid = sent(base, PAIR), sent(base, MID)
    base_b = sent(base, FLIP_B)

    keep3, send3, cots, turned = first_terms(
        place, activations, other, cotangent, cot_other, rows
    )
    got3 = sent(send3, FLIP_B)
    keep2, keep10, send2, send10 = terms(place, activations, other, turned, rows)
    first = gate(place, after(one, keep10), mid, base_b)
    got2 = sent(after(send2, first, got3), FLIP_B)

    sum3 = added(after(keep3, first), got3)
    far = sent(sum3, IN)
    two_mid = sent(after(one, first, keep10), MID)
    two_end = sent(mid, OUT)
    one_b = sent(after(one, got3), FLIP_B)
    whole, out, keys = projected(
        first, 0, after(activations, keep10), other, cots, base, base_b
    )
    got10 = sent(after(send10, got2, out), FLIP_B)
    got = sent(out, SWAP)
    sum2 = added(keep2, got2)
    two = two_mid + two_end
    near = sent(after(sum2, far, two, out, one_b), IN)
    mid_far = sent(added(sum2, far), MID)
    three_end = sent(after(two_mid, out), OUT)
    two_b = sent(after(two, got10), FLIP_B)
    whole, out, keys = projected(
        place, 1, after(activations, out), other, cots, one, one_b, (whole, None, keys), got
    )
    got = sent(out, SWAP)

    three = mid + three_end
    three_b = sent(after(three, two_b), FLIP_B)
    sum_mid = sent(added(sum3, after(near, three, out)), MID)
    sum_one = sent(added(keep10[1], got10[1], mid_far), PAIR)
    whole, out, keys = projected(
        place, 2, after(activations, out), other, cots, two, two_b, (whole, None, keys), got
    )
    got = sent(out, SWAP)
    sum_mid, sum_one = after(sum_mid, out), after(sum_one, out)
    last = [
        keep10[0, a].astype(F32)
        + got10[0, a].astype(F32)
        + sum_mid[a].astype(F32)
        + sum_one[a].astype(F32)
        for a in (0, 1)
    ]
    over = last[1].astype(BF16)
    arrived = sent(over, FLIP_A)

    whole, out, keys, keys_far = projected(
        place, 3, after(activations, over), other, cots, three, three_b, (whole, None, keys), got
    )
    grad_input, key_values, grad_weight = finished(
        place,
        whole,
        sent(out, SWAP),
        keys,
        sent(after(keys_far, arrived), SWAP),
        last[0],
        arrived,
        1.0 / math.sqrt(32 * tokens),
    )
    return (key_values, grad_input, grad_weight)


def swapped(array):
    return lax.ppermute(array, "core", [(0, 1), (1, 0)])


def by_collectives(activations, cotangent, kv_weight):
    blocks, chips = lax.axis_size("blk"), lax.axis_size("chip")
    core = lax.axis_index("core")
    tokens, features = activations.shape
    rows, cols = kv_weight.shape
    columns = cotangent.shape[1]
    by_core = activations.reshape(tokens, chips, 2, rows)
    mine = lax.dynamic_index_in_dim(by_core, core, 2, keepdims=False)
    other = lax.dynamic_index_in_dim(by_core, 1 - core, 2, keepdims=False)
    acts = jnp.concatenate([mine, swapped(other)], 0)
    cots = jnp.concatenate([cotangent, swapped(cotangent)], 0)
    weight = lax.all_gather(kv_weight, ("blk", "chip"), axis=0, tiled=False)
    weight = weight.reshape(blocks, chips, rows, cols)
    parts = jnp.einsum(
        "tzr,tbc->bzrc", acts, cots.reshape(2 * tokens, blocks, cols), preferred_element_type=F32
    ).astype(BF16).reshape(blocks * chips, rows, cols)
    total = lax.psum_scatter(parts, ("blk", "chip"), scatter_dimension=0, tiled=False)
    count = tokens * blocks * chips * 2
    grad_weight = (total.astype(F32) * (1.0 / math.sqrt(count))).astype(BF16)
    full = weight.transpose(1, 2, 0, 3).reshape(chips * rows, columns)
    keys = jnp.dot(acts.reshape(2 * tokens, chips * rows), full, preferred_element_type=F32)
    key_values = (keys[:tokens] + swapped(keys[tokens:])).astype(BF16)
    inputs = lax.dot_general(
        cots, full, (((1,), (1,)), ((), ())), preferred_element_type=F32
    ).astype(BF16).reshape(2 * tokens, chips, rows)
    near, far = inputs[:tokens], swapped(inputs[tokens:])
    low = jnp.where(core == 0, near, far)
    high = jnp.where(core == 0, far, near)
    grad_input = jnp.stack([low, high], 2).reshape(tokens, features)
    return (key_values, grad_input, grad_weight)


def solution(mesh):
    blocks, shards = mesh.shape["blk"], mesh.shape["shard"]
    split = Mesh(mesh.devices.reshape(blocks, shards // 2, 2), AXES)
    by_token = P(AXES, None)
    by_piece = P(("chip", "core"), "blk")
    return jax.shard_map(
        by_hops if (blocks, shards) == (4, 8) else by_collectives,
        mesh=split,
        in_specs=(by_token, by_token, by_piece),
        out_specs=(by_token, by_token, by_piece),
        check_vma=False,
    )
```

```python
import math

import jax
import jax.numpy as jnp
from jax import lax
from jax.experimental import pallas as pl
from jax.experimental.pallas import tpu as pltpu
from jax.sharding import Mesh, PartitionSpec as P

F32, BF16 = jnp.float32, jnp.bfloat16
AXES = ("blk", "chip", "core")
SHRINK = 1000
MIB = 2**20
GATE = 10**7
ONCE = pl.Buffered(1)


def hops(move):
    pairs = []
    for blk in range(4):
        for z in range(4):
            for core in range(2):
                to = move(blk, z, core)
                if to is not None:
                    pairs.append(((blk * 4 + z) * 2 + core, (to[0] * 4 + to[1]) * 2 + to[2]))
    return pairs


def middle(z):
    return z in (1, 2)


SWAP = hops(lambda b, z, c: (b, z, 1 - c))
FLIP_A = hops(lambda b, z, c: (b ^ (1 + c), z, c))
FLIP_B = hops(lambda b, z, c: (b ^ (2 - c), z, c))
PAIR = hops(lambda b, z, c: (b, z ^ 1, c))
MID = hops(lambda b, z, c: (b, z ^ 3, c) if middle(z) else None)
OUT = hops(lambda b, z, c: (b, z ^ 1, c) if middle(z) else None)
IN = hops(lambda b, z, c: (b, z ^ 1, c) if not middle(z) else None)


def after(array, *others):
    return lax.optimization_barrier((array, *others))[0]


def sent(array, pairs):
    return lax.ppermute(array, AXES, pairs)


def column_block(place, a, b):
    core = place[1]
    return place[2] ^ (a * (1 + core)) ^ (b * (2 - core))


def cost(flops, moved, shrink=SHRINK):
    return pl.CostEstimate(flops=flops // shrink, bytes_accessed=moved // shrink, transcendentals=0)


def gate(place, *arrays):
    def kernel(*refs):
        for i in range(3):
            refs[-1][i] = refs[0][i]

    return pl.pallas_call(
        kernel,
        in_specs=[pl.BlockSpec(memory_space=pltpu.SMEM)]
        + [pl.BlockSpec(memory_space=pl.ANY)] * len(arrays),
        out_specs=pl.BlockSpec(memory_space=pltpu.SMEM),
        out_shape=jax.ShapeDtypeStruct(place.shape, place.dtype),
        compiler_params=pltpu.CompilerParams(vmem_limit_bytes=MIB),
        cost_estimate=cost(0, GATE, 1),
        name="gate",
    )(place, *arrays)


def first_term_kernel(place, mine, other, cot_mine, cot_other, keep, send, cots, turned):
    tokens, cols = cot_mine.shape[0], cot_mine.shape[1] // 4

    @pl.when(pl.program_id(0) == 0)
    def _():
        for b in (0, 1):
            for a in (0, 1):
                at = pl.ds(pl.multiple_of(column_block(place, a, b) * cols, cols), cols)
                to = slice((2 * b + a) * cols, (2 * b + a + 1) * cols)
                for array, half in ((cot_mine, slice(0, tokens)), (cot_other, slice(tokens, None))):
                    piece = array[:, at]
                    cots[half, to] = piece
                    turned[to, half] = piece.T

    tall = jnp.concatenate([mine[...], other[...]], 0)
    for b, out in ((1, send), (0, keep)):
        part = turned[2 * b * cols : (2 * b + 2) * cols]
        out[...] = jnp.dot(part, tall, preferred_element_type=F32).astype(BF16).reshape(out.shape)


def first_terms(place, activations, other, cot_mine, cot_other, rows):
    tokens, columns = cot_mine.shape
    part, cols = rows // 2, columns // 4
    mine = pl.BlockSpec((tokens, part), lambda r, s: (0, 2 * (2 * (s[0] ^ 3) + s[1]) + r))
    piece = pl.BlockSpec((2, cols, part), lambda r, s: (0, 0, r))

    held = pl.BlockSpec((tokens, columns), lambda r, s: (0, 0), pipeline_mode=ONCE)

    def whole(*shape):
        return pl.BlockSpec(shape, lambda r, s: (0, 0))

    return pl.pallas_call(
        first_term_kernel,
        grid_spec=pltpu.PrefetchScalarGridSpec(
            num_scalar_prefetch=1,
            grid=(2,),
            in_specs=[mine, mine, held, held],
            out_specs=[piece, piece, whole(2 * tokens, columns), whole(columns, 2 * tokens)],
        ),
        out_shape=[jax.ShapeDtypeStruct((2, cols, rows), BF16)] * 2
        + [
            jax.ShapeDtypeStruct((2 * tokens, columns), BF16),
            jax.ShapeDtypeStruct((columns, 2 * tokens), BF16),
        ],
        compiler_params=pltpu.CompilerParams(vmem_limit_bytes=22 * MIB),
        cost_estimate=cost(4 * tokens * rows * columns, 4 * tokens * rows + 4 * rows * columns),
        name="terms",
    )(place, activations, other, cot_mine, cot_other)


def term_kernel(place, mine, other, turned, keep2, keep10, send2, send10):
    rows = turned.shape[0] // 2
    for first in (True, False):

        @pl.when((pl.program_id(0) == 0) == first)
        def _():
            tall = jnp.concatenate([mine[...], other[...]], 0)
            for b, out in ((1, send2 if first else send10), (0, keep2 if first else keep10)):
                part = turned[b * rows : (b + 1) * rows]
                out[...] = (
                    jnp.dot(part, tall, preferred_element_type=F32).astype(BF16).reshape(out.shape)
                )


def terms(place, activations, other, turned, rows):
    columns, tokens = turned.shape[0], activations.shape[0]
    part, cols = rows // 2, columns // 4
    mine = pl.BlockSpec((tokens, part), lambda i, r, s: (0, 2 * (2 * (s[0] ^ (2 - i)) + s[1]) + r))
    pieces = [
        pl.BlockSpec((2, cols, part), lambda i, r, s: (0, 0, jnp.where(i == 0, r, 1))),
        pl.BlockSpec(
            (1, 2, cols, part),
            lambda i, r, s: (jnp.where(i == 2, 0, 1), 0, 0, jnp.where(i == 0, 0, r)),
        ),
    ]
    return pl.pallas_call(
        term_kernel,
        grid_spec=pltpu.PrefetchScalarGridSpec(
            num_scalar_prefetch=1,
            grid=(3, 2),
            in_specs=[mine, mine, pl.BlockSpec(turned.shape, lambda i, r, s: (0, 0), pipeline_mode=ONCE)],
            out_specs=pieces * 2,
        ),
        out_shape=[
            jax.ShapeDtypeStruct((2, cols, rows), BF16),
            jax.ShapeDtypeStruct((2, 2, cols, rows), BF16),
        ]
        * 2,
        compiler_params=pltpu.CompilerParams(vmem_limit_bytes=16 * MIB),
        cost_estimate=cost(12 * tokens * rows * columns, 12 * tokens * rows + 12 * rows * columns),
        name="terms",
    )(place, activations, other, turned)


def project_kernel(place, acts, other, cots, here, there, *refs, first, last, lays):
    near, far, *keys = refs[0 if first else 2 + lays : -1]
    acc = refs[-1]
    tokens, cols = acts.shape[0], here.shape[2]
    step = pl.program_id(0)

    @pl.when(step < 2)
    def _():
        weight = jnp.concatenate([here[0], here[1], there[0], there[1]], 1)
        total = lax.dot_general(
            cots[...], weight, (((1,), (1,)), ((), ())), preferred_element_type=F32
        ).astype(BF16)
        near[...] = total[:tokens]
        far[...] = total[tokens:]
        tall = jnp.concatenate([acts[...], other[...]], 0)
        sums = jnp.dot(tall, weight, preferred_element_type=F32)

        @pl.when(step == 0)
        def _():
            acc[...] = sums if first else refs[0][...] + sums

        @pl.when(step == 1)
        def _():
            if last:
                for b in (0, 1):
                    for a in (0, 1):
                        at = pl.ds(pl.multiple_of(column_block(place, a, b) * cols, cols), cols)
                        to = slice((2 * b + a) * cols, (2 * b + a + 1) * cols)
                        keys[0][:, at] = acc[:tokens, to] + sums[:tokens, to]
                        keys[1][:, at] = acc[tokens:, to] + sums[tokens:, to]
            else:
                keys[0][...] = acc[...] + sums

    if lays:

        @pl.when(step >= 2)
        def _():
            near[...] = refs[1][...]


def projected(place, k, activations, other, cots, here, there, so_far=None, got=None):
    tokens, columns = activations.shape[0], cots.shape[1]
    _, rows, cols = here.shape
    part = rows // 2
    first, last, lays = k == 0, k == 3, got is not None

    def whole(*shape):
        return pl.BlockSpec(shape, lambda r, s: (0, 0))

    held = pl.BlockSpec((2 * tokens, columns), lambda r, s: (0, 0), pipeline_mode=ONCE)

    def out_at(r, s):
        own = 2 * (2 * (s[0] ^ k) + s[1]) + r
        received = 2 * (2 * (s[0] ^ (k - 2)) + 1 - s[1]) + r - 2
        return (0, jnp.where(r < 2, own, received) if lays else own)

    mine = pl.BlockSpec(
        (tokens, part), lambda r, s: (0, 2 * (2 * (s[0] ^ k) + s[1]) + jnp.minimum(r, 1))
    )
    piece = pl.BlockSpec((2, part, cols), lambda r, s: (0, jnp.minimum(r, 1), 0))
    one = jax.ShapeDtypeStruct((tokens, columns), F32)
    return pl.pallas_call(
        lambda *refs: project_kernel(*refs, first=first, last=last, lays=lays),
        grid_spec=pltpu.PrefetchScalarGridSpec(
            num_scalar_prefetch=1,
            grid=(4 if lays else 2,),
            in_specs=[mine, mine, held, piece, piece]
            + ([] if first else [held])
            + ([pl.BlockSpec((tokens, part), lambda r, s: (0, jnp.maximum(r - 2, 0)))] * lays)
            + ([] if first else [pl.BlockSpec(memory_space=pl.ANY)]),
            out_specs=[
                pl.BlockSpec((tokens, part), out_at),
                pl.BlockSpec((tokens, part), lambda r, s: (0, jnp.minimum(r, 1))),
            ]
            + ([whole(tokens, columns)] * 2 if last else [whole(2 * tokens, columns)]),
            scratch_shapes=[pltpu.VMEM((2 * tokens, columns), F32)],
        ),
        out_shape=[
            jax.ShapeDtypeStruct(activations.shape, BF16),
            jax.ShapeDtypeStruct((tokens, rows), BF16),
        ]
        + ([one, one] if last else [jax.ShapeDtypeStruct((2 * tokens, columns), F32)]),
        input_output_aliases={} if first else {7 + lays: 0},
        compiler_params=pltpu.CompilerParams(vmem_limit_bytes=28 * MIB),
        cost_estimate=cost(
            8 * tokens * rows * columns,
            8 * tokens * rows + 2 * rows * columns + 8 * tokens * columns,
        ),
        name="project",
    )(
        place, activations, other, cots, here, there,
        *([] if first else [so_far[2], *([got] * lays), so_far[0]]),
    )


def finish_kernel(place, got2, got3, near, far, last, arrived, whole, out, keys, weight, *, scale):
    for k, got in ((0, got2), (1, got3)):

        @pl.when(lax.div(pl.program_id(0), 2) == k)
        def _():
            out[...] = got[...]

    keys[...] = (near[...] + far[...]).astype(BF16)
    weight[...] = ((last[...] + arrived[...].astype(F32)) * scale).T.astype(BF16)


def finished(place, whole, got2, got3, keys_near, keys_far, last, arrived, scale):
    tokens, rows = got3.shape
    cols, columns = last.shape[0], keys_near.shape[1]
    part = rows // 2
    wide = pl.BlockSpec((tokens, columns // 4), lambda r, s: (0, r))
    flat = pl.BlockSpec((cols, rows // 4), lambda r, s: (0, r))

    def laid_at(r, s):
        return (0, 2 * (2 * (s[0] ^ (2 + lax.div(r, 2))) + 1 - s[1]) + lax.rem(r, 2))

    return pl.pallas_call(
        lambda *refs: finish_kernel(*refs, scale=scale),
        grid_spec=pltpu.PrefetchScalarGridSpec(
            num_scalar_prefetch=1,
            grid=(4,),
            in_specs=[
                pl.BlockSpec((tokens, part), lambda r, s: (0, jnp.minimum(r, 1))),
                pl.BlockSpec((tokens, part), lambda r, s: (0, jnp.maximum(r - 2, 0))),
                wide,
                wide,
                flat,
                flat,
                pl.BlockSpec(memory_space=pl.ANY),
            ],
            out_specs=[
                pl.BlockSpec((tokens, part), laid_at),
                wide,
                pl.BlockSpec((rows // 4, cols), lambda r, s: (r, 0)),
            ],
        ),
        out_shape=[
            jax.ShapeDtypeStruct(whole.shape, BF16),
            jax.ShapeDtypeStruct((tokens, columns), BF16),
            jax.ShapeDtypeStruct((rows, cols), BF16),
        ],
        input_output_aliases={7: 0},
        compiler_params=pltpu.CompilerParams(vmem_limit_bytes=12 * MIB),
        cost_estimate=cost(0, 8 * tokens * rows + 10 * tokens * columns),
        name="finish",
    )(place, got2, got3, keys_near, keys_far, last, arrived, whole)


def added(*arrays):
    total = arrays[0].astype(F32)
    for array in arrays[1:]:
        total = total + array.astype(F32)
    return total.astype(BF16)


def by_hops(activations, cotangent, kv_weight):
    rows = kv_weight.shape[0]
    tokens = activations.shape[0]
    place = jnp.stack([lax.axis_index(name) for name in ("chip", "core", "blk")]).astype(jnp.int32)

    other, cot_other = sent(activations, SWAP), sent(cotangent, SWAP)
    base = jnp.stack([kv_weight, sent(kv_weight, FLIP_A)])
    one, mid = sent(base, PAIR), sent(base, MID)
    base_b = sent(base, FLIP_B)

    keep3, send3, cots, turned = first_terms(
        place, activations, other, cotangent, cot_other, rows
    )
    got3 = sent(send3, FLIP_B)
    keep2, keep10, send2, send10 = terms(place, activations, other, turned, rows)
    first = gate(place, after(one, keep10), mid, base_b)
    got2 = sent(after(send2, first, got3), FLIP_B)

    sum3 = added(after(keep3, first), got3)
    far = sent(sum3, IN)
    two_mid = sent(after(one, first, sum3), MID)
    two_end = sent(after(mid, sum3), OUT)
    one_b = sent(after(one, got3), FLIP_B)
    whole, out0, keys = projected(
        first, 0, after(activations, keep10, sum3), other, cots, base, base_b
    )
    got0 = sent(out0, SWAP)
    second = gate(place, after(far, out0), two_mid, two_end, got2, one_b)

    sum2_far = added(after(keep2, second), got2, far)
    mid_far = sent(sum2_far, MID)
    near = sent(after(added(keep2, got2), sum2_far), IN)
    three_end = sent(after(two_mid, second), OUT)
    got10 = sent(after(send10, second), FLIP_B)
    two = after(two_mid, second) + two_end
    whole, out1, keys = projected(
        second, 1, after(activations, sum2_far), other, cots, one, one_b, (whole, None, keys)
    )
    got1 = sent(out1, SWAP)
    third = gate(place, after(near, out1), mid_far, three_end, got10)

    sum1 = added(after(keep10[1], third), got10[1], mid_far)
    sum_one = sent(sum1, PAIR)
    sum3_near = added(sum3, after(near, third))
    sum_mid = sent(sum3_near, MID)
    two_b = sent(after(two, third), FLIP_B)
    three = after(mid, third) + three_end
    three_b = sent(three, FLIP_B)
    whole, out2, keys = projected(
        third, 2, after(activations, sum3_near), other, cots, two, two_b, (whole, None, keys), got0
    )
    whole, out3, keys, keys_far = projected(
        place, 3, after(activations, out2), other, cots, three, three_b, (whole, None, keys), got1
    )
    sum_mid, sum_one = after(sum_mid, out3), after(sum_one, out3)
    last = [
        keep10[0, a].astype(F32)
        + got10[0, a].astype(F32)
        + sum_mid[a].astype(F32)
        + sum_one[a].astype(F32)
        for a in (0, 1)
    ]
    grad_input, key_values, grad_weight = finished(
        place,
        whole,
        sent(out2, SWAP),
        sent(out3, SWAP),
        keys,
        sent(keys_far, SWAP),
        last[0],
        sent(last[1].astype(BF16), FLIP_A),
        1.0 / math.sqrt(32 * tokens),
    )
    return (key_values, grad_input, grad_weight)


def swapped(array):
    return lax.ppermute(array, "core", [(0, 1), (1, 0)])


def by_collectives(activations, cotangent, kv_weight):
    blocks, chips = lax.axis_size("blk"), lax.axis_size("chip")
    core = lax.axis_index("core")
    tokens, features = activations.shape
    rows, cols = kv_weight.shape
    columns = cotangent.shape[1]
    by_core = activations.reshape(tokens, chips, 2, rows)
    mine = lax.dynamic_index_in_dim(by_core, core, 2, keepdims=False)
    other = lax.dynamic_index_in_dim(by_core, 1 - core, 2, keepdims=False)
    acts = jnp.concatenate([mine, swapped(other)], 0)
    cots = jnp.concatenate([cotangent, swapped(cotangent)], 0)
    weight = lax.all_gather(kv_weight, ("blk", "chip"), axis=0, tiled=False)
    weight = weight.reshape(blocks, chips, rows, cols)
    parts = jnp.einsum(
        "tzr,tbc->bzrc", acts, cots.reshape(2 * tokens, blocks, cols), preferred_element_type=F32
    ).astype(BF16).reshape(blocks * chips, rows, cols)
    total = lax.psum_scatter(parts, ("blk", "chip"), scatter_dimension=0, tiled=False)
    count = tokens * blocks * chips * 2
    grad_weight = (total.astype(F32) * (1.0 / math.sqrt(count))).astype(BF16)
    full = weight.transpose(1, 2, 0, 3).reshape(chips * rows, columns)
    keys = jnp.dot(acts.reshape(2 * tokens, chips * rows), full, preferred_element_type=F32)
    key_values = (keys[:tokens] + swapped(keys[tokens:])).astype(BF16)
    inputs = lax.dot_general(
        cots, full, (((1,), (1,)), ((), ())), preferred_element_type=F32
    ).astype(BF16).reshape(2 * tokens, chips, rows)
    near, far = inputs[:tokens], swapped(inputs[tokens:])
    low = jnp.where(core == 0, near, far)
    high = jnp.where(core == 0, far, near)
    grad_input = jnp.stack([low, high], 2).reshape(tokens, features)
    return (key_values, grad_input, grad_weight)


def solution(mesh):
    blocks, shards = mesh.shape["blk"], mesh.shape["shard"]
    split = Mesh(mesh.devices.reshape(blocks, shards // 2, 2), AXES)
    by_token = P(AXES, None)
    by_piece = P(("chip", "core"), "blk")
    return jax.shard_map(
        by_hops if (blocks, shards) == (4, 8) else by_collectives,
        mesh=split,
        in_specs=(by_token, by_token, by_piece),
        out_specs=(by_token, by_token, by_piece),
        check_vma=False,
    )
```

```python
import math

import jax
import jax.numpy as jnp
from jax import lax
from jax.experimental import pallas as pl
from jax.experimental.pallas import tpu as pltpu
from jax.sharding import Mesh, PartitionSpec as P

F32, BF16 = jnp.float32, jnp.bfloat16
AXES = ("blk", "chip", "core")
SHRINK = 1000
MIB = 2**20
GATE = 10**7
ONCE = pl.Buffered(1)


def hops(move):
    pairs = []
    for blk in range(4):
        for z in range(4):
            for core in range(2):
                to = move(blk, z, core)
                if to is not None:
                    pairs.append(((blk * 4 + z) * 2 + core, (to[0] * 4 + to[1]) * 2 + to[2]))
    return pairs


def middle(z):
    return z in (1, 2)


SWAP = hops(lambda b, z, c: (b, z, 1 - c))
FLIP_A = hops(lambda b, z, c: (b ^ (1 + c), z, c))
FLIP_B = hops(lambda b, z, c: (b ^ (2 - c), z, c))
PAIR = hops(lambda b, z, c: (b, z ^ 1, c))
MID = hops(lambda b, z, c: (b, z ^ 3, c) if middle(z) else None)
OUT = hops(lambda b, z, c: (b, z ^ 1, c) if middle(z) else None)
IN = hops(lambda b, z, c: (b, z ^ 1, c) if not middle(z) else None)


def after(array, *others):
    return lax.optimization_barrier((array, *others))[0]


def sent(array, pairs):
    return lax.ppermute(array, AXES, pairs)


def column_block(place, a, b):
    core = place[1]
    return place[2] ^ (a * (1 + core)) ^ (b * (2 - core))


def cost(flops, moved, shrink=SHRINK):
    return pl.CostEstimate(flops=flops // shrink, bytes_accessed=moved // shrink, transcendentals=0)


def gate(place, *arrays):
    def kernel(*refs):
        for i in range(3):
            refs[-1][i] = refs[0][i]

    return pl.pallas_call(
        kernel,
        in_specs=[pl.BlockSpec(memory_space=pltpu.SMEM)]
        + [pl.BlockSpec(memory_space=pl.ANY)] * len(arrays),
        out_specs=pl.BlockSpec(memory_space=pltpu.SMEM),
        out_shape=jax.ShapeDtypeStruct(place.shape, place.dtype),
        compiler_params=pltpu.CompilerParams(vmem_limit_bytes=MIB),
        cost_estimate=cost(0, GATE, 1),
        name="gate",
    )(place, *arrays)


def first_term_kernel(place, mine, other, cot_mine, cot_other, keep, send, cots, turned):
    tokens, cols = cot_mine.shape[0], cot_mine.shape[1] // 4

    @pl.when(pl.program_id(0) == 0)
    def _():
        for b in (0, 1):
            for a in (0, 1):
                at = pl.ds(pl.multiple_of(column_block(place, a, b) * cols, cols), cols)
                to = slice((2 * b + a) * cols, (2 * b + a + 1) * cols)
                for array, half in ((cot_mine, slice(0, tokens)), (cot_other, slice(tokens, None))):
                    piece = array[:, at]
                    cots[half, to] = piece
                    turned[to, half] = piece.T

    tall = jnp.concatenate([mine[...], other[...]], 0)
    for b, out in ((1, send), (0, keep)):
        part = turned[2 * b * cols : (2 * b + 2) * cols]
        out[...] = jnp.dot(part, tall, preferred_element_type=F32).astype(BF16).reshape(out.shape)


def first_terms(place, activations, other, cot_mine, cot_other, rows):
    tokens, columns = cot_mine.shape
    part, cols = rows // 2, columns // 4
    mine = pl.BlockSpec((tokens, part), lambda r, s: (0, 2 * (2 * (s[0] ^ 3) + s[1]) + r))
    piece = pl.BlockSpec((2, cols, part), lambda r, s: (0, 0, r))

    held = pl.BlockSpec((tokens, columns), lambda r, s: (0, 0), pipeline_mode=ONCE)

    def whole(*shape):
        return pl.BlockSpec(shape, lambda r, s: (0, 0))

    return pl.pallas_call(
        first_term_kernel,
        grid_spec=pltpu.PrefetchScalarGridSpec(
            num_scalar_prefetch=1,
            grid=(2,),
            in_specs=[mine, mine, held, held],
            out_specs=[piece, piece, whole(2 * tokens, columns), whole(columns, 2 * tokens)],
        ),
        out_shape=[jax.ShapeDtypeStruct((2, cols, rows), BF16)] * 2
        + [
            jax.ShapeDtypeStruct((2 * tokens, columns), BF16),
            jax.ShapeDtypeStruct((columns, 2 * tokens), BF16),
        ],
        compiler_params=pltpu.CompilerParams(vmem_limit_bytes=22 * MIB),
        cost_estimate=cost(4 * tokens * rows * columns, 4 * tokens * rows + 4 * rows * columns),
        name="terms",
    )(place, activations, other, cot_mine, cot_other)


def term_kernel(place, mine, other, turned, *outs):
    rows = turned.shape[0] // 2
    for i in range(3):

        @pl.when(pl.program_id(0) == i)
        def _():
            tall = jnp.concatenate([mine[...], other[...]], 0)
            for b in (1, 0):
                out = outs[3 * b + i]
                part = turned[b * rows : (b + 1) * rows]
                out[...] = (
                    jnp.dot(part, tall, preferred_element_type=F32).astype(BF16).reshape(out.shape)
                )


def terms(place, activations, other, turned, rows):
    columns, tokens = turned.shape[0], activations.shape[0]
    part, cols = rows // 2, columns // 4
    mine = pl.BlockSpec((tokens, part), lambda i, r, s: (0, 2 * (2 * (s[0] ^ (2 - i)) + s[1]) + r))
    pieces = [
        pl.BlockSpec((2, cols, part), lambda i, r, s, n=n: (0, 0, jnp.clip(2 * (i - n) + r, 0, 1)))
        for n in range(3)
    ]
    return pl.pallas_call(
        term_kernel,
        grid_spec=pltpu.PrefetchScalarGridSpec(
            num_scalar_prefetch=1,
            grid=(3, 2),
            in_specs=[
                mine,
                mine,
                pl.BlockSpec(turned.shape, lambda i, r, s: (0, 0), pipeline_mode=ONCE),
            ],
            out_specs=pieces * 2,
        ),
        out_shape=[jax.ShapeDtypeStruct((2, cols, rows), BF16)] * 6,
        compiler_params=pltpu.CompilerParams(vmem_limit_bytes=18 * MIB),
        cost_estimate=cost(12 * tokens * rows * columns, 12 * tokens * rows + 12 * rows * columns),
        name="terms",
    )(place, activations, other, turned)


def project_kernel(place, acts, other, cots, here, there, *refs, first, last, lays):
    near, far, *keys = refs[0 if first else 2 + lays : -1]
    acc = refs[-1]
    tokens, cols = acts.shape[0], here.shape[2]
    step = pl.program_id(0)

    @pl.when(step < 2)
    def _():
        weight = jnp.concatenate([here[0], here[1], there[0], there[1]], 1)
        total = lax.dot_general(
            cots[...], weight, (((1,), (1,)), ((), ())), preferred_element_type=F32
        ).astype(BF16)
        near[...] = total[:tokens]
        far[...] = total[tokens:]
        tall = jnp.concatenate([acts[...], other[...]], 0)
        sums = jnp.dot(tall, weight, preferred_element_type=F32)

        @pl.when(step == 0)
        def _():
            acc[...] = sums if first else refs[0][...] + sums

        @pl.when(step == 1)
        def _():
            if last:
                for b in (0, 1):
                    for a in (0, 1):
                        at = pl.ds(pl.multiple_of(column_block(place, a, b) * cols, cols), cols)
                        to = slice((2 * b + a) * cols, (2 * b + a + 1) * cols)
                        keys[0][:, at] = acc[:tokens, to] + sums[:tokens, to]
                        keys[1][:, at] = acc[tokens:, to] + sums[tokens:, to]
            else:
                keys[0][...] = acc[...] + sums

    if lays:

        @pl.when(step >= 2)
        def _():
            near[...] = refs[1][...]


def projected(place, k, activations, other, cots, here, there, so_far=None, got=None):
    tokens, columns = activations.shape[0], cots.shape[1]
    _, rows, cols = here.shape
    part = rows // 2
    first, last, lays = k == 0, k == 3, got is not None

    def whole(*shape):
        return pl.BlockSpec(shape, lambda r, s: (0, 0))

    held = pl.BlockSpec((2 * tokens, columns), lambda r, s: (0, 0), pipeline_mode=ONCE)

    def out_at(r, s):
        own = 2 * (2 * (s[0] ^ k) + s[1]) + r
        received = 2 * (2 * (s[0] ^ (k - 2)) + 1 - s[1]) + r - 2
        return (0, jnp.where(r < 2, own, received) if lays else own)

    mine = pl.BlockSpec(
        (tokens, part), lambda r, s: (0, 2 * (2 * (s[0] ^ k) + s[1]) + jnp.minimum(r, 1))
    )
    piece = pl.BlockSpec((2, part, cols), lambda r, s: (0, jnp.minimum(r, 1), 0))
    one = jax.ShapeDtypeStruct((tokens, columns), F32)
    return pl.pallas_call(
        lambda *refs: project_kernel(*refs, first=first, last=last, lays=lays),
        grid_spec=pltpu.PrefetchScalarGridSpec(
            num_scalar_prefetch=1,
            grid=(4 if lays else 2,),
            in_specs=[mine, mine, held, piece, piece]
            + ([] if first else [held])
            + ([pl.BlockSpec((tokens, part), lambda r, s: (0, jnp.maximum(r - 2, 0)))] * lays)
            + ([] if first else [pl.BlockSpec(memory_space=pl.ANY)]),
            out_specs=[
                pl.BlockSpec((tokens, part), out_at),
                pl.BlockSpec((tokens, part), lambda r, s: (0, jnp.minimum(r, 1))),
            ]
            + ([whole(tokens, columns)] * 2 if last else [whole(2 * tokens, columns)]),
            scratch_shapes=[pltpu.VMEM((2 * tokens, columns), F32)],
        ),
        out_shape=[
            jax.ShapeDtypeStruct(activations.shape, BF16),
            jax.ShapeDtypeStruct((tokens, rows), BF16),
        ]
        + ([one, one] if last else [jax.ShapeDtypeStruct((2 * tokens, columns), F32)]),
        input_output_aliases={} if first else {7 + lays: 0},
        compiler_params=pltpu.CompilerParams(vmem_limit_bytes=28 * MIB),
        cost_estimate=cost(
            8 * tokens * rows * columns,
            8 * tokens * rows + 2 * rows * columns + 8 * tokens * columns,
        ),
        name="project",
    )(
        place, activations, other, cots, here, there,
        *([] if first else [so_far[2], *([got] * lays), so_far[0]]),
    )


def finish_kernel(place, got2, got3, near, far, last, arrived, whole, out, keys, weight, *, scale):
    for k, got in ((0, got2), (1, got3)):

        @pl.when(lax.div(pl.program_id(0), 2) == k)
        def _():
            out[...] = got[...]

    keys[...] = (near[...] + far[...]).astype(BF16)
    weight[...] = ((last[...] + arrived[...].astype(F32)) * scale).T.astype(BF16)


def finished(place, whole, got2, got3, keys_near, keys_far, last, arrived, scale):
    tokens, rows = got3.shape
    cols, columns = last.shape[0], keys_near.shape[1]
    part = rows // 2
    wide = pl.BlockSpec((tokens, columns // 4), lambda r, s: (0, r))
    flat = pl.BlockSpec((cols, rows // 4), lambda r, s: (0, r))

    def laid_at(r, s):
        return (0, 2 * (2 * (s[0] ^ (2 + lax.div(r, 2))) + 1 - s[1]) + lax.rem(r, 2))

    return pl.pallas_call(
        lambda *refs: finish_kernel(*refs, scale=scale),
        grid_spec=pltpu.PrefetchScalarGridSpec(
            num_scalar_prefetch=1,
            grid=(4,),
            in_specs=[
                pl.BlockSpec((tokens, part), lambda r, s: (0, jnp.minimum(r, 1))),
                pl.BlockSpec((tokens, part), lambda r, s: (0, jnp.maximum(r - 2, 0))),
                wide,
                wide,
                flat,
                flat,
                pl.BlockSpec(memory_space=pl.ANY),
            ],
            out_specs=[
                pl.BlockSpec((tokens, part), laid_at),
                wide,
                pl.BlockSpec((rows // 4, cols), lambda r, s: (r, 0)),
            ],
        ),
        out_shape=[
            jax.ShapeDtypeStruct(whole.shape, BF16),
            jax.ShapeDtypeStruct((tokens, columns), BF16),
            jax.ShapeDtypeStruct((rows, cols), BF16),
        ],
        input_output_aliases={7: 0},
        compiler_params=pltpu.CompilerParams(vmem_limit_bytes=12 * MIB),
        cost_estimate=cost(0, 8 * tokens * rows + 10 * tokens * columns),
        name="finish",
    )(place, got2, got3, keys_near, keys_far, last, arrived, whole)


def added(*arrays):
    total = arrays[0].astype(F32)
    for array in arrays[1:]:
        total = total + array.astype(F32)
    return total.astype(BF16)


def by_hops(activations, cotangent, kv_weight):
    rows = kv_weight.shape[0]
    tokens = activations.shape[0]
    place = jnp.stack([lax.axis_index(name) for name in ("chip", "core", "blk")]).astype(jnp.int32)

    other, cot_other = sent(activations, SWAP), sent(cotangent, SWAP)
    base = jnp.stack([kv_weight, sent(kv_weight, FLIP_A)])
    one, mid = sent(base, PAIR), sent(base, MID)
    base_b = sent(base, FLIP_B)

    keep3, send3, cots, turned = first_terms(
        place, activations, other, cotangent, cot_other, rows
    )
    got3 = sent(send3, FLIP_B)
    keep2, keep1, keep0, send2, send1, send0 = terms(place, activations, other, turned, rows)
    first = gate(place, after(one, keep0), mid, base_b)

    sum3 = added(after(keep3, first), got3)
    far = sent(sum3, IN)
    two_mid = sent(after(one, first, sum3), MID)
    two_end = sent(after(mid, sum3), OUT)
    got2 = sent(after(send2, sum3), FLIP_B)
    one_b = sent(after(one, sum3), FLIP_B)
    whole, out0, keys = projected(
        first, 0, after(activations, keep0, sum3), other, cots, base, base_b
    )
    got_out0 = sent(out0, SWAP)

    sum2_far = added(after(far, two_mid, two_end, one_b, out0), keep2, got2)
    mid_far = sent(sum2_far, MID)
    near = sent(after(added(keep2, got2), sum2_far), IN)
    three_end = sent(after(two_mid, sum2_far), OUT)
    got1 = sent(after(send1, sum2_far), FLIP_B)
    two = after(two_mid, sum2_far) + two_end
    two_b = sent(two, FLIP_B)
    whole, out1, keys = projected(
        place, 1, after(activations, sum2_far), other, cots, one, one_b, (whole, None, keys)
    )
    got_out1 = sent(out1, SWAP)

    sum1 = added(after(mid_far, near, three_end, two_b, out1), keep1, got1)
    sum_one = sent(sum1, PAIR)
    sum3_near = added(sum3, after(near, sum1))
    sum_mid = sent(sum3_near, MID)
    three = after(mid, sum1) + three_end
    three_b = sent(three, FLIP_B)
    got0 = sent(after(send0, three_b), FLIP_B)
    whole, out2, keys = projected(
        place,
        2,
        after(activations, sum3_near),
        other,
        cots,
        two,
        two_b,
        (whole, None, keys),
        got_out0,
    )
    whole, out3, keys, keys_far = projected(
        place, 3, after(activations, out2), other, cots, three, three_b, (whole, None, keys), got_out1
    )
    sum_mid, sum_one = after(sum_mid, out3), after(sum_one, out3)
    last = [
        keep0[a].astype(F32)
        + got0[a].astype(F32)
        + sum_mid[a].astype(F32)
        + sum_one[a].astype(F32)
        for a in (0, 1)
    ]
    grad_input, key_values, grad_weight = finished(
        place,
        whole,
        sent(out2, SWAP),
        sent(out3, SWAP),
        keys,
        sent(keys_far, SWAP),
        last[0],
        sent(last[1].astype(BF16), FLIP_A),
        1.0 / math.sqrt(32 * tokens),
    )
    return (key_values, grad_input, grad_weight)


def swapped(array):
    return lax.ppermute(array, "core", [(0, 1), (1, 0)])


def by_collectives(activations, cotangent, kv_weight):
    blocks, chips = lax.axis_size("blk"), lax.axis_size("chip")
    core = lax.axis_index("core")
    tokens, features = activations.shape
    rows, cols = kv_weight.shape
    columns = cotangent.shape[1]
    by_core = activations.reshape(tokens, chips, 2, rows)
    mine = lax.dynamic_index_in_dim(by_core, core, 2, keepdims=False)
    other = lax.dynamic_index_in_dim(by_core, 1 - core, 2, keepdims=False)
    acts = jnp.concatenate([mine, swapped(other)], 0)
    cots = jnp.concatenate([cotangent, swapped(cotangent)], 0)
    weight = lax.all_gather(kv_weight, ("blk", "chip"), axis=0, tiled=False)
    weight = weight.reshape(blocks, chips, rows, cols)
    parts = jnp.einsum(
        "tzr,tbc->bzrc", acts, cots.reshape(2 * tokens, blocks, cols), preferred_element_type=F32
    ).astype(BF16).reshape(blocks * chips, rows, cols)
    total = lax.psum_scatter(parts, ("blk", "chip"), scatter_dimension=0, tiled=False)
    count = tokens * blocks * chips * 2
    grad_weight = (total.astype(F32) * (1.0 / math.sqrt(count))).astype(BF16)
    full = weight.transpose(1, 2, 0, 3).reshape(chips * rows, columns)
    keys = jnp.dot(acts.reshape(2 * tokens, chips * rows), full, preferred_element_type=F32)
    key_values = (keys[:tokens] + swapped(keys[tokens:])).astype(BF16)
    inputs = lax.dot_general(
        cots, full, (((1,), (1,)), ((), ())), preferred_element_type=F32
    ).astype(BF16).reshape(2 * tokens, chips, rows)
    near, far = inputs[:tokens], swapped(inputs[tokens:])
    low = jnp.where(core == 0, near, far)
    high = jnp.where(core == 0, far, near)
    grad_input = jnp.stack([low, high], 2).reshape(tokens, features)
    return (key_values, grad_input, grad_weight)


def solution(mesh):
    blocks, shards = mesh.shape["blk"], mesh.shape["shard"]
    split = Mesh(mesh.devices.reshape(blocks, shards // 2, 2), AXES)
    by_token = P(AXES, None)
    by_piece = P(("chip", "core"), "blk")
    return jax.shard_map(
        by_hops if (blocks, shards) == (4, 8) else by_collectives,
        mesh=split,
        in_specs=(by_token, by_token, by_piece),
        out_specs=(by_token, by_token, by_piece),
        check_vma=False,
    )
```

```python
import math

import jax
import jax.numpy as jnp
from jax import lax
from jax.experimental import pallas as pl
from jax.experimental.pallas import tpu as pltpu
from jax.sharding import Mesh, PartitionSpec as P

F32, BF16 = jnp.float32, jnp.bfloat16
AXES = ("blk", "chip", "core")
SHRINK = 1000
MIB = 2**20
GATE = 10**7
ONCE = pl.Buffered(1)


def hops(move):
    pairs = []
    for blk in range(4):
        for z in range(4):
            for core in range(2):
                to = move(blk, z, core)
                if to is not None:
                    pairs.append(((blk * 4 + z) * 2 + core, (to[0] * 4 + to[1]) * 2 + to[2]))
    return pairs


def middle(z):
    return z in (1, 2)


SWAP = hops(lambda b, z, c: (b, z, 1 - c))
FLIP_A = hops(lambda b, z, c: (b ^ (1 + c), z, c))
FLIP_B = hops(lambda b, z, c: (b ^ (2 - c), z, c))
PAIR = hops(lambda b, z, c: (b, z ^ 1, c))
MID = hops(lambda b, z, c: (b, z ^ 3, c) if middle(z) else None)
OUT = hops(lambda b, z, c: (b, z ^ 1, c) if middle(z) else None)
IN = hops(lambda b, z, c: (b, z ^ 1, c) if not middle(z) else None)


def after(array, *others):
    return lax.optimization_barrier((array, *others))[0]


def sent(array, pairs):
    return lax.ppermute(array, AXES, pairs)


def column_block(place, a, b):
    core = place[1]
    return place[2] ^ (a * (1 + core)) ^ (b * (2 - core))


def cost(flops, moved, shrink=SHRINK):
    return pl.CostEstimate(flops=flops // shrink, bytes_accessed=moved // shrink, transcendentals=0)


def gate(place, *arrays):
    def kernel(*refs):
        for i in range(3):
            refs[-1][i] = refs[0][i]

    return pl.pallas_call(
        kernel,
        in_specs=[pl.BlockSpec(memory_space=pltpu.SMEM)]
        + [pl.BlockSpec(memory_space=pl.ANY)] * len(arrays),
        out_specs=pl.BlockSpec(memory_space=pltpu.SMEM),
        out_shape=jax.ShapeDtypeStruct(place.shape, place.dtype),
        compiler_params=pltpu.CompilerParams(vmem_limit_bytes=MIB),
        cost_estimate=cost(0, GATE, 1),
        name="gate",
    )(place, *arrays)


def first_term_kernel(place, mine, other, cot_mine, cot_other, keep, send, cots, turned):
    tokens, cols = cot_mine.shape[0], cot_mine.shape[1] // 4

    @pl.when(pl.program_id(0) == 0)
    def _():
        for b in (0, 1):
            for a in (0, 1):
                at = pl.ds(pl.multiple_of(column_block(place, a, b) * cols, cols), cols)
                to = slice((2 * b + a) * cols, (2 * b + a + 1) * cols)
                for array, half in ((cot_mine, slice(0, tokens)), (cot_other, slice(tokens, None))):
                    piece = array[:, at]
                    cots[half, to] = piece
                    turned[to, half] = piece.T

    tall = jnp.concatenate([mine[...], other[...]], 0)
    for b, out in ((1, send), (0, keep)):
        part = turned[2 * b * cols : (2 * b + 2) * cols]
        out[...] = jnp.dot(part, tall, preferred_element_type=F32).astype(BF16).reshape(out.shape)


def first_terms(place, activations, other, cot_mine, cot_other, rows):
    tokens, columns = cot_mine.shape
    part, cols = rows // 2, columns // 4
    mine = pl.BlockSpec((tokens, part), lambda r, s: (0, 2 * (2 * (s[0] ^ 3) + s[1]) + r))
    piece = pl.BlockSpec((2, cols, part), lambda r, s: (0, 0, r))

    held = pl.BlockSpec((tokens, columns), lambda r, s: (0, 0), pipeline_mode=ONCE)

    def whole(*shape):
        return pl.BlockSpec(shape, lambda r, s: (0, 0))

    return pl.pallas_call(
        first_term_kernel,
        grid_spec=pltpu.PrefetchScalarGridSpec(
            num_scalar_prefetch=1,
            grid=(2,),
            in_specs=[mine, mine, held, held],
            out_specs=[piece, piece, whole(2 * tokens, columns), whole(columns, 2 * tokens)],
        ),
        out_shape=[jax.ShapeDtypeStruct((2, cols, rows), BF16)] * 2
        + [
            jax.ShapeDtypeStruct((2 * tokens, columns), BF16),
            jax.ShapeDtypeStruct((columns, 2 * tokens), BF16),
        ],
        compiler_params=pltpu.CompilerParams(vmem_limit_bytes=22 * MIB),
        cost_estimate=cost(4 * tokens * rows * columns, 4 * tokens * rows + 4 * rows * columns),
        name="terms",
    )(place, activations, other, cot_mine, cot_other)


def term_kernel(place, mine, other, turned, *outs):
    rows = turned.shape[0] // 2
    for i in range(3):

        @pl.when(pl.program_id(0) == i)
        def _():
            tall = jnp.concatenate([mine[...], other[...]], 0)
            for b in (1, 0):
                out = outs[3 * b + i]
                part = turned[b * rows : (b + 1) * rows]
                out[...] = (
                    jnp.dot(part, tall, preferred_element_type=F32).astype(BF16).reshape(out.shape)
                )


def terms(place, activations, other, turned, rows):
    columns, tokens = turned.shape[0], activations.shape[0]
    part, cols = rows // 2, columns // 4
    mine = pl.BlockSpec((tokens, part), lambda i, r, s: (0, 2 * (2 * (s[0] ^ (2 - i)) + s[1]) + r))
    pieces = [
        pl.BlockSpec((2, cols, part), lambda i, r, s, n=n: (0, 0, jnp.clip(2 * (i - n) + r, 0, 1)))
        for n in range(3)
    ]
    return pl.pallas_call(
        term_kernel,
        grid_spec=pltpu.PrefetchScalarGridSpec(
            num_scalar_prefetch=1,
            grid=(3, 2),
            in_specs=[
                mine,
                mine,
                pl.BlockSpec(turned.shape, lambda i, r, s: (0, 0), pipeline_mode=ONCE),
            ],
            out_specs=pieces * 2,
        ),
        out_shape=[jax.ShapeDtypeStruct((2, cols, rows), BF16)] * 6,
        compiler_params=pltpu.CompilerParams(vmem_limit_bytes=18 * MIB),
        cost_estimate=cost(12 * tokens * rows * columns, 12 * tokens * rows + 12 * rows * columns),
        name="terms",
    )(place, activations, other, turned)


def project_kernel(place, acts, other, cots, here, there, *refs, first, last):
    near, far, *keys = refs[0 if first else 2 : -1]
    acc = refs[-1]
    tokens, cols = acts.shape[0], here.shape[2]
    step = pl.program_id(0)

    weight = jnp.concatenate([here[0], here[1], there[0], there[1]], 1)
    total = lax.dot_general(
        cots[...], weight, (((1,), (1,)), ((), ())), preferred_element_type=F32
    ).astype(BF16)
    near[...] = total[:tokens]
    far[...] = total[tokens:]
    tall = jnp.concatenate([acts[...], other[...]], 0)
    sums = jnp.dot(tall, weight, preferred_element_type=F32)

    @pl.when(step == 0)
    def _():
        acc[...] = sums if first else refs[0][...] + sums

    @pl.when(step == 1)
    def _():
        if last:
            for b in (0, 1):
                for a in (0, 1):
                    at = pl.ds(pl.multiple_of(column_block(place, a, b) * cols, cols), cols)
                    to = slice((2 * b + a) * cols, (2 * b + a + 1) * cols)
                    keys[0][:, at] = acc[:tokens, to] + sums[:tokens, to]
                    keys[1][:, at] = acc[tokens:, to] + sums[tokens:, to]
        else:
            keys[0][...] = acc[...] + sums


def projected(place, k, activations, other, cots, here, there, so_far=None):
    tokens, columns = activations.shape[0], cots.shape[1]
    _, rows, cols = here.shape
    part = rows // 2
    first, last = k == 0, k == 3

    def whole(*shape):
        return pl.BlockSpec(shape, lambda r, s: (0, 0))

    held = pl.BlockSpec((2 * tokens, columns), lambda r, s: (0, 0), pipeline_mode=ONCE)

    mine = pl.BlockSpec(
        (tokens, part), lambda r, s: (0, 2 * (2 * (s[0] ^ k) + s[1]) + r)
    )
    piece = pl.BlockSpec((2, part, cols), lambda r, s: (0, r, 0))
    one = jax.ShapeDtypeStruct((tokens, columns), F32)
    return pl.pallas_call(
        lambda *refs: project_kernel(*refs, first=first, last=last),
        grid_spec=pltpu.PrefetchScalarGridSpec(
            num_scalar_prefetch=1,
            grid=(2,),
            in_specs=[mine, mine, held, piece, piece]
            + ([] if first else [held, pl.BlockSpec(memory_space=pl.ANY)]),
            out_specs=[mine, pl.BlockSpec((tokens, part), lambda r, s: (0, r))]
            + ([whole(tokens, columns)] * 2 if last else [whole(2 * tokens, columns)]),
            scratch_shapes=[pltpu.VMEM((2 * tokens, columns), F32)],
        ),
        out_shape=[
            jax.ShapeDtypeStruct(activations.shape, BF16),
            jax.ShapeDtypeStruct((tokens, rows), BF16),
        ]
        + ([one, one] if last else [jax.ShapeDtypeStruct((2 * tokens, columns), F32)]),
        input_output_aliases={} if first else {7: 0},
        compiler_params=pltpu.CompilerParams(vmem_limit_bytes=28 * MIB),
        cost_estimate=cost(
            8 * tokens * rows * columns,
            8 * tokens * rows + 2 * rows * columns + 8 * tokens * columns,
        ),
        name="project",
    )(
        place, activations, other, cots, here, there,
        *([] if first else [so_far[2], so_far[0]]),
    )


def lay_kernel(place, *refs):
    for k in range(3):

        @pl.when(pl.program_id(0) == k)
        def _():
            refs[-1][...] = refs[k][...]


def laid(place, whole, parts):
    tokens, rows = parts[0].shape
    return pl.pallas_call(
        lay_kernel,
        grid_spec=pltpu.PrefetchScalarGridSpec(
            num_scalar_prefetch=1,
            grid=(3,),
            in_specs=[pl.BlockSpec((tokens, rows), lambda i, s: (0, 0), pipeline_mode=ONCE)] * 3
            + [pl.BlockSpec(memory_space=pl.ANY)],
            out_specs=pl.BlockSpec((tokens, rows), lambda i, s: (0, 2 * (s[0] ^ i) + 1 - s[1])),
        ),
        out_shape=jax.ShapeDtypeStruct(whole.shape, BF16),
        input_output_aliases={4: 0},
        compiler_params=pltpu.CompilerParams(vmem_limit_bytes=8 * MIB),
        cost_estimate=cost(0, 12 * tokens * rows),
        name="lay",
    )(place, *parts, whole)


def finish_kernel(place, got, near, far, last, arrived, whole, out, keys, weight, *, scale):
    out[...] = got[...]
    keys[...] = (near[...] + far[...]).astype(BF16)
    weight[...] = ((last[...] + arrived[...].astype(F32)) * scale).T.astype(BF16)


def finished(place, whole, got, keys_near, keys_far, last, arrived, scale):
    tokens, rows = got.shape
    cols, columns = last.shape[0], keys_near.shape[1]
    part, some = rows // 2, columns // 2
    wide = pl.BlockSpec((tokens, some), lambda r, s: (0, r))
    flat = pl.BlockSpec((cols, part), lambda r, s: (0, r))
    return pl.pallas_call(
        lambda *refs: finish_kernel(*refs, scale=scale),
        grid_spec=pltpu.PrefetchScalarGridSpec(
            num_scalar_prefetch=1,
            grid=(2,),
            in_specs=[
                pl.BlockSpec((tokens, part), lambda r, s: (0, r)),
                wide,
                wide,
                flat,
                flat,
                pl.BlockSpec(memory_space=pl.ANY),
            ],
            out_specs=[
                pl.BlockSpec((tokens, part), lambda r, s: (0, 2 * (2 * (s[0] ^ 3) + 1 - s[1]) + r)),
                wide,
                pl.BlockSpec((part, cols), lambda r, s: (r, 0)),
            ],
        ),
        out_shape=[
            jax.ShapeDtypeStruct(whole.shape, BF16),
            jax.ShapeDtypeStruct((tokens, columns), BF16),
            jax.ShapeDtypeStruct((rows, cols), BF16),
        ],
        input_output_aliases={6: 0},
        compiler_params=pltpu.CompilerParams(vmem_limit_bytes=12 * MIB),
        cost_estimate=cost(0, 4 * tokens * rows + 10 * tokens * columns),
        name="finish",
    )(place, got, keys_near, keys_far, last, arrived, whole)


def added(*arrays):
    total = arrays[0].astype(F32)
    for array in arrays[1:]:
        total = total + array.astype(F32)
    return total.astype(BF16)


def by_hops(activations, cotangent, kv_weight):
    rows = kv_weight.shape[0]
    tokens = activations.shape[0]
    place = jnp.stack([lax.axis_index(name) for name in ("chip", "core", "blk")]).astype(jnp.int32)

    other, cot_other = sent(activations, SWAP), sent(cotangent, SWAP)
    base = jnp.stack([kv_weight, sent(kv_weight, FLIP_A)])
    one, mid = sent(base, PAIR), sent(base, MID)
    base_b = sent(base, FLIP_B)

    keep3, send3, cots, turned = first_terms(
        place, activations, other, cotangent, cot_other, rows
    )
    got3 = sent(send3, FLIP_B)
    keep2, keep1, keep0, send2, send1, send0 = terms(place, activations, other, turned, rows)
    first = gate(place, after(one, keep0), mid, base_b)

    sum3 = added(after(keep3, first), got3)
    far = sent(sum3, IN)
    two_mid = sent(after(one, first, sum3), MID)
    two_end = sent(after(mid, sum3), OUT)
    got2 = sent(after(send2, sum3), FLIP_B)
    one_b = sent(after(one, sum3), FLIP_B)
    whole, out0, keys = projected(
        first, 0, after(activations, keep0, sum3), other, cots, base, base_b
    )

    sum2_far = added(after(far, two_mid, two_end, one_b, out0), keep2, got2)
    mid_far = sent(sum2_far, MID)
    near = sent(after(added(keep2, got2), sum2_far), IN)
    three_end = sent(after(two_mid, sum2_far), OUT)
    got1 = sent(after(send1, sum2_far), FLIP_B)
    two = after(two_mid, sum2_far) + two_end
    two_b = sent(two, FLIP_B)
    whole, out1, keys = projected(
        place, 1, after(activations, sum2_far), other, cots, one, one_b, (whole, None, keys)
    )

    sum3_near = added(sum3, near)
    sum_mid = sent(sum3_near, MID)
    part1 = added(after(keep1, sum3_near), mid_far)
    sum1 = added(after(part1, three_end, two_b, out1), got1)
    sum_one = sent(sum1, PAIR)
    three = after(mid, sum1) + three_end
    three_b = sent(three, FLIP_B)
    whole, out2, keys = projected(
        place, 2, after(activations, sum1), other, cots, two, two_b, (whole, None, keys)
    )
    got0 = sent(after(send0, three_b, out2), FLIP_B)
    part0 = [keep0[a].astype(F32) + sum_mid[a].astype(F32) for a in (0, 1)]
    whole, out3, keys, keys_far = projected(
        place, 3, after(activations, out2, *part0), other, cots, three, three_b, (whole, None, keys)
    )
    sum_one = after(sum_one, out3)
    last = [part0[a] + got0[a].astype(F32) + sum_one[a].astype(F32) for a in (0, 1)]
    over = last[1].astype(BF16)
    whole = laid(
        place,
        whole,
        (sent(out0, SWAP), sent(out1, SWAP), sent(out2, SWAP)),
    )
    grad_input, key_values, grad_weight = finished(
        place,
        whole,
        sent(out3, SWAP),
        keys,
        sent(keys_far, SWAP),
        last[0],
        sent(over, FLIP_A),
        1.0 / math.sqrt(32 * tokens),
    )
    return (key_values, grad_input, grad_weight)


def swapped(array):
    return lax.ppermute(array, "core", [(0, 1), (1, 0)])


def by_collectives(activations, cotangent, kv_weight):
    blocks, chips = lax.axis_size("blk"), lax.axis_size("chip")
    core = lax.axis_index("core")
    tokens, features = activations.shape
    rows, cols = kv_weight.shape
    columns = cotangent.shape[1]
    by_core = activations.reshape(tokens, chips, 2, rows)
    mine = lax.dynamic_index_in_dim(by_core, core, 2, keepdims=False)
    other = lax.dynamic_index_in_dim(by_core, 1 - core, 2, keepdims=False)
    acts = jnp.concatenate([mine, swapped(other)], 0)
    cots = jnp.concatenate([cotangent, swapped(cotangent)], 0)
    weight = lax.all_gather(kv_weight, ("blk", "chip"), axis=0, tiled=False)
    weight = weight.reshape(blocks, chips, rows, cols)
    parts = jnp.einsum(
        "tzr,tbc->bzrc", acts, cots.reshape(2 * tokens, blocks, cols), preferred_element_type=F32
    ).astype(BF16).reshape(blocks * chips, rows, cols)
    total = lax.psum_scatter(parts, ("blk", "chip"), scatter_dimension=0, tiled=False)
    count = tokens * blocks * chips * 2
    grad_weight = (total.astype(F32) * (1.0 / math.sqrt(count))).astype(BF16)
    full = weight.transpose(1, 2, 0, 3).reshape(chips * rows, columns)
    keys = jnp.dot(acts.reshape(2 * tokens, chips * rows), full, preferred_element_type=F32)
    key_values = (keys[:tokens] + swapped(keys[tokens:])).astype(BF16)
    inputs = lax.dot_general(
        cots, full, (((1,), (1,)), ((), ())), preferred_element_type=F32
    ).astype(BF16).reshape(2 * tokens, chips, rows)
    near, far = inputs[:tokens], swapped(inputs[tokens:])
    low = jnp.where(core == 0, near, far)
    high = jnp.where(core == 0, far, near)
    grad_input = jnp.stack([low, high], 2).reshape(tokens, features)
    return (key_values, grad_input, grad_weight)


def solution(mesh):
    blocks, shards = mesh.shape["blk"], mesh.shape["shard"]
    split = Mesh(mesh.devices.reshape(blocks, shards // 2, 2), AXES)
    by_token = P(AXES, None)
    by_piece = P(("chip", "core"), "blk")
    return jax.shard_map(
        by_hops if (blocks, shards) == (4, 8) else by_collectives,
        mesh=split,
        in_specs=(by_token, by_token, by_piece),
        out_specs=(by_token, by_token, by_piece),
        check_vma=False,
    )
```

```python
import math

import jax
import jax.numpy as jnp
from jax import lax
from jax.experimental import pallas as pl
from jax.experimental.pallas import tpu as pltpu
from jax.sharding import Mesh, PartitionSpec as P

F32, BF16 = jnp.float32, jnp.bfloat16
AXES = ("blk", "chip", "core")
SHRINK = 1000
MIB = 2**20
GATE = 10**7
ONCE = pl.Buffered(1)


def hops(move):
    pairs = []
    for blk in range(4):
        for z in range(4):
            for core in range(2):
                to = move(blk, z, core)
                if to is not None:
                    pairs.append(((blk * 4 + z) * 2 + core, (to[0] * 4 + to[1]) * 2 + to[2]))
    return pairs


def middle(z):
    return z in (1, 2)


SWAP = hops(lambda b, z, c: (b, z, 1 - c))
FLIP_A = hops(lambda b, z, c: (b ^ (1 + c), z, c))
FLIP_B = hops(lambda b, z, c: (b ^ (2 - c), z, c))
PAIR = hops(lambda b, z, c: (b, z ^ 1, c))
MID = hops(lambda b, z, c: (b, z ^ 3, c) if middle(z) else None)
OUT = hops(lambda b, z, c: (b, z ^ 1, c) if middle(z) else None)
IN = hops(lambda b, z, c: (b, z ^ 1, c) if not middle(z) else None)


def after(array, *others):
    return lax.optimization_barrier((array, *others))[0]


def sent(array, pairs):
    return lax.ppermute(array, AXES, pairs)


def column_block(place, a, b):
    core = place[1]
    return place[2] ^ (a * (1 + core)) ^ (b * (2 - core))


def cost(flops, moved, shrink=SHRINK):
    return pl.CostEstimate(flops=flops // shrink, bytes_accessed=moved // shrink, transcendentals=0)


def gate(place, *arrays):
    def kernel(*refs):
        for i in range(3):
            refs[-1][i] = refs[0][i]

    return pl.pallas_call(
        kernel,
        in_specs=[pl.BlockSpec(memory_space=pltpu.SMEM)]
        + [pl.BlockSpec(memory_space=pl.ANY)] * len(arrays),
        out_specs=pl.BlockSpec(memory_space=pltpu.SMEM),
        out_shape=jax.ShapeDtypeStruct(place.shape, place.dtype),
        compiler_params=pltpu.CompilerParams(vmem_limit_bytes=MIB),
        cost_estimate=cost(0, GATE, 1),
        name="gate",
    )(place, *arrays)


def first_term_kernel(place, mine, other, cot_mine, cot_other, keep, send, cots, turned):
    tokens, cols = cot_mine.shape[0], cot_mine.shape[1] // 4

    @pl.when(pl.program_id(0) == 0)
    def _():
        for b in (0, 1):
            for a in (0, 1):
                at = pl.ds(pl.multiple_of(column_block(place, a, b) * cols, cols), cols)
                to = slice((2 * b + a) * cols, (2 * b + a + 1) * cols)
                for array, half in ((cot_mine, slice(0, tokens)), (cot_other, slice(tokens, None))):
                    piece = array[:, at]
                    cots[half, to] = piece
                    turned[to, half] = piece.T

    tall = jnp.concatenate([mine[...], other[...]], 0)
    for b, out in ((1, send), (0, keep)):
        part = turned[2 * b * cols : (2 * b + 2) * cols]
        out[...] = jnp.dot(part, tall, preferred_element_type=F32).astype(BF16).reshape(out.shape)


def first_terms(place, activations, other, cot_mine, cot_other, rows):
    tokens, columns = cot_mine.shape
    part, cols = rows // 2, columns // 4
    mine = pl.BlockSpec((tokens, part), lambda r, s: (0, 2 * (2 * (s[0] ^ 3) + s[1]) + r))
    piece = pl.BlockSpec((2, cols, part), lambda r, s: (0, 0, r))

    held = pl.BlockSpec((tokens, columns), lambda r, s: (0, 0), pipeline_mode=ONCE)

    def whole(*shape):
        return pl.BlockSpec(shape, lambda r, s: (0, 0))

    return pl.pallas_call(
        first_term_kernel,
        grid_spec=pltpu.PrefetchScalarGridSpec(
            num_scalar_prefetch=1,
            grid=(2,),
            in_specs=[mine, mine, held, held],
            out_specs=[piece, piece, whole(2 * tokens, columns), whole(columns, 2 * tokens)],
        ),
        out_shape=[jax.ShapeDtypeStruct((2, cols, rows), BF16)] * 2
        + [
            jax.ShapeDtypeStruct((2 * tokens, columns), BF16),
            jax.ShapeDtypeStruct((columns, 2 * tokens), BF16),
        ],
        compiler_params=pltpu.CompilerParams(vmem_limit_bytes=22 * MIB),
        cost_estimate=cost(4 * tokens * rows * columns, 4 * tokens * rows + 4 * rows * columns),
        name="terms",
    )(place, activations, other, cot_mine, cot_other)


def term_kernel(place, mine, other, turned, *outs):
    rows = turned.shape[0] // 2
    for i in range(3):

        @pl.when(pl.program_id(0) == i)
        def _():
            tall = jnp.concatenate([mine[...], other[...]], 0)
            for b in (1, 0):
                out = outs[3 * b + i]
                part = turned[b * rows : (b + 1) * rows]
                out[...] = (
                    jnp.dot(part, tall, preferred_element_type=F32).astype(BF16).reshape(out.shape)
                )


def terms(place, activations, other, turned, rows):
    columns, tokens = turned.shape[0], activations.shape[0]
    part, cols = rows // 2, columns // 4
    mine = pl.BlockSpec((tokens, part), lambda i, r, s: (0, 2 * (2 * (s[0] ^ (2 - i)) + s[1]) + r))
    pieces = [
        pl.BlockSpec((2, cols, part), lambda i, r, s, n=n: (0, 0, jnp.clip(2 * (i - n) + r, 0, 1)))
        for n in range(3)
    ]
    return pl.pallas_call(
        term_kernel,
        grid_spec=pltpu.PrefetchScalarGridSpec(
            num_scalar_prefetch=1,
            grid=(3, 2),
            in_specs=[
                mine,
                mine,
                pl.BlockSpec(turned.shape, lambda i, r, s: (0, 0), pipeline_mode=ONCE),
            ],
            out_specs=pieces * 2,
        ),
        out_shape=[jax.ShapeDtypeStruct((2, cols, rows), BF16)] * 6,
        compiler_params=pltpu.CompilerParams(vmem_limit_bytes=18 * MIB),
        cost_estimate=cost(12 * tokens * rows * columns, 12 * tokens * rows + 12 * rows * columns),
        name="terms",
    )(place, activations, other, turned)


def project_kernel(place, acts, other, cots, here, there, *refs, first, last):
    near, far, *keys = refs[0 if first else 2 : -1]
    acc = refs[-1]
    tokens, cols = acts.shape[0], here.shape[2]
    step = pl.program_id(0)

    weight = jnp.concatenate([here[0], here[1], there[0], there[1]], 1)
    total = lax.dot_general(
        cots[...], weight, (((1,), (1,)), ((), ())), preferred_element_type=F32
    ).astype(BF16)
    near[...] = total[:tokens]
    far[...] = total[tokens:]
    tall = jnp.concatenate([acts[...], other[...]], 0)
    sums = jnp.dot(tall, weight, preferred_element_type=F32)

    @pl.when(step == 0)
    def _():
        acc[...] = sums if first else refs[0][...] + sums

    @pl.when(step == 1)
    def _():
        if last:
            for b in (0, 1):
                for a in (0, 1):
                    at = pl.ds(pl.multiple_of(column_block(place, a, b) * cols, cols), cols)
                    to = slice((2 * b + a) * cols, (2 * b + a + 1) * cols)
                    keys[0][:, at] = acc[:tokens, to] + sums[:tokens, to]
                    keys[1][:, at] = acc[tokens:, to] + sums[tokens:, to]
        else:
            keys[0][...] = acc[...] + sums


def projected(place, k, activations, other, cots, here, there, so_far=None):
    tokens, columns = activations.shape[0], cots.shape[1]
    _, rows, cols = here.shape
    part = rows // 2
    first, last = k == 0, k == 3

    def whole(*shape):
        return pl.BlockSpec(shape, lambda r, s: (0, 0))

    held = pl.BlockSpec((2 * tokens, columns), lambda r, s: (0, 0), pipeline_mode=ONCE)

    mine = pl.BlockSpec(
        (tokens, part), lambda r, s: (0, 2 * (2 * (s[0] ^ k) + s[1]) + r)
    )
    piece = pl.BlockSpec((2, part, cols), lambda r, s: (0, r, 0))
    one = jax.ShapeDtypeStruct((tokens, columns), F32)
    return pl.pallas_call(
        lambda *refs: project_kernel(*refs, first=first, last=last),
        grid_spec=pltpu.PrefetchScalarGridSpec(
            num_scalar_prefetch=1,
            grid=(2,),
            in_specs=[mine, mine, held, piece, piece]
            + ([] if first else [held, pl.BlockSpec(memory_space=pl.ANY)]),
            out_specs=[mine, pl.BlockSpec((tokens, part), lambda r, s: (0, r))]
            + ([whole(tokens, columns)] * 2 if last else [whole(2 * tokens, columns)]),
            scratch_shapes=[pltpu.VMEM((2 * tokens, columns), F32)],
        ),
        out_shape=[
            jax.ShapeDtypeStruct(activations.shape, BF16),
            jax.ShapeDtypeStruct((tokens, rows), BF16),
        ]
        + ([one, one] if last else [jax.ShapeDtypeStruct((2 * tokens, columns), F32)]),
        input_output_aliases={} if first else {7: 0},
        compiler_params=pltpu.CompilerParams(vmem_limit_bytes=28 * MIB),
        cost_estimate=cost(
            8 * tokens * rows * columns,
            8 * tokens * rows + 2 * rows * columns + 8 * tokens * columns,
        ),
        name="project",
    )(
        place, activations, other, cots, here, there,
        *([] if first else [so_far[2], so_far[0]]),
    )


def lay_kernel(place, *refs):
    for k in range(3):

        @pl.when(pl.program_id(0) == k)
        def _():
            refs[-1][...] = refs[k][...]


def laid(place, whole, parts):
    tokens, rows = parts[0].shape
    return pl.pallas_call(
        lay_kernel,
        grid_spec=pltpu.PrefetchScalarGridSpec(
            num_scalar_prefetch=1,
            grid=(3,),
            in_specs=[pl.BlockSpec((tokens, rows), lambda i, s: (0, 0), pipeline_mode=ONCE)] * 3
            + [pl.BlockSpec(memory_space=pl.ANY)],
            out_specs=pl.BlockSpec((tokens, rows), lambda i, s: (0, 2 * (s[0] ^ i) + 1 - s[1])),
        ),
        out_shape=jax.ShapeDtypeStruct(whole.shape, BF16),
        input_output_aliases={4: 0},
        compiler_params=pltpu.CompilerParams(vmem_limit_bytes=8 * MIB),
        cost_estimate=cost(0, 12 * tokens * rows),
        name="lay",
    )(place, *parts, whole)


def finish_kernel(place, got, near, far, last, arrived, whole, out, keys, weight, *, scale):
    out[...] = got[...]
    keys[...] = (near[...] + far[...]).astype(BF16)
    weight[...] = ((last[...] + arrived[...].astype(F32)) * scale).T.astype(BF16)


def finished(place, whole, got, keys_near, keys_far, last, arrived, scale):
    tokens, rows = got.shape
    cols, columns = last.shape[0], keys_near.shape[1]
    part, some = rows // 2, columns // 2
    wide = pl.BlockSpec((tokens, some), lambda r, s: (0, r))
    flat = pl.BlockSpec((cols, part), lambda r, s: (0, r))
    return pl.pallas_call(
        lambda *refs: finish_kernel(*refs, scale=scale),
        grid_spec=pltpu.PrefetchScalarGridSpec(
            num_scalar_prefetch=1,
            grid=(2,),
            in_specs=[
                pl.BlockSpec((tokens, part), lambda r, s: (0, r)),
                wide,
                wide,
                flat,
                flat,
                pl.BlockSpec(memory_space=pl.ANY),
            ],
            out_specs=[
                pl.BlockSpec((tokens, part), lambda r, s: (0, 2 * (2 * (s[0] ^ 3) + 1 - s[1]) + r)),
                wide,
                pl.BlockSpec((part, cols), lambda r, s: (r, 0)),
            ],
        ),
        out_shape=[
            jax.ShapeDtypeStruct(whole.shape, BF16),
            jax.ShapeDtypeStruct((tokens, columns), BF16),
            jax.ShapeDtypeStruct((rows, cols), BF16),
        ],
        input_output_aliases={6: 0},
        compiler_params=pltpu.CompilerParams(vmem_limit_bytes=12 * MIB),
        cost_estimate=cost(0, 4 * tokens * rows + 10 * tokens * columns),
        name="finish",
    )(place, got, keys_near, keys_far, last, arrived, whole)


def added(*arrays):
    total = arrays[0].astype(F32)
    for array in arrays[1:]:
        total = total + array.astype(F32)
    return total.astype(BF16)


def by_hops(activations, cotangent, kv_weight):
    rows = kv_weight.shape[0]
    tokens = activations.shape[0]
    place = jnp.stack([lax.axis_index(name) for name in ("chip", "core", "blk")]).astype(jnp.int32)

    other, cot_other = sent(activations, SWAP), sent(cotangent, SWAP)
    base = jnp.stack([kv_weight, sent(kv_weight, FLIP_A)])
    one, mid = sent(base, PAIR), sent(base, MID)
    base_b = sent(base, FLIP_B)

    keep3, send3, cots, turned = first_terms(
        place, activations, other, cotangent, cot_other, rows
    )
    got3 = sent(send3, FLIP_B)
    keep2, keep1, keep0, send2, send1, send0 = terms(place, activations, other, turned, rows)
    first = gate(place, after(one, keep0), mid, base_b)

    sum3 = added(after(keep3, first), got3)
    far = sent(sum3, IN)
    two_mid = sent(after(one, first, sum3), MID)
    two_end = sent(after(mid, sum3), OUT)
    got2 = sent(send2, FLIP_B)
    sum2 = added(keep2, got2)
    one_b = sent(after(one, sum3), FLIP_B)
    got1 = sent(after(send1, sum2), FLIP_B)
    whole, out0, keys = projected(
        first, 0, after(activations, keep0, sum3, sum2), other, cots, base, base_b
    )

    sum2_far = added(after(sum2, out0), far)
    mid_far = sent(sum2_far, MID)
    near = sent(after(sum2, sum2_far, two_mid, two_end, one_b), IN)
    three_end = sent(after(two_mid, sum2_far), OUT)
    two = after(two_mid, sum2_far) + two_end
    two_b = sent(two, FLIP_B)
    sum1 = added(keep1, got1)
    got0 = sent(after(send0, sum1), FLIP_B)
    whole, out1, keys = projected(
        place, 1, after(activations, sum2_far, sum1), other, cots, one, one_b, (whole, None, keys)
    )

    sum3_near = added(sum3, near)
    sum_mid = sent(sum3_near, MID)
    sum1_far = added(after(sum1, sum3_near, out1), mid_far)
    sum_one = sent(after(sum1_far, three_end, two_b), PAIR)
    three = after(mid, sum1_far) + three_end
    three_b = sent(three, FLIP_B)
    sum0 = added(keep0, got0)
    whole, out2, keys = projected(
        place,
        2,
        after(activations, sum1_far, sum0),
        other,
        cots,
        two,
        two_b,
        (whole, None, keys),
    )
    whole, out3, keys, keys_far = projected(
        place, 3, after(activations, out2), other, cots, three, three_b, (whole, None, keys)
    )
    sum_one = after(sum_one, out3)
    last = [
        sum0[a].astype(F32) + sum_mid[a].astype(F32) + sum_one[a].astype(F32) for a in (0, 1)
    ]
    over = last[1].astype(BF16)
    whole = laid(
        place,
        whole,
        (sent(out0, SWAP), sent(out1, SWAP), sent(out2, SWAP)),
    )
    grad_input, key_values, grad_weight = finished(
        place,
        whole,
        sent(out3, SWAP),
        keys,
        sent(keys_far, SWAP),
        last[0],
        sent(over, FLIP_A),
        1.0 / math.sqrt(32 * tokens),
    )
    return (key_values, grad_input, grad_weight)


def swapped(array):
    return lax.ppermute(array, "core", [(0, 1), (1, 0)])


def by_collectives(activations, cotangent, kv_weight):
    blocks, chips = lax.axis_size("blk"), lax.axis_size("chip")
    core = lax.axis_index("core")
    tokens, features = activations.shape
    rows, cols = kv_weight.shape
    columns = cotangent.shape[1]
    by_core = activations.reshape(tokens, chips, 2, rows)
    mine = lax.dynamic_index_in_dim(by_core, core, 2, keepdims=False)
    other = lax.dynamic_index_in_dim(by_core, 1 - core, 2, keepdims=False)
    acts = jnp.concatenate([mine, swapped(other)], 0)
    cots = jnp.concatenate([cotangent, swapped(cotangent)], 0)
    weight = lax.all_gather(kv_weight, ("blk", "chip"), axis=0, tiled=False)
    weight = weight.reshape(blocks, chips, rows, cols)
    parts = jnp.einsum(
        "tzr,tbc->bzrc", acts, cots.reshape(2 * tokens, blocks, cols), preferred_element_type=F32
    ).astype(BF16).reshape(blocks * chips, rows, cols)
    total = lax.psum_scatter(parts, ("blk", "chip"), scatter_dimension=0, tiled=False)
    count = tokens * blocks * chips * 2
    grad_weight = (total.astype(F32) * (1.0 / math.sqrt(count))).astype(BF16)
    full = weight.transpose(1, 2, 0, 3).reshape(chips * rows, columns)
    keys = jnp.dot(acts.reshape(2 * tokens, chips * rows), full, preferred_element_type=F32)
    key_values = (keys[:tokens] + swapped(keys[tokens:])).astype(BF16)
    inputs = lax.dot_general(
        cots, full, (((1,), (1,)), ((), ())), preferred_element_type=F32
    ).astype(BF16).reshape(2 * tokens, chips, rows)
    near, far = inputs[:tokens], swapped(inputs[tokens:])
    low = jnp.where(core == 0, near, far)
    high = jnp.where(core == 0, far, near)
    grad_input = jnp.stack([low, high], 2).reshape(tokens, features)
    return (key_values, grad_input, grad_weight)


def solution(mesh):
    blocks, shards = mesh.shape["blk"], mesh.shape["shard"]
    split = Mesh(mesh.devices.reshape(blocks, shards // 2, 2), AXES)
    by_token = P(AXES, None)
    by_piece = P(("chip", "core"), "blk")
    return jax.shard_map(
        by_hops if (blocks, shards) == (4, 8) else by_collectives,
        mesh=split,
        in_specs=(by_token, by_token, by_piece),
        out_specs=(by_token, by_token, by_piece),
        check_vma=False,
    )
```

```python
import math

import jax
import jax.numpy as jnp
from jax import lax
from jax.experimental import pallas as pl
from jax.experimental.pallas import tpu as pltpu
from jax.sharding import Mesh, PartitionSpec as P

F32, BF16 = jnp.float32, jnp.bfloat16
AXES = ("blk", "chip", "core")
SHRINK = 1000
MIB = 2**20
GATE = 10**7
ONCE = pl.Buffered(1)


def hops(move):
    pairs = []
    for blk in range(4):
        for z in range(4):
            for core in range(2):
                to = move(blk, z, core)
                if to is not None:
                    pairs.append(((blk * 4 + z) * 2 + core, (to[0] * 4 + to[1]) * 2 + to[2]))
    return pairs


def middle(z):
    return z in (1, 2)


SWAP = hops(lambda b, z, c: (b, z, 1 - c))
FLIP_A = hops(lambda b, z, c: (b ^ (1 + c), z, c))
FLIP_B = hops(lambda b, z, c: (b ^ (2 - c), z, c))
PAIR = hops(lambda b, z, c: (b, z ^ 1, c))
MID = hops(lambda b, z, c: (b, z ^ 3, c) if middle(z) else None)
OUT = hops(lambda b, z, c: (b, z ^ 1, c) if middle(z) else None)
IN = hops(lambda b, z, c: (b, z ^ 1, c) if not middle(z) else None)


def after(array, *others):
    return lax.optimization_barrier((array, *others))[0]


def sent(array, pairs):
    return lax.ppermute(array, AXES, pairs)


def column_block(place, a, b):
    core = place[1]
    return place[2] ^ (a * (1 + core)) ^ (b * (2 - core))


def cost(flops, moved, shrink=SHRINK):
    return pl.CostEstimate(flops=flops // shrink, bytes_accessed=moved // shrink, transcendentals=0)


def gate(place, *arrays):
    def kernel(*refs):
        for i in range(3):
            refs[-1][i] = refs[0][i]

    return pl.pallas_call(
        kernel,
        in_specs=[pl.BlockSpec(memory_space=pltpu.SMEM)]
        + [pl.BlockSpec(memory_space=pl.ANY)] * len(arrays),
        out_specs=pl.BlockSpec(memory_space=pltpu.SMEM),
        out_shape=jax.ShapeDtypeStruct(place.shape, place.dtype),
        compiler_params=pltpu.CompilerParams(vmem_limit_bytes=MIB),
        cost_estimate=cost(0, GATE, 1),
        name="gate",
    )(place, *arrays)


def first_term_kernel(place, mine, other, cot_mine, cot_other, keep, send, cots, turned):
    tokens, cols = cot_mine.shape[0], cot_mine.shape[1] // 4

    @pl.when(pl.program_id(0) == 0)
    def _():
        for b in (0, 1):
            for a in (0, 1):
                at = pl.ds(pl.multiple_of(column_block(place, a, b) * cols, cols), cols)
                to = slice((2 * b + a) * cols, (2 * b + a + 1) * cols)
                for array, half in ((cot_mine, slice(0, tokens)), (cot_other, slice(tokens, None))):
                    piece = array[:, at]
                    cots[half, to] = piece
                    turned[to, half] = piece.T

    tall = jnp.concatenate([mine[...], other[...]], 0)
    for b, out in ((1, send), (0, keep)):
        part = turned[2 * b * cols : (2 * b + 2) * cols]
        out[...] = jnp.dot(part, tall, preferred_element_type=F32).astype(BF16).reshape(out.shape)


def first_terms(place, activations, other, cot_mine, cot_other, rows):
    tokens, columns = cot_mine.shape
    part, cols = rows // 2, columns // 4
    mine = pl.BlockSpec((tokens, part), lambda r, s: (0, 2 * (2 * (s[0] ^ 3) + s[1]) + r))
    piece = pl.BlockSpec((2, cols, part), lambda r, s: (0, 0, r))

    held = pl.BlockSpec((tokens, columns), lambda r, s: (0, 0), pipeline_mode=ONCE)

    def whole(*shape):
        return pl.BlockSpec(shape, lambda r, s: (0, 0))

    return pl.pallas_call(
        first_term_kernel,
        grid_spec=pltpu.PrefetchScalarGridSpec(
            num_scalar_prefetch=1,
            grid=(2,),
            in_specs=[mine, mine, held, held],
            out_specs=[piece, piece, whole(2 * tokens, columns), whole(columns, 2 * tokens)],
        ),
        out_shape=[jax.ShapeDtypeStruct((2, cols, rows), BF16)] * 2
        + [
            jax.ShapeDtypeStruct((2 * tokens, columns), BF16),
            jax.ShapeDtypeStruct((columns, 2 * tokens), BF16),
        ],
        compiler_params=pltpu.CompilerParams(vmem_limit_bytes=22 * MIB),
        cost_estimate=cost(4 * tokens * rows * columns, 4 * tokens * rows + 4 * rows * columns),
        name="terms",
    )(place, activations, other, cot_mine, cot_other)


def term_kernel(place, mine, other, turned, *outs):
    rows = turned.shape[0] // 2
    for i in range(3):

        @pl.when(pl.program_id(0) == i)
        def _():
            tall = jnp.concatenate([mine[...], other[...]], 0)
            for b in (1, 0):
                out = outs[3 * b + i]
                part = turned[b * rows : (b + 1) * rows]
                out[...] = (
                    jnp.dot(part, tall, preferred_element_type=F32).astype(BF16).reshape(out.shape)
                )


def terms(place, activations, other, turned, rows):
    columns, tokens = turned.shape[0], activations.shape[0]
    part, cols = rows // 2, columns // 4
    mine = pl.BlockSpec((tokens, part), lambda i, r, s: (0, 2 * (2 * (s[0] ^ (2 - i)) + s[1]) + r))
    pieces = [
        pl.BlockSpec((2, cols, part), lambda i, r, s, n=n: (0, 0, jnp.clip(2 * (i - n) + r, 0, 1)))
        for n in range(3)
    ]
    return pl.pallas_call(
        term_kernel,
        grid_spec=pltpu.PrefetchScalarGridSpec(
            num_scalar_prefetch=1,
            grid=(3, 2),
            in_specs=[
                mine,
                mine,
                pl.BlockSpec(turned.shape, lambda i, r, s: (0, 0), pipeline_mode=ONCE),
            ],
            out_specs=pieces * 2,
        ),
        out_shape=[jax.ShapeDtypeStruct((2, cols, rows), BF16)] * 6,
        compiler_params=pltpu.CompilerParams(vmem_limit_bytes=18 * MIB),
        cost_estimate=cost(12 * tokens * rows * columns, 12 * tokens * rows + 12 * rows * columns),
        name="terms",
    )(place, activations, other, turned)


def project_kernel(place, acts, other, cots, here, there, *refs, first, last):
    near, far, *keys = refs[0 if first else 2 : -1]
    acc = refs[-1]
    tokens, cols = acts.shape[0], here.shape[2]
    step = pl.program_id(0)

    weight = jnp.concatenate([here[0], here[1], there[0], there[1]], 1)
    total = lax.dot_general(
        cots[...], weight, (((1,), (1,)), ((), ())), preferred_element_type=F32
    ).astype(BF16)
    near[...] = total[:tokens]
    far[...] = total[tokens:]
    tall = jnp.concatenate([acts[...], other[...]], 0)
    sums = jnp.dot(tall, weight, preferred_element_type=F32)

    @pl.when(step == 0)
    def _():
        acc[...] = sums if first else refs[0][...] + sums

    @pl.when(step == 1)
    def _():
        if last:
            for b in (0, 1):
                for a in (0, 1):
                    at = pl.ds(pl.multiple_of(column_block(place, a, b) * cols, cols), cols)
                    to = slice((2 * b + a) * cols, (2 * b + a + 1) * cols)
                    keys[0][:, at] = acc[:tokens, to] + sums[:tokens, to]
                    keys[1][:, at] = acc[tokens:, to] + sums[tokens:, to]
        else:
            keys[0][...] = acc[...] + sums


def projected(place, k, activations, other, cots, here, there, so_far=None):
    tokens, columns = activations.shape[0], cots.shape[1]
    _, rows, cols = here.shape
    part = rows // 2
    first, last = k == 0, k == 3

    def whole(*shape):
        return pl.BlockSpec(shape, lambda r, s: (0, 0))

    held = pl.BlockSpec((2 * tokens, columns), lambda r, s: (0, 0), pipeline_mode=ONCE)

    mine = pl.BlockSpec(
        (tokens, part), lambda r, s: (0, 2 * (2 * (s[0] ^ k) + s[1]) + r)
    )
    piece = pl.BlockSpec((2, part, cols), lambda r, s: (0, r, 0))
    one = jax.ShapeDtypeStruct((tokens, columns), F32)
    return pl.pallas_call(
        lambda *refs: project_kernel(*refs, first=first, last=last),
        grid_spec=pltpu.PrefetchScalarGridSpec(
            num_scalar_prefetch=1,
            grid=(2,),
            in_specs=[mine, mine, held, piece, piece]
            + ([] if first else [held, pl.BlockSpec(memory_space=pl.ANY)]),
            out_specs=[mine, pl.BlockSpec((tokens, part), lambda r, s: (0, r))]
            + ([whole(tokens, columns)] * 2 if last else [whole(2 * tokens, columns)]),
            scratch_shapes=[pltpu.VMEM((2 * tokens, columns), F32)],
        ),
        out_shape=[
            jax.ShapeDtypeStruct(activations.shape, BF16),
            jax.ShapeDtypeStruct((tokens, rows), BF16),
        ]
        + ([one, one] if last else [jax.ShapeDtypeStruct((2 * tokens, columns), F32)]),
        input_output_aliases={} if first else {7: 0},
        compiler_params=pltpu.CompilerParams(vmem_limit_bytes=28 * MIB),
        cost_estimate=cost(
            8 * tokens * rows * columns,
            8 * tokens * rows + 2 * rows * columns + 8 * tokens * columns,
        ),
        name="project",
    )(
        place, activations, other, cots, here, there,
        *([] if first else [so_far[2], so_far[0]]),
    )


def lay_kernel(place, *refs):
    for k in range(3):

        @pl.when(pl.program_id(0) == k)
        def _():
            refs[-1][...] = refs[k][...]


def laid(place, whole, parts):
    tokens, rows = parts[0].shape
    return pl.pallas_call(
        lay_kernel,
        grid_spec=pltpu.PrefetchScalarGridSpec(
            num_scalar_prefetch=1,
            grid=(3,),
            in_specs=[pl.BlockSpec((tokens, rows), lambda i, s: (0, 0), pipeline_mode=ONCE)] * 3
            + [pl.BlockSpec(memory_space=pl.ANY)],
            out_specs=pl.BlockSpec((tokens, rows), lambda i, s: (0, 2 * (s[0] ^ i) + 1 - s[1])),
        ),
        out_shape=jax.ShapeDtypeStruct(whole.shape, BF16),
        input_output_aliases={4: 0},
        compiler_params=pltpu.CompilerParams(vmem_limit_bytes=8 * MIB),
        cost_estimate=cost(0, 12 * tokens * rows),
        name="lay",
    )(place, *parts, whole)


def finish_kernel(place, got, near, far, last, arrived, whole, out, keys, weight, *, scale):
    out[...] = got[...]
    keys[...] = (near[...] + far[...]).astype(BF16)
    weight[...] = ((last[...] + arrived[...].astype(F32)) * scale).T.astype(BF16)


def finished(place, whole, got, keys_near, keys_far, last, arrived, scale):
    tokens, rows = got.shape
    cols, columns = last.shape[0], keys_near.shape[1]
    part, some = rows // 2, columns // 2
    wide = pl.BlockSpec((tokens, some), lambda r, s: (0, r))
    flat = pl.BlockSpec((cols, part), lambda r, s: (0, r))
    return pl.pallas_call(
        lambda *refs: finish_kernel(*refs, scale=scale),
        grid_spec=pltpu.PrefetchScalarGridSpec(
            num_scalar_prefetch=1,
            grid=(2,),
            in_specs=[
                pl.BlockSpec((tokens, part), lambda r, s: (0, r)),
                wide,
                wide,
                flat,
                flat,
                pl.BlockSpec(memory_space=pl.ANY),
            ],
            out_specs=[
                pl.BlockSpec((tokens, part), lambda r, s: (0, 2 * (2 * (s[0] ^ 3) + 1 - s[1]) + r)),
                wide,
                pl.BlockSpec((part, cols), lambda r, s: (r, 0)),
            ],
        ),
        out_shape=[
            jax.ShapeDtypeStruct(whole.shape, BF16),
            jax.ShapeDtypeStruct((tokens, columns), BF16),
            jax.ShapeDtypeStruct((rows, cols), BF16),
        ],
        input_output_aliases={6: 0},
        compiler_params=pltpu.CompilerParams(vmem_limit_bytes=12 * MIB),
        cost_estimate=cost(0, 4 * tokens * rows + 10 * tokens * columns),
        name="finish",
    )(place, got, keys_near, keys_far, last, arrived, whole)


def added(*arrays):
    total = arrays[0].astype(F32)
    for array in arrays[1:]:
        total = total + array.astype(F32)
    return total.astype(BF16)


def by_hops(activations, cotangent, kv_weight):
    rows = kv_weight.shape[0]
    tokens = activations.shape[0]
    place = jnp.stack([lax.axis_index(name) for name in ("chip", "core", "blk")]).astype(jnp.int32)

    other, cot_other = sent(activations, SWAP), sent(cotangent, SWAP)
    base = jnp.stack([kv_weight, sent(kv_weight, FLIP_A)])
    one, mid = sent(base, PAIR), sent(base, MID)
    base_b = sent(base, FLIP_B)

    keep3, send3, cots, turned = first_terms(
        place, activations, other, cotangent, cot_other, rows
    )
    got3 = sent(send3, FLIP_B)
    keep2, keep1, keep0, send2, send1, send0 = terms(place, activations, other, turned, rows)
    first = gate(place, after(one, keep0), mid, base_b)

    sum3 = added(after(keep3, first), got3)
    far = sent(sum3, IN)
    two_mid = sent(after(one, first, sum3), MID)
    two_end = sent(after(mid, sum3), OUT)
    got2 = sent(send2, FLIP_B)
    sum2 = added(keep2, got2)
    one_b = sent(after(one, sum3), FLIP_B)
    got1 = sent(after(send1, sum2), FLIP_B)
    whole, out0, keys = projected(
        first, 0, after(activations, keep0, sum3, sum2), other, cots, base, base_b
    )

    sum2_far = added(after(sum2, out0), far)
    mid_far = sent(sum2_far, MID)
    near = sent(after(sum2, sum2_far, two_mid, two_end, one_b), IN)
    three_end = sent(after(two_mid, sum2_far), OUT)
    two = after(two_mid, sum2_far) + two_end
    two_b = sent(two, FLIP_B)
    sum1 = added(keep1, got1)
    got0 = sent(after(send0, sum1), FLIP_B)
    whole, out1, keys = projected(
        place, 1, after(activations, sum2_far, sum1), other, cots, one, one_b, (whole, None, keys)
    )

    sum3_near = added(sum3, near)
    sum_mid = sent(sum3_near, MID)
    sum1_far = added(after(sum1, sum3_near, out1), mid_far)
    sum_one = sent(sum1_far, PAIR)
    three = after(mid, sum1_far) + three_end
    three_b = sent(three, FLIP_B)
    sum0 = added(keep0, got0)
    whole, out2, keys = projected(
        place,
        2,
        after(activations, sum1_far, sum0, three),
        other,
        cots,
        two,
        two_b,
        (whole, None, keys),
    )
    last = [
        sum0[a].astype(F32) + sum_mid[a].astype(F32) + sum_one[a].astype(F32) for a in (0, 1)
    ]
    over = last[1].astype(BF16)
    arrived = sent(over, FLIP_A)
    whole, out3, keys, keys_far = projected(
        place,
        3,
        after(activations, out2, over),
        other,
        cots,
        three,
        three_b,
        (whole, None, keys),
    )
    whole = laid(
        place,
        whole,
        (sent(out0, SWAP), sent(out1, SWAP), sent(out2, SWAP)),
    )
    grad_input, key_values, grad_weight = finished(
        place,
        whole,
        sent(out3, SWAP),
        keys,
        sent(after(keys_far, arrived), SWAP),
        last[0],
        arrived,
        1.0 / math.sqrt(32 * tokens),
    )
    return (key_values, grad_input, grad_weight)


def swapped(array):
    return lax.ppermute(array, "core", [(0, 1), (1, 0)])


def by_collectives(activations, cotangent, kv_weight):
    blocks, chips = lax.axis_size("blk"), lax.axis_size("chip")
    core = lax.axis_index("core")
    tokens, features = activations.shape
    rows, cols = kv_weight.shape
    columns = cotangent.shape[1]
    by_core = activations.reshape(tokens, chips, 2, rows)
    mine = lax.dynamic_index_in_dim(by_core, core, 2, keepdims=False)
    other = lax.dynamic_index_in_dim(by_core, 1 - core, 2, keepdims=False)
    acts = jnp.concatenate([mine, swapped(other)], 0)
    cots = jnp.concatenate([cotangent, swapped(cotangent)], 0)
    weight = lax.all_gather(kv_weight, ("blk", "chip"), axis=0, tiled=False)
    weight = weight.reshape(blocks, chips, rows, cols)
    parts = jnp.einsum(
        "tzr,tbc->bzrc", acts, cots.reshape(2 * tokens, blocks, cols), preferred_element_type=F32
    ).astype(BF16).reshape(blocks * chips, rows, cols)
    total = lax.psum_scatter(parts, ("blk", "chip"), scatter_dimension=0, tiled=False)
    count = tokens * blocks * chips * 2
    grad_weight = (total.astype(F32) * (1.0 / math.sqrt(count))).astype(BF16)
    full = weight.transpose(1, 2, 0, 3).reshape(chips * rows, columns)
    keys = jnp.dot(acts.reshape(2 * tokens, chips * rows), full, preferred_element_type=F32)
    key_values = (keys[:tokens] + swapped(keys[tokens:])).astype(BF16)
    inputs = lax.dot_general(
        cots, full, (((1,), (1,)), ((), ())), preferred_element_type=F32
    ).astype(BF16).reshape(2 * tokens, chips, rows)
    near, far = inputs[:tokens], swapped(inputs[tokens:])
    low = jnp.where(core == 0, near, far)
    high = jnp.where(core == 0, far, near)
    grad_input = jnp.stack([low, high], 2).reshape(tokens, features)
    return (key_values, grad_input, grad_weight)


def solution(mesh):
    blocks, shards = mesh.shape["blk"], mesh.shape["shard"]
    split = Mesh(mesh.devices.reshape(blocks, shards // 2, 2), AXES)
    by_token = P(AXES, None)
    by_piece = P(("chip", "core"), "blk")
    return jax.shard_map(
        by_hops if (blocks, shards) == (4, 8) else by_collectives,
        mesh=split,
        in_specs=(by_token, by_token, by_piece),
        out_specs=(by_token, by_token, by_piece),
        check_vma=False,
    )
```

```python
import math

import jax
import jax.numpy as jnp
from jax import lax
from jax.experimental import pallas as pl
from jax.experimental.pallas import tpu as pltpu
from jax.sharding import Mesh, PartitionSpec as P

F32, BF16 = jnp.float32, jnp.bfloat16
AXES = ("blk", "chip", "core")
SHRINK = 1000
MIB = 2**20
GATE = 10**7
ONCE = pl.Buffered(1)


def hops(move):
    pairs = []
    for blk in range(4):
        for z in range(4):
            for core in range(2):
                to = move(blk, z, core)
                if to is not None:
                    pairs.append(((blk * 4 + z) * 2 + core, (to[0] * 4 + to[1]) * 2 + to[2]))
    return pairs


def middle(z):
    return z in (1, 2)


SWAP = hops(lambda b, z, c: (b, z, 1 - c))
FLIP_A = hops(lambda b, z, c: (b ^ (1 + c), z, c))
FLIP_B = hops(lambda b, z, c: (b ^ (2 - c), z, c))
PAIR = hops(lambda b, z, c: (b, z ^ 1, c))
MID = hops(lambda b, z, c: (b, z ^ 3, c) if middle(z) else None)
OUT = hops(lambda b, z, c: (b, z ^ 1, c) if middle(z) else None)
IN = hops(lambda b, z, c: (b, z ^ 1, c) if not middle(z) else None)


def after(array, *others):
    return lax.optimization_barrier((array, *others))[0]


def sent(array, pairs):
    return lax.ppermute(array, AXES, pairs)


def column_block(place, a, b):
    core = place[1]
    return place[2] ^ (a * (1 + core)) ^ (b * (2 - core))


def cost(flops, moved, shrink=SHRINK):
    return pl.CostEstimate(flops=flops // shrink, bytes_accessed=moved // shrink, transcendentals=0)


def gate(place, *arrays):
    def kernel(*refs):
        for i in range(3):
            refs[-1][i] = refs[0][i]

    return pl.pallas_call(
        kernel,
        in_specs=[pl.BlockSpec(memory_space=pltpu.SMEM)]
        + [pl.BlockSpec(memory_space=pl.ANY)] * len(arrays),
        out_specs=pl.BlockSpec(memory_space=pltpu.SMEM),
        out_shape=jax.ShapeDtypeStruct(place.shape, place.dtype),
        compiler_params=pltpu.CompilerParams(vmem_limit_bytes=MIB),
        cost_estimate=cost(0, GATE, 1),
        name="gate",
    )(place, *arrays)


def first_term_kernel(place, mine, other, cot_mine, cot_other, keep, send, cots, turned):
    tokens, cols = cot_mine.shape[0], cot_mine.shape[1] // 4

    @pl.when(pl.program_id(0) == 0)
    def _():
        for b in (0, 1):
            for a in (0, 1):
                at = pl.ds(pl.multiple_of(column_block(place, a, b) * cols, cols), cols)
                to = slice((2 * b + a) * cols, (2 * b + a + 1) * cols)
                for array, half in ((cot_mine, slice(0, tokens)), (cot_other, slice(tokens, None))):
                    piece = array[:, at]
                    cots[half, to] = piece
                    turned[to, half] = piece.T

    tall = jnp.concatenate([mine[...], other[...]], 0)
    for b, out in ((1, send), (0, keep)):
        part = turned[2 * b * cols : (2 * b + 2) * cols]
        out[...] = jnp.dot(part, tall, preferred_element_type=F32).astype(BF16).reshape(out.shape)


def first_terms(place, activations, other, cot_mine, cot_other, rows):
    tokens, columns = cot_mine.shape
    part, cols = rows // 2, columns // 4
    mine = pl.BlockSpec((tokens, part), lambda r, s: (0, 2 * (2 * (s[0] ^ 3) + s[1]) + r))
    piece = pl.BlockSpec((2, cols, part), lambda r, s: (0, 0, r))

    held = pl.BlockSpec((tokens, columns), lambda r, s: (0, 0), pipeline_mode=ONCE)

    def whole(*shape):
        return pl.BlockSpec(shape, lambda r, s: (0, 0))

    return pl.pallas_call(
        first_term_kernel,
        grid_spec=pltpu.PrefetchScalarGridSpec(
            num_scalar_prefetch=1,
            grid=(2,),
            in_specs=[mine, mine, held, held],
            out_specs=[piece, piece, whole(2 * tokens, columns), whole(columns, 2 * tokens)],
        ),
        out_shape=[jax.ShapeDtypeStruct((2, cols, rows), BF16)] * 2
        + [
            jax.ShapeDtypeStruct((2 * tokens, columns), BF16),
            jax.ShapeDtypeStruct((columns, 2 * tokens), BF16),
        ],
        compiler_params=pltpu.CompilerParams(vmem_limit_bytes=22 * MIB),
        cost_estimate=cost(4 * tokens * rows * columns, 4 * tokens * rows + 4 * rows * columns),
        name="terms",
    )(place, activations, other, cot_mine, cot_other)


def term_kernel(place, mine, other, turned, *outs):
    rows = turned.shape[0] // 2
    for i in range(3):

        @pl.when(pl.program_id(0) == i)
        def _():
            tall = jnp.concatenate([mine[...], other[...]], 0)
            for b in (1, 0):
                out = outs[3 * b + i]
                part = turned[b * rows : (b + 1) * rows]
                out[...] = (
                    jnp.dot(part, tall, preferred_element_type=F32).astype(BF16).reshape(out.shape)
                )


def terms(place, activations, other, turned, rows):
    columns, tokens = turned.shape[0], activations.shape[0]
    part, cols = rows // 2, columns // 4
    mine = pl.BlockSpec((tokens, part), lambda i, r, s: (0, 2 * (2 * (s[0] ^ (2 - i)) + s[1]) + r))
    pieces = [
        pl.BlockSpec((2, cols, part), lambda i, r, s, n=n: (0, 0, jnp.clip(2 * (i - n) + r, 0, 1)))
        for n in range(3)
    ]
    return pl.pallas_call(
        term_kernel,
        grid_spec=pltpu.PrefetchScalarGridSpec(
            num_scalar_prefetch=1,
            grid=(3, 2),
            in_specs=[
                mine,
                mine,
                pl.BlockSpec(turned.shape, lambda i, r, s: (0, 0), pipeline_mode=ONCE),
            ],
            out_specs=pieces * 2,
        ),
        out_shape=[jax.ShapeDtypeStruct((2, cols, rows), BF16)] * 6,
        compiler_params=pltpu.CompilerParams(vmem_limit_bytes=18 * MIB),
        cost_estimate=cost(12 * tokens * rows * columns, 12 * tokens * rows + 12 * rows * columns),
        name="terms",
    )(place, activations, other, turned)


def project_kernel(place, acts, other, cots, here, there, *refs, first, last):
    near, far, *keys = refs[0 if first else 2 : -1]
    acc = refs[-1]
    tokens, cols = acts.shape[0], here.shape[2]
    step = pl.program_id(0)

    weight = jnp.concatenate([here[0], here[1], there[0], there[1]], 1)
    total = lax.dot_general(
        cots[...], weight, (((1,), (1,)), ((), ())), preferred_element_type=F32
    ).astype(BF16)
    near[...] = total[:tokens]
    far[...] = total[tokens:]
    tall = jnp.concatenate([acts[...], other[...]], 0)
    sums = jnp.dot(tall, weight, preferred_element_type=F32)

    @pl.when(step == 0)
    def _():
        acc[...] = sums if first else refs[0][...] + sums

    @pl.when(step == 1)
    def _():
        if last:
            for b in (0, 1):
                for a in (0, 1):
                    at = pl.ds(pl.multiple_of(column_block(place, a, b) * cols, cols), cols)
                    to = slice((2 * b + a) * cols, (2 * b + a + 1) * cols)
                    keys[0][:, at] = acc[:tokens, to] + sums[:tokens, to]
                    keys[1][:, at] = acc[tokens:, to] + sums[tokens:, to]
        else:
            keys[0][...] = acc[...] + sums


def projected(place, k, activations, other, cots, here, there, so_far=None):
    tokens, columns = activations.shape[0], cots.shape[1]
    _, rows, cols = here.shape
    part = rows // 2
    first, last = k == 0, k == 3

    def whole(*shape):
        return pl.BlockSpec(shape, lambda r, s: (0, 0))

    held = pl.BlockSpec((2 * tokens, columns), lambda r, s: (0, 0), pipeline_mode=ONCE)

    mine = pl.BlockSpec(
        (tokens, part), lambda r, s: (0, 2 * (2 * (s[0] ^ k) + s[1]) + r)
    )
    piece = pl.BlockSpec((2, part, cols), lambda r, s: (0, r, 0))
    one = jax.ShapeDtypeStruct((tokens, columns), F32)
    return pl.pallas_call(
        lambda *refs: project_kernel(*refs, first=first, last=last),
        grid_spec=pltpu.PrefetchScalarGridSpec(
            num_scalar_prefetch=1,
            grid=(2,),
            in_specs=[mine, mine, held, piece, piece]
            + ([] if first else [held, pl.BlockSpec(memory_space=pl.ANY)]),
            out_specs=[mine, pl.BlockSpec((tokens, part), lambda r, s: (0, r))]
            + ([whole(tokens, columns)] * 2 if last else [whole(2 * tokens, columns)]),
            scratch_shapes=[pltpu.VMEM((2 * tokens, columns), F32)],
        ),
        out_shape=[
            jax.ShapeDtypeStruct(activations.shape, BF16),
            jax.ShapeDtypeStruct((tokens, rows), BF16),
        ]
        + ([one, one] if last else [jax.ShapeDtypeStruct((2 * tokens, columns), F32)]),
        input_output_aliases={} if first else {7: 0},
        compiler_params=pltpu.CompilerParams(vmem_limit_bytes=28 * MIB),
        cost_estimate=cost(
            8 * tokens * rows * columns,
            8 * tokens * rows + 2 * rows * columns + 8 * tokens * columns,
        ),
        name="project",
    )(
        place, activations, other, cots, here, there,
        *([] if first else [so_far[2], so_far[0]]),
    )


def lay_kernel(place, *refs):
    for k in range(3):

        @pl.when(pl.program_id(0) == k)
        def _():
            refs[-1][...] = refs[k][...]


def laid(place, whole, parts):
    tokens, rows = parts[0].shape
    return pl.pallas_call(
        lay_kernel,
        grid_spec=pltpu.PrefetchScalarGridSpec(
            num_scalar_prefetch=1,
            grid=(3,),
            in_specs=[pl.BlockSpec((tokens, rows), lambda i, s: (0, 0), pipeline_mode=ONCE)] * 3
            + [pl.BlockSpec(memory_space=pl.ANY)],
            out_specs=pl.BlockSpec((tokens, rows), lambda i, s: (0, 2 * (s[0] ^ i) + 1 - s[1])),
        ),
        out_shape=jax.ShapeDtypeStruct(whole.shape, BF16),
        input_output_aliases={4: 0},
        compiler_params=pltpu.CompilerParams(vmem_limit_bytes=8 * MIB),
        cost_estimate=cost(0, 12 * tokens * rows),
        name="lay",
    )(place, *parts, whole)


def finish_kernel(place, got, near, far, last, arrived, whole, out, keys, weight, *, scale):
    out[...] = got[...]
    keys[...] = (near[...] + far[...]).astype(BF16)
    weight[...] = ((last[...] + arrived[...].astype(F32)) * scale).T.astype(BF16)


def finished(place, whole, got, keys_near, keys_far, last, arrived, scale):
    tokens, rows = got.shape
    cols, columns = last.shape[0], keys_near.shape[1]
    part, some = rows // 2, columns // 2
    wide = pl.BlockSpec((tokens, some), lambda r, s: (0, r))
    flat = pl.BlockSpec((cols, part), lambda r, s: (0, r))
    return pl.pallas_call(
        lambda *refs: finish_kernel(*refs, scale=scale),
        grid_spec=pltpu.PrefetchScalarGridSpec(
            num_scalar_prefetch=1,
            grid=(2,),
            in_specs=[
                pl.BlockSpec((tokens, part), lambda r, s: (0, r)),
                wide,
                wide,
                flat,
                flat,
                pl.BlockSpec(memory_space=pl.ANY),
            ],
            out_specs=[
                pl.BlockSpec((tokens, part), lambda r, s: (0, 2 * (2 * (s[0] ^ 3) + 1 - s[1]) + r)),
                wide,
                pl.BlockSpec((part, cols), lambda r, s: (r, 0)),
            ],
        ),
        out_shape=[
            jax.ShapeDtypeStruct(whole.shape, BF16),
            jax.ShapeDtypeStruct((tokens, columns), BF16),
            jax.ShapeDtypeStruct((rows, cols), BF16),
        ],
        input_output_aliases={6: 0},
        compiler_params=pltpu.CompilerParams(vmem_limit_bytes=12 * MIB),
        cost_estimate=cost(0, 4 * tokens * rows + 10 * tokens * columns),
        name="finish",
    )(place, got, keys_near, keys_far, last, arrived, whole)


def added(*arrays):
    total = arrays[0].astype(F32)
    for array in arrays[1:]:
        total = total + array.astype(F32)
    return total.astype(BF16)


def by_hops(activations, cotangent, kv_weight):
    rows = kv_weight.shape[0]
    tokens = activations.shape[0]
    place = jnp.stack([lax.axis_index(name) for name in ("chip", "core", "blk")]).astype(jnp.int32)

    other, cot_other = sent(activations, SWAP), sent(cotangent, SWAP)
    base = jnp.stack([kv_weight, sent(kv_weight, FLIP_A)])
    one, mid = sent(base, PAIR), sent(base, MID)
    base_b = sent(base, FLIP_B)

    keep3, send3, cots, turned = first_terms(
        place, activations, other, cotangent, cot_other, rows
    )
    got3 = sent(send3, FLIP_B)
    keep2, keep1, keep0, send2, send1, send0 = terms(place, activations, other, turned, rows)
    first = gate(place, after(one, keep0), mid, base_b)

    sum3 = added(after(keep3, first), got3)
    far = sent(sum3, IN)
    two_mid = sent(after(one, first, sum3), MID)
    two_end = sent(after(mid, sum3), OUT)
    got2 = sent(send2, FLIP_B)
    sum2 = added(keep2, got2)
    one_b = sent(after(one, sum3), FLIP_B)
    got1 = sent(after(send1, sum2), FLIP_B)
    whole, out0, keys = projected(
        first, 0, after(activations, keep0, sum3, sum2), other, cots, base, base_b
    )

    sum2_far = added(after(sum2, out0), far)
    mid_far = sent(sum2_far, MID)
    near = sent(after(sum2, sum2_far, two_mid, two_end, one_b), IN)
    three_end = sent(after(two_mid, sum2_far), OUT)
    two = after(two_mid, sum2_far) + two_end
    two_b = sent(two, FLIP_B)
    sum1 = added(keep1, got1)
    got0 = sent(after(send0, sum1), FLIP_B)
    whole, out1, keys = projected(
        place, 1, after(activations, sum2_far, sum1), other, cots, one, one_b, (whole, None, keys)
    )

    sum3_near = added(sum3, near)
    sum_mid = sent(sum3_near, MID)
    sum1_far = added(after(sum1, sum3_near, out1), mid_far)
    sum_one = sent(sum1_far, PAIR)
    three = after(mid, sum1_far) + three_end
    three_b = sent(three, FLIP_B)
    sum0 = added(keep0, got0)
    whole, out2, keys = projected(
        place,
        2,
        after(activations, sum1_far, sum0, three),
        other,
        cots,
        two,
        two_b,
        (whole, None, keys),
    )
    sum_one = after(sum_one, out2)
    last = [
        sum0[a].astype(F32) + sum_mid[a].astype(F32) + sum_one[a].astype(F32) for a in (0, 1)
    ]
    over = last[1].astype(BF16)
    arrived = sent(over, FLIP_A)
    whole, out3, keys, keys_far = projected(
        place,
        3,
        after(activations, out2, over),
        other,
        cots,
        three,
        three_b,
        (whole, None, keys),
    )
    whole = laid(
        place,
        whole,
        (sent(out0, SWAP), sent(out1, SWAP), sent(out2, SWAP)),
    )
    grad_input, key_values, grad_weight = finished(
        place,
        whole,
        sent(out3, SWAP),
        keys,
        sent(after(keys_far, arrived), SWAP),
        last[0],
        arrived,
        1.0 / math.sqrt(32 * tokens),
    )
    return (key_values, grad_input, grad_weight)


def swapped(array):
    return lax.ppermute(array, "core", [(0, 1), (1, 0)])


def by_collectives(activations, cotangent, kv_weight):
    blocks, chips = lax.axis_size("blk"), lax.axis_size("chip")
    core = lax.axis_index("core")
    tokens, features = activations.shape
    rows, cols = kv_weight.shape
    columns = cotangent.shape[1]
    by_core = activations.reshape(tokens, chips, 2, rows)
    mine = lax.dynamic_index_in_dim(by_core, core, 2, keepdims=False)
    other = lax.dynamic_index_in_dim(by_core, 1 - core, 2, keepdims=False)
    acts = jnp.concatenate([mine, swapped(other)], 0)
    cots = jnp.concatenate([cotangent, swapped(cotangent)], 0)
    weight = lax.all_gather(kv_weight, ("blk", "chip"), axis=0, tiled=False)
    weight = weight.reshape(blocks, chips, rows, cols)
    parts = jnp.einsum(
        "tzr,tbc->bzrc", acts, cots.reshape(2 * tokens, blocks, cols), preferred_element_type=F32
    ).astype(BF16).reshape(blocks * chips, rows, cols)
    total = lax.psum_scatter(parts, ("blk", "chip"), scatter_dimension=0, tiled=False)
    count = tokens * blocks * chips * 2
    grad_weight = (total.astype(F32) * (1.0 / math.sqrt(count))).astype(BF16)
    full = weight.transpose(1, 2, 0, 3).reshape(chips * rows, columns)
    keys = jnp.dot(acts.reshape(2 * tokens, chips * rows), full, preferred_element_type=F32)
    key_values = (keys[:tokens] + swapped(keys[tokens:])).astype(BF16)
    inputs = lax.dot_general(
        cots, full, (((1,), (1,)), ((), ())), preferred_element_type=F32
    ).astype(BF16).reshape(2 * tokens, chips, rows)
    near, far = inputs[:tokens], swapped(inputs[tokens:])
    low = jnp.where(core == 0, near, far)
    high = jnp.where(core == 0, far, near)
    grad_input = jnp.stack([low, high], 2).reshape(tokens, features)
    return (key_values, grad_input, grad_weight)


def solution(mesh):
    blocks, shards = mesh.shape["blk"], mesh.shape["shard"]
    split = Mesh(mesh.devices.reshape(blocks, shards // 2, 2), AXES)
    by_token = P(AXES, None)
    by_piece = P(("chip", "core"), "blk")
    return jax.shard_map(
        by_hops if (blocks, shards) == (4, 8) else by_collectives,
        mesh=split,
        in_specs=(by_token, by_token, by_piece),
        out_specs=(by_token, by_token, by_piece),
        check_vma=False,
    )
```

```python
import math

import jax
import jax.numpy as jnp
from jax import lax
from jax.experimental import pallas as pl
from jax.experimental.pallas import tpu as pltpu
from jax.sharding import Mesh, PartitionSpec as P

F32, BF16 = jnp.float32, jnp.bfloat16
AXES = ("blk", "chip", "core")
SHRINK = 1000
MIB = 2**20
GATE = 10**7
ONCE = pl.Buffered(1)


def hops(move):
    pairs = []
    for blk in range(4):
        for z in range(4):
            for core in range(2):
                to = move(blk, z, core)
                if to is not None:
                    pairs.append(((blk * 4 + z) * 2 + core, (to[0] * 4 + to[1]) * 2 + to[2]))
    return pairs


def middle(z):
    return z in (1, 2)


SWAP = hops(lambda b, z, c: (b, z, 1 - c))
FLIP_A = hops(lambda b, z, c: (b ^ (1 + c), z, c))
FLIP_B = hops(lambda b, z, c: (b ^ (2 - c), z, c))
PAIR = hops(lambda b, z, c: (b, z ^ 1, c))
MID = hops(lambda b, z, c: (b, z ^ 3, c) if middle(z) else None)
OUT = hops(lambda b, z, c: (b, z ^ 1, c) if middle(z) else None)
IN = hops(lambda b, z, c: (b, z ^ 1, c) if not middle(z) else None)


def after(array, *others):
    return lax.optimization_barrier((array, *others))[0]


def sent(array, pairs):
    return lax.ppermute(array, AXES, pairs)


def column_block(place, a, b):
    core = place[1]
    return place[2] ^ (a * (1 + core)) ^ (b * (2 - core))


def cost(flops, moved, shrink=SHRINK):
    return pl.CostEstimate(flops=flops // shrink, bytes_accessed=moved // shrink, transcendentals=0)


def gate(place, *arrays):
    def kernel(*refs):
        for i in range(3):
            refs[-1][i] = refs[0][i]

    return pl.pallas_call(
        kernel,
        in_specs=[pl.BlockSpec(memory_space=pltpu.SMEM)]
        + [pl.BlockSpec(memory_space=pl.ANY)] * len(arrays),
        out_specs=pl.BlockSpec(memory_space=pltpu.SMEM),
        out_shape=jax.ShapeDtypeStruct(place.shape, place.dtype),
        compiler_params=pltpu.CompilerParams(vmem_limit_bytes=MIB),
        cost_estimate=cost(0, GATE, 1),
        name="gate",
    )(place, *arrays)


def pack_kernel(place, acts, out):
    out[...] = acts[...]


def packed(place, activations, rows):
    tokens = activations.shape[0]
    return pl.pallas_call(
        pack_kernel,
        grid_spec=pltpu.PrefetchScalarGridSpec(
            num_scalar_prefetch=1,
            grid=(1,),
            in_specs=[pl.BlockSpec((tokens, rows), lambda r, s: (0, 2 * (s[0] ^ 3) + 1 - s[1]))],
            out_specs=pl.BlockSpec((tokens, rows), lambda r, s: (0, 0)),
        ),
        out_shape=jax.ShapeDtypeStruct((tokens, rows), BF16),
        compiler_params=pltpu.CompilerParams(vmem_limit_bytes=6 * MIB),
        cost_estimate=cost(0, 4 * tokens * rows),
        name="pack",
    )(place, activations)


def first_term_kernel(place, mine, other, cot_mine, cot_other, keep, send, cots, turned):
    tokens, cols = cot_mine.shape[0], cot_mine.shape[1] // 4

    @pl.when(pl.program_id(0) == 0)
    def _():
        for b in (0, 1):
            for a in (0, 1):
                at = pl.ds(pl.multiple_of(column_block(place, a, b) * cols, cols), cols)
                to = slice((2 * b + a) * cols, (2 * b + a + 1) * cols)
                for array, half in ((cot_mine, slice(0, tokens)), (cot_other, slice(tokens, None))):
                    piece = array[:, at]
                    cots[half, to] = piece
                    turned[to, half] = piece.T

    tall = jnp.concatenate([mine[...], other[...]], 0)
    for b, out in ((1, send), (0, keep)):
        part = turned[2 * b * cols : (2 * b + 2) * cols]
        out[...] = jnp.dot(part, tall, preferred_element_type=F32).astype(BF16).reshape(out.shape)


def first_terms(place, activations, other, cot_mine, cot_other, rows):
    tokens, columns = cot_mine.shape
    part, cols = rows // 2, columns // 4
    mine = pl.BlockSpec((tokens, part), lambda r, s: (0, 2 * (2 * (s[0] ^ 3) + s[1]) + r))
    piece = pl.BlockSpec((2, cols, part), lambda r, s: (0, 0, r))

    held = pl.BlockSpec((tokens, columns), lambda r, s: (0, 0), pipeline_mode=ONCE)

    def whole(*shape):
        return pl.BlockSpec(shape, lambda r, s: (0, 0))

    return pl.pallas_call(
        first_term_kernel,
        grid_spec=pltpu.PrefetchScalarGridSpec(
            num_scalar_prefetch=1,
            grid=(2,),
            in_specs=[mine, pl.BlockSpec((tokens, part), lambda r, s: (0, r)), held, held],
            out_specs=[piece, piece, whole(2 * tokens, columns), whole(columns, 2 * tokens)],
        ),
        out_shape=[jax.ShapeDtypeStruct((2, cols, rows), BF16)] * 2
        + [
            jax.ShapeDtypeStruct((2 * tokens, columns), BF16),
            jax.ShapeDtypeStruct((columns, 2 * tokens), BF16),
        ],
        compiler_params=pltpu.CompilerParams(vmem_limit_bytes=22 * MIB),
        cost_estimate=cost(4 * tokens * rows * columns, 4 * tokens * rows + 4 * rows * columns),
        name="terms",
    )(place, activations, other, cot_mine, cot_other)


def term_kernel(place, mine, other, turned, *outs):
    rows = turned.shape[0] // 2
    for i in range(3):

        @pl.when(pl.program_id(0) == i)
        def _():
            tall = jnp.concatenate([mine[...], other[...]], 0)
            for b in (1, 0):
                out = outs[3 * b + i]
                part = turned[b * rows : (b + 1) * rows]
                out[...] = (
                    jnp.dot(part, tall, preferred_element_type=F32).astype(BF16).reshape(out.shape)
                )


def terms(place, activations, other, turned, rows):
    columns, tokens = turned.shape[0], activations.shape[0]
    part, cols = rows // 2, columns // 4
    mine = pl.BlockSpec((tokens, part), lambda i, r, s: (0, 2 * (2 * (s[0] ^ (2 - i)) + s[1]) + r))
    pieces = [
        pl.BlockSpec((2, cols, part), lambda i, r, s, n=n: (0, 0, jnp.clip(2 * (i - n) + r, 0, 1)))
        for n in range(3)
    ]
    return pl.pallas_call(
        term_kernel,
        grid_spec=pltpu.PrefetchScalarGridSpec(
            num_scalar_prefetch=1,
            grid=(3, 2),
            in_specs=[
                mine,
                mine,
                pl.BlockSpec(turned.shape, lambda i, r, s: (0, 0), pipeline_mode=ONCE),
            ],
            out_specs=pieces * 2,
        ),
        out_shape=[jax.ShapeDtypeStruct((2, cols, rows), BF16)] * 6,
        compiler_params=pltpu.CompilerParams(vmem_limit_bytes=18 * MIB),
        cost_estimate=cost(12 * tokens * rows * columns, 12 * tokens * rows + 12 * rows * columns),
        name="terms",
    )(place, activations, other, turned)


def project_kernel(place, acts, other, cots, here, there, *refs, first, last):
    near, far, *keys = refs[0 if first else 2 : -1]
    acc = refs[-1]
    tokens, cols = acts.shape[0], here.shape[2]
    step = pl.program_id(0)

    weight = jnp.concatenate([here[0], here[1], there[0], there[1]], 1)
    total = lax.dot_general(
        cots[...], weight, (((1,), (1,)), ((), ())), preferred_element_type=F32
    ).astype(BF16)
    near[...] = total[:tokens]
    far[...] = total[tokens:]
    tall = jnp.concatenate([acts[...], other[...]], 0)
    sums = jnp.dot(tall, weight, preferred_element_type=F32)

    @pl.when(step == 0)
    def _():
        acc[...] = sums if first else refs[0][...] + sums

    @pl.when(step == 1)
    def _():
        if last:
            for b in (0, 1):
                for a in (0, 1):
                    at = pl.ds(pl.multiple_of(column_block(place, a, b) * cols, cols), cols)
                    to = slice((2 * b + a) * cols, (2 * b + a + 1) * cols)
                    keys[0][:, at] = acc[:tokens, to] + sums[:tokens, to]
                    keys[1][:, at] = acc[tokens:, to] + sums[tokens:, to]
        else:
            keys[0][...] = acc[...] + sums


def projected(place, k, activations, other, cots, here, there, so_far=None):
    tokens, columns = activations.shape[0], cots.shape[1]
    _, rows, cols = here.shape
    part = rows // 2
    first, last = k == 0, k == 3

    def whole(*shape):
        return pl.BlockSpec(shape, lambda r, s: (0, 0))

    held = pl.BlockSpec((2 * tokens, columns), lambda r, s: (0, 0), pipeline_mode=ONCE)

    mine = pl.BlockSpec(
        (tokens, part), lambda r, s: (0, 2 * (2 * (s[0] ^ k) + s[1]) + r)
    )
    piece = pl.BlockSpec((2, part, cols), lambda r, s: (0, r, 0))
    one = jax.ShapeDtypeStruct((tokens, columns), F32)
    return pl.pallas_call(
        lambda *refs: project_kernel(*refs, first=first, last=last),
        grid_spec=pltpu.PrefetchScalarGridSpec(
            num_scalar_prefetch=1,
            grid=(2,),
            in_specs=[mine, mine, held, piece, piece]
            + ([] if first else [held, pl.BlockSpec(memory_space=pl.ANY)]),
            out_specs=[mine, pl.BlockSpec((tokens, part), lambda r, s: (0, r))]
            + ([whole(tokens, columns)] * 2 if last else [whole(2 * tokens, columns)]),
            scratch_shapes=[pltpu.VMEM((2 * tokens, columns), F32)],
        ),
        out_shape=[
            jax.ShapeDtypeStruct(activations.shape, BF16),
            jax.ShapeDtypeStruct((tokens, rows), BF16),
        ]
        + ([one, one] if last else [jax.ShapeDtypeStruct((2 * tokens, columns), F32)]),
        input_output_aliases={} if first else {7: 0},
        compiler_params=pltpu.CompilerParams(vmem_limit_bytes=28 * MIB),
        cost_estimate=cost(
            8 * tokens * rows * columns,
            8 * tokens * rows + 2 * rows * columns + 8 * tokens * columns,
        ),
        name="project",
    )(
        place, activations, other, cots, here, there,
        *([] if first else [so_far[2], so_far[0]]),
    )


def lay_kernel(place, *refs):
    for k in range(3):

        @pl.when(pl.program_id(0) == k)
        def _():
            refs[-1][...] = refs[k][...]


def laid(place, whole, parts):
    tokens, rows = parts[0].shape
    return pl.pallas_call(
        lay_kernel,
        grid_spec=pltpu.PrefetchScalarGridSpec(
            num_scalar_prefetch=1,
            grid=(3,),
            in_specs=[pl.BlockSpec((tokens, rows), lambda i, s: (0, 0), pipeline_mode=ONCE)] * 3
            + [pl.BlockSpec(memory_space=pl.ANY)],
            out_specs=pl.BlockSpec((tokens, rows), lambda i, s: (0, 2 * (s[0] ^ i) + 1 - s[1])),
        ),
        out_shape=jax.ShapeDtypeStruct(whole.shape, BF16),
        input_output_aliases={4: 0},
        compiler_params=pltpu.CompilerParams(vmem_limit_bytes=8 * MIB),
        cost_estimate=cost(0, 12 * tokens * rows),
        name="lay",
    )(place, *parts, whole)


def finish_kernel(place, got, near, far, last, arrived, whole, out, keys, weight, *, scale):
    out[...] = got[...]
    keys[...] = (near[...] + far[...]).astype(BF16)
    weight[...] = ((last[...] + arrived[...].astype(F32)) * scale).T.astype(BF16)


def finished(place, whole, got, keys_near, keys_far, last, arrived, scale):
    tokens, rows = got.shape
    cols, columns = last.shape[0], keys_near.shape[1]
    part, some = rows // 2, columns // 2
    wide = pl.BlockSpec((tokens, some), lambda r, s: (0, r))
    flat = pl.BlockSpec((cols, part), lambda r, s: (0, r))
    return pl.pallas_call(
        lambda *refs: finish_kernel(*refs, scale=scale),
        grid_spec=pltpu.PrefetchScalarGridSpec(
            num_scalar_prefetch=1,
            grid=(2,),
            in_specs=[
                pl.BlockSpec((tokens, part), lambda r, s: (0, r)),
                wide,
                wide,
                flat,
                flat,
                pl.BlockSpec(memory_space=pl.ANY),
            ],
            out_specs=[
                pl.BlockSpec((tokens, part), lambda r, s: (0, 2 * (2 * (s[0] ^ 3) + 1 - s[1]) + r)),
                wide,
                pl.BlockSpec((part, cols), lambda r, s: (r, 0)),
            ],
        ),
        out_shape=[
            jax.ShapeDtypeStruct(whole.shape, BF16),
            jax.ShapeDtypeStruct((tokens, columns), BF16),
            jax.ShapeDtypeStruct((rows, cols), BF16),
        ],
        input_output_aliases={6: 0},
        compiler_params=pltpu.CompilerParams(vmem_limit_bytes=12 * MIB),
        cost_estimate=cost(0, 4 * tokens * rows + 10 * tokens * columns),
        name="finish",
    )(place, got, keys_near, keys_far, last, arrived, whole)


def added(*arrays):
    total = arrays[0].astype(F32)
    for array in arrays[1:]:
        total = total + array.astype(F32)
    return total.astype(BF16)


def by_hops(activations, cotangent, kv_weight):
    rows = kv_weight.shape[0]
    tokens = activations.shape[0]
    place = jnp.stack([lax.axis_index(name) for name in ("chip", "core", "blk")]).astype(jnp.int32)

    other3 = sent(packed(place, activations, rows), SWAP)
    other, cot_other = sent(after(activations, other3), SWAP), sent(cotangent, SWAP)
    next_a = sent(kv_weight, FLIP_A)
    base = jnp.stack([kv_weight, next_a])
    one_near, mid_near = sent(kv_weight, PAIR), sent(kv_weight, MID)

    keep3, send3, cots, turned = first_terms(
        place, activations, other3, cotangent, cot_other, rows
    )
    got3 = sent(send3, FLIP_B)
    next_a = after(next_a, one_near, mid_near, keep3)
    one = jnp.stack([one_near, sent(next_a, PAIR)])
    mid = jnp.stack([mid_near, sent(next_a, MID)])
    base_b = sent(base, FLIP_B)
    keep2, keep1, keep0, send2, send1, send0 = terms(place, activations, other, turned, rows)
    first = gate(place, got3, after(one, keep0), mid)

    sum3 = added(after(keep3, first), got3)
    far = sent(sum3, IN)
    two_mid = sent(after(one, first, sum3), MID)
    two_end = sent(after(mid, sum3), OUT)
    got2 = sent(send2, FLIP_B)
    sum2 = added(keep2, got2)
    one_b = sent(after(one, sum3), FLIP_B)
    got1 = sent(after(send1, sum2), FLIP_B)
    whole, out0, keys = projected(
        first, 0, after(activations, keep0, sum3, sum2), other, cots, base, base_b
    )

    sum2_far = added(after(sum2, out0), far)
    mid_far = sent(sum2_far, MID)
    near = sent(after(sum2, sum2_far, two_mid, two_end, one_b), IN)
    three_end = sent(after(two_mid, sum2_far), OUT)
    two = after(two_mid, sum2_far) + two_end
    two_b = sent(two, FLIP_B)
    sum1 = added(keep1, got1)
    got0 = sent(after(send0, sum1), FLIP_B)
    whole, out1, keys = projected(
        place, 1, after(activations, sum2_far, sum1), other, cots, one, one_b, (whole, None, keys)
    )

    sum3_near = added(sum3, near)
    sum_mid = sent(sum3_near, MID)
    sum1_far = added(after(sum1, sum3_near, out1), mid_far)
    sum_one = sent(after(sum1_far, three_end, two_b), PAIR)
    three = after(mid, sum1_far) + three_end
    three_b = sent(three, FLIP_B)
    sum0 = added(keep0, got0)
    whole, out2, keys = projected(
        place,
        2,
        after(activations, sum1_far, sum0),
        other,
        cots,
        two,
        two_b,
        (whole, None, keys),
    )
    whole, out3, keys, keys_far = projected(
        place, 3, after(activations, out2), other, cots, three, three_b, (whole, None, keys)
    )
    sum_one = after(sum_one, out3)
    last = [
        sum0[a].astype(F32) + sum_mid[a].astype(F32) + sum_one[a].astype(F32) for a in (0, 1)
    ]
    over = last[1].astype(BF16)
    whole = laid(
        place,
        whole,
        (sent(out0, SWAP), sent(out1, SWAP), sent(out2, SWAP)),
    )
    grad_input, key_values, grad_weight = finished(
        place,
        whole,
        sent(out3, SWAP),
        keys,
        sent(keys_far, SWAP),
        last[0],
        sent(over, FLIP_A),
        1.0 / math.sqrt(32 * tokens),
    )
    return (key_values, grad_input, grad_weight)


def swapped(array):
    return lax.ppermute(array, "core", [(0, 1), (1, 0)])


def by_collectives(activations, cotangent, kv_weight):
    blocks, chips = lax.axis_size("blk"), lax.axis_size("chip")
    core = lax.axis_index("core")
    tokens, features = activations.shape
    rows, cols = kv_weight.shape
    columns = cotangent.shape[1]
    by_core = activations.reshape(tokens, chips, 2, rows)
    mine = lax.dynamic_index_in_dim(by_core, core, 2, keepdims=False)
    other = lax.dynamic_index_in_dim(by_core, 1 - core, 2, keepdims=False)
    acts = jnp.concatenate([mine, swapped(other)], 0)
    cots = jnp.concatenate([cotangent, swapped(cotangent)], 0)
    weight = lax.all_gather(kv_weight, ("blk", "chip"), axis=0, tiled=False)
    weight = weight.reshape(blocks, chips, rows, cols)
    parts = jnp.einsum(
        "tzr,tbc->bzrc", acts, cots.reshape(2 * tokens, blocks, cols), preferred_element_type=F32
    ).astype(BF16).reshape(blocks * chips, rows, cols)
    total = lax.psum_scatter(parts, ("blk", "chip"), scatter_dimension=0, tiled=False)
    count = tokens * blocks * chips * 2
    grad_weight = (total.astype(F32) * (1.0 / math.sqrt(count))).astype(BF16)
    full = weight.transpose(1, 2, 0, 3).reshape(chips * rows, columns)
    keys = jnp.dot(acts.reshape(2 * tokens, chips * rows), full, preferred_element_type=F32)
    key_values = (keys[:tokens] + swapped(keys[tokens:])).astype(BF16)
    inputs = lax.dot_general(
        cots, full, (((1,), (1,)), ((), ())), preferred_element_type=F32
    ).astype(BF16).reshape(2 * tokens, chips, rows)
    near, far = inputs[:tokens], swapped(inputs[tokens:])
    low = jnp.where(core == 0, near, far)
    high = jnp.where(core == 0, far, near)
    grad_input = jnp.stack([low, high], 2).reshape(tokens, features)
    return (key_values, grad_input, grad_weight)


def solution(mesh):
    blocks, shards = mesh.shape["blk"], mesh.shape["shard"]
    split = Mesh(mesh.devices.reshape(blocks, shards // 2, 2), AXES)
    by_token = P(AXES, None)
    by_piece = P(("chip", "core"), "blk")
    return jax.shard_map(
        by_hops if (blocks, shards) == (4, 8) else by_collectives,
        mesh=split,
        in_specs=(by_token, by_token, by_piece),
        out_specs=(by_token, by_token, by_piece),
        check_vma=False,
    )
```

```python
import math

import jax
import jax.numpy as jnp
from jax import lax
from jax.experimental import pallas as pl
from jax.experimental.pallas import tpu as pltpu
from jax.sharding import Mesh, PartitionSpec as P

F32, BF16 = jnp.float32, jnp.bfloat16
AXES = ("blk", "chip", "core")
SHRINK = 1000
MIB = 2**20
GATE = 10**7
ONCE = pl.Buffered(1)


def hops(move):
    pairs = []
    for blk in range(4):
        for z in range(4):
            for core in range(2):
                to = move(blk, z, core)
                if to is not None:
                    pairs.append(((blk * 4 + z) * 2 + core, (to[0] * 4 + to[1]) * 2 + to[2]))
    return pairs


def middle(z):
    return z in (1, 2)


SWAP = hops(lambda b, z, c: (b, z, 1 - c))
FLIP_A = hops(lambda b, z, c: (b ^ (1 + c), z, c))
FLIP_B = hops(lambda b, z, c: (b ^ (2 - c), z, c))
PAIR = hops(lambda b, z, c: (b, z ^ 1, c))
MID = hops(lambda b, z, c: (b, z ^ 3, c) if middle(z) else None)
OUT = hops(lambda b, z, c: (b, z ^ 1, c) if middle(z) else None)
IN = hops(lambda b, z, c: (b, z ^ 1, c) if not middle(z) else None)


def after(array, *others):
    return lax.optimization_barrier((array, *others))[0]


def sent(array, pairs):
    return lax.ppermute(array, AXES, pairs)


def column_block(place, a, b):
    core = place[1]
    return place[2] ^ (a * (1 + core)) ^ (b * (2 - core))


def cost(flops, moved, shrink=SHRINK):
    return pl.CostEstimate(flops=flops // shrink, bytes_accessed=moved // shrink, transcendentals=0)


def gate(place, *arrays):
    def kernel(*refs):
        for i in range(3):
            refs[-1][i] = refs[0][i]

    return pl.pallas_call(
        kernel,
        in_specs=[pl.BlockSpec(memory_space=pltpu.SMEM)]
        + [pl.BlockSpec(memory_space=pl.ANY)] * len(arrays),
        out_specs=pl.BlockSpec(memory_space=pltpu.SMEM),
        out_shape=jax.ShapeDtypeStruct(place.shape, place.dtype),
        compiler_params=pltpu.CompilerParams(vmem_limit_bytes=MIB),
        cost_estimate=cost(0, GATE, 1),
        name="gate",
    )(place, *arrays)


def pack_kernel(place, acts, out):
    out[...] = acts[...]


def packed(place, activations, rows):
    tokens = activations.shape[0]
    return pl.pallas_call(
        pack_kernel,
        grid_spec=pltpu.PrefetchScalarGridSpec(
            num_scalar_prefetch=1,
            grid=(1,),
            in_specs=[pl.BlockSpec((tokens, rows), lambda r, s: (0, 2 * (s[0] ^ 3) + 1 - s[1]))],
            out_specs=pl.BlockSpec((tokens, rows), lambda r, s: (0, 0)),
        ),
        out_shape=jax.ShapeDtypeStruct((tokens, rows), BF16),
        compiler_params=pltpu.CompilerParams(vmem_limit_bytes=6 * MIB),
        cost_estimate=cost(0, 4 * tokens * rows),
        name="pack",
    )(place, activations)


def first_term_kernel(place, mine, other, cot_mine, cot_other, keep, send, cots, turned):
    tokens, cols = cot_mine.shape[0], cot_mine.shape[1] // 4

    @pl.when(pl.program_id(0) == 0)
    def _():
        for b in (0, 1):
            for a in (0, 1):
                at = pl.ds(pl.multiple_of(column_block(place, a, b) * cols, cols), cols)
                to = slice((2 * b + a) * cols, (2 * b + a + 1) * cols)
                for array, half in ((cot_mine, slice(0, tokens)), (cot_other, slice(tokens, None))):
                    piece = array[:, at]
                    cots[half, to] = piece
                    turned[to, half] = piece.T

    tall = jnp.concatenate([mine[...], other[...]], 0)
    for b, out in ((1, send), (0, keep)):
        part = turned[2 * b * cols : (2 * b + 2) * cols]
        out[...] = jnp.dot(part, tall, preferred_element_type=F32).astype(BF16).reshape(out.shape)


def first_terms(place, activations, other, cot_mine, cot_other, rows):
    tokens, columns = cot_mine.shape
    part, cols = rows // 2, columns // 4
    mine = pl.BlockSpec((tokens, part), lambda r, s: (0, 2 * (2 * (s[0] ^ 3) + s[1]) + r))
    piece = pl.BlockSpec((2, cols, part), lambda r, s: (0, 0, r))

    held = pl.BlockSpec((tokens, columns), lambda r, s: (0, 0), pipeline_mode=ONCE)

    def whole(*shape):
        return pl.BlockSpec(shape, lambda r, s: (0, 0))

    return pl.pallas_call(
        first_term_kernel,
        grid_spec=pltpu.PrefetchScalarGridSpec(
            num_scalar_prefetch=1,
            grid=(2,),
            in_specs=[mine, pl.BlockSpec((tokens, part), lambda r, s: (0, r)), held, held],
            out_specs=[piece, piece, whole(2 * tokens, columns), whole(columns, 2 * tokens)],
        ),
        out_shape=[jax.ShapeDtypeStruct((2, cols, rows), BF16)] * 2
        + [
            jax.ShapeDtypeStruct((2 * tokens, columns), BF16),
            jax.ShapeDtypeStruct((columns, 2 * tokens), BF16),
        ],
        compiler_params=pltpu.CompilerParams(vmem_limit_bytes=22 * MIB),
        cost_estimate=cost(4 * tokens * rows * columns, 4 * tokens * rows + 4 * rows * columns),
        name="terms",
    )(place, activations, other, cot_mine, cot_other)


def term_kernel(place, mine, other, turned, *outs):
    rows = turned.shape[0] // 2
    for i in range(3):

        @pl.when(pl.program_id(0) == i)
        def _():
            tall = jnp.concatenate([mine[...], other[...]], 0)
            for b in (1, 0):
                out = outs[3 * b + i]
                part = turned[b * rows : (b + 1) * rows]
                out[...] = (
                    jnp.dot(part, tall, preferred_element_type=F32).astype(BF16).reshape(out.shape)
                )


def terms(place, activations, other, turned, rows):
    columns, tokens = turned.shape[0], activations.shape[0]
    part, cols = rows // 2, columns // 4
    mine = pl.BlockSpec((tokens, part), lambda i, r, s: (0, 2 * (2 * (s[0] ^ (2 - i)) + s[1]) + r))
    pieces = [
        pl.BlockSpec((2, cols, part), lambda i, r, s, n=n: (0, 0, jnp.clip(2 * (i - n) + r, 0, 1)))
        for n in range(3)
    ]
    return pl.pallas_call(
        term_kernel,
        grid_spec=pltpu.PrefetchScalarGridSpec(
            num_scalar_prefetch=1,
            grid=(3, 2),
            in_specs=[
                mine,
                mine,
                pl.BlockSpec(turned.shape, lambda i, r, s: (0, 0), pipeline_mode=ONCE),
            ],
            out_specs=pieces * 2,
        ),
        out_shape=[jax.ShapeDtypeStruct((2, cols, rows), BF16)] * 6,
        compiler_params=pltpu.CompilerParams(vmem_limit_bytes=18 * MIB),
        cost_estimate=cost(12 * tokens * rows * columns, 12 * tokens * rows + 12 * rows * columns),
        name="terms",
    )(place, activations, other, turned)


def project_kernel(place, acts, other, cots, here, there, *refs, first, last):
    near, far, *keys = refs[0 if first else 2 : -1]
    acc = refs[-1]
    tokens, cols = acts.shape[0], here.shape[2]
    step = pl.program_id(0)

    weight = jnp.concatenate([here[0], here[1], there[0], there[1]], 1)
    total = lax.dot_general(
        cots[...], weight, (((1,), (1,)), ((), ())), preferred_element_type=F32
    ).astype(BF16)
    near[...] = total[:tokens]
    far[...] = total[tokens:]
    tall = jnp.concatenate([acts[...], other[...]], 0)
    sums = jnp.dot(tall, weight, preferred_element_type=F32)

    @pl.when(step == 0)
    def _():
        acc[...] = sums if first else refs[0][...] + sums

    @pl.when(step == 1)
    def _():
        if last:
            for b in (0, 1):
                for a in (0, 1):
                    at = pl.ds(pl.multiple_of(column_block(place, a, b) * cols, cols), cols)
                    to = slice((2 * b + a) * cols, (2 * b + a + 1) * cols)
                    keys[0][:, at] = acc[:tokens, to] + sums[:tokens, to]
                    keys[1][:, at] = acc[tokens:, to] + sums[tokens:, to]
        else:
            keys[0][...] = acc[...] + sums


def projected(place, k, activations, other, cots, here, there, so_far=None):
    tokens, columns = activations.shape[0], cots.shape[1]
    _, rows, cols = here.shape
    part = rows // 2
    first, last = k == 0, k == 3

    def whole(*shape):
        return pl.BlockSpec(shape, lambda r, s: (0, 0))

    held = pl.BlockSpec((2 * tokens, columns), lambda r, s: (0, 0), pipeline_mode=ONCE)

    mine = pl.BlockSpec(
        (tokens, part), lambda r, s: (0, 2 * (2 * (s[0] ^ k) + s[1]) + r)
    )
    piece = pl.BlockSpec((2, part, cols), lambda r, s: (0, r, 0))
    one = jax.ShapeDtypeStruct((tokens, columns), F32)
    return pl.pallas_call(
        lambda *refs: project_kernel(*refs, first=first, last=last),
        grid_spec=pltpu.PrefetchScalarGridSpec(
            num_scalar_prefetch=1,
            grid=(2,),
            in_specs=[mine, mine, held, piece, piece]
            + ([] if first else [held, pl.BlockSpec(memory_space=pl.ANY)]),
            out_specs=[mine, pl.BlockSpec((tokens, part), lambda r, s: (0, r))]
            + ([whole(tokens, columns)] * 2 if last else [whole(2 * tokens, columns)]),
            scratch_shapes=[pltpu.VMEM((2 * tokens, columns), F32)],
        ),
        out_shape=[
            jax.ShapeDtypeStruct(activations.shape, BF16),
            jax.ShapeDtypeStruct((tokens, rows), BF16),
        ]
        + ([one, one] if last else [jax.ShapeDtypeStruct((2 * tokens, columns), F32)]),
        input_output_aliases={} if first else {7: 0},
        compiler_params=pltpu.CompilerParams(vmem_limit_bytes=28 * MIB),
        cost_estimate=cost(
            8 * tokens * rows * columns,
            8 * tokens * rows + 2 * rows * columns + 8 * tokens * columns,
        ),
        name="project",
    )(
        place, activations, other, cots, here, there,
        *([] if first else [so_far[2], so_far[0]]),
    )


def lay_kernel(place, *refs):
    for k in range(3):

        @pl.when(pl.program_id(0) == k)
        def _():
            refs[-1][...] = refs[k][...]


def laid(place, whole, parts):
    tokens, rows = parts[0].shape
    return pl.pallas_call(
        lay_kernel,
        grid_spec=pltpu.PrefetchScalarGridSpec(
            num_scalar_prefetch=1,
            grid=(3,),
            in_specs=[pl.BlockSpec((tokens, rows), lambda i, s: (0, 0), pipeline_mode=ONCE)] * 3
            + [pl.BlockSpec(memory_space=pl.ANY)],
            out_specs=pl.BlockSpec((tokens, rows), lambda i, s: (0, 2 * (s[0] ^ i) + 1 - s[1])),
        ),
        out_shape=jax.ShapeDtypeStruct(whole.shape, BF16),
        input_output_aliases={4: 0},
        compiler_params=pltpu.CompilerParams(vmem_limit_bytes=8 * MIB),
        cost_estimate=cost(0, 12 * tokens * rows),
        name="lay",
    )(place, *parts, whole)


def finish_kernel(place, got, near, far, last, arrived, whole, out, keys, weight, *, scale):
    out[...] = got[...]
    keys[...] = (near[...] + far[...]).astype(BF16)
    weight[...] = ((last[...] + arrived[...].astype(F32)) * scale).T.astype(BF16)


def finished(place, whole, got, keys_near, keys_far, last, arrived, scale):
    tokens, rows = got.shape
    cols, columns = last.shape[0], keys_near.shape[1]
    part, some = rows // 2, columns // 2
    wide = pl.BlockSpec((tokens, some), lambda r, s: (0, r))
    flat = pl.BlockSpec((cols, part), lambda r, s: (0, r))
    return pl.pallas_call(
        lambda *refs: finish_kernel(*refs, scale=scale),
        grid_spec=pltpu.PrefetchScalarGridSpec(
            num_scalar_prefetch=1,
            grid=(2,),
            in_specs=[
                pl.BlockSpec((tokens, part), lambda r, s: (0, r)),
                wide,
                wide,
                flat,
                flat,
                pl.BlockSpec(memory_space=pl.ANY),
            ],
            out_specs=[
                pl.BlockSpec((tokens, part), lambda r, s: (0, 2 * (2 * (s[0] ^ 3) + 1 - s[1]) + r)),
                wide,
                pl.BlockSpec((part, cols), lambda r, s: (r, 0)),
            ],
        ),
        out_shape=[
            jax.ShapeDtypeStruct(whole.shape, BF16),
            jax.ShapeDtypeStruct((tokens, columns), BF16),
            jax.ShapeDtypeStruct((rows, cols), BF16),
        ],
        input_output_aliases={6: 0},
        compiler_params=pltpu.CompilerParams(vmem_limit_bytes=12 * MIB),
        cost_estimate=cost(0, 4 * tokens * rows + 10 * tokens * columns),
        name="finish",
    )(place, got, keys_near, keys_far, last, arrived, whole)


def added(*arrays):
    total = arrays[0].astype(F32)
    for array in arrays[1:]:
        total = total + array.astype(F32)
    return total.astype(BF16)


def by_hops(activations, cotangent, kv_weight):
    rows = kv_weight.shape[0]
    tokens = activations.shape[0]
    place = jnp.stack([lax.axis_index(name) for name in ("chip", "core", "blk")]).astype(jnp.int32)

    other3 = sent(packed(place, activations, rows), SWAP)
    other, cot_other = sent(after(activations, other3), SWAP), sent(cotangent, SWAP)
    next_a = sent(kv_weight, FLIP_A)
    base = jnp.stack([kv_weight, next_a])
    one_near, mid_near = sent(kv_weight, PAIR), sent(kv_weight, MID)

    keep3, send3, cots, turned = first_terms(
        place, activations, other3, cotangent, cot_other, rows
    )
    got3 = sent(send3, FLIP_B)
    next_a = after(next_a, one_near, mid_near, keep3)
    keep2, keep1, keep0, send2, send1, send0 = terms(place, activations, other, turned, rows)
    one = jnp.stack([after(one_near, keep0), sent(next_a, PAIR)])
    mid = jnp.stack([after(mid_near, keep0), sent(next_a, MID)])
    base_b = sent(base, FLIP_B)
    first = gate(place, got3, after(one, keep0), mid, base_b)

    sum3 = added(after(keep3, first), got3)
    far = sent(sum3, IN)
    two_mid = sent(after(one, first, sum3), MID)
    two_end = sent(after(mid, sum3), OUT)
    got2 = sent(send2, FLIP_B)
    sum2 = added(keep2, got2)
    one_b = sent(after(one, sum3), FLIP_B)
    got1 = sent(after(send1, sum2), FLIP_B)
    whole, out0, keys = projected(
        first, 0, after(activations, keep0, sum3, sum2), other, cots, base, base_b
    )

    sum2_far = added(after(sum2, out0), far)
    mid_far = sent(sum2_far, MID)
    near = sent(after(sum2, sum2_far, two_mid, two_end, one_b), IN)
    three_end = sent(after(two_mid, sum2_far), OUT)
    two = after(two_mid, sum2_far) + two_end
    two_b = sent(two, FLIP_B)
    sum1 = added(keep1, got1)
    got0 = sent(after(send0, sum1), FLIP_B)
    whole, out1, keys = projected(
        place, 1, after(activations, sum2_far, sum1), other, cots, one, one_b, (whole, None, keys)
    )

    sum3_near = added(after(sum3, out1), near)
    sum_mid = sent(sum3_near, MID)
    sum1_far = added(after(sum1, sum3_near, out1), mid_far)
    sum_one = sent(after(sum1_far, three_end, two_b), PAIR)
    three = after(mid, sum1_far) + three_end
    three_b = sent(three, FLIP_B)
    sum0 = added(keep0, got0)
    whole, out2, keys = projected(
        place,
        2,
        after(activations, sum1_far, sum0),
        other,
        cots,
        two,
        two_b,
        (whole, None, keys),
    )
    whole, out3, keys, keys_far = projected(
        place, 3, after(activations, out2), other, cots, three, three_b, (whole, None, keys)
    )
    sum_one = after(sum_one, out3)
    last = [
        sum0[a].astype(F32) + sum_mid[a].astype(F32) + sum_one[a].astype(F32) for a in (0, 1)
    ]
    over = last[1].astype(BF16)
    whole = laid(
        place,
        whole,
        (sent(out0, SWAP), sent(out1, SWAP), sent(out2, SWAP)),
    )
    grad_input, key_values, grad_weight = finished(
        place,
        whole,
        sent(out3, SWAP),
        keys,
        sent(keys_far, SWAP),
        last[0],
        sent(over, FLIP_A),
        1.0 / math.sqrt(32 * tokens),
    )
    return (key_values, grad_input, grad_weight)


def swapped(array):
    return lax.ppermute(array, "core", [(0, 1), (1, 0)])


def by_collectives(activations, cotangent, kv_weight):
    blocks, chips = lax.axis_size("blk"), lax.axis_size("chip")
    core = lax.axis_index("core")
    tokens, features = activations.shape
    rows, cols = kv_weight.shape
    columns = cotangent.shape[1]
    by_core = activations.reshape(tokens, chips, 2, rows)
    mine = lax.dynamic_index_in_dim(by_core, core, 2, keepdims=False)
    other = lax.dynamic_index_in_dim(by_core, 1 - core, 2, keepdims=False)
    acts = jnp.concatenate([mine, swapped(other)], 0)
    cots = jnp.concatenate([cotangent, swapped(cotangent)], 0)
    weight = lax.all_gather(kv_weight, ("blk", "chip"), axis=0, tiled=False)
    weight = weight.reshape(blocks, chips, rows, cols)
    parts = jnp.einsum(
        "tzr,tbc->bzrc", acts, cots.reshape(2 * tokens, blocks, cols), preferred_element_type=F32
    ).astype(BF16).reshape(blocks * chips, rows, cols)
    total = lax.psum_scatter(parts, ("blk", "chip"), scatter_dimension=0, tiled=False)
    count = tokens * blocks * chips * 2
    grad_weight = (total.astype(F32) * (1.0 / math.sqrt(count))).astype(BF16)
    full = weight.transpose(1, 2, 0, 3).reshape(chips * rows, columns)
    keys = jnp.dot(acts.reshape(2 * tokens, chips * rows), full, preferred_element_type=F32)
    key_values = (keys[:tokens] + swapped(keys[tokens:])).astype(BF16)
    inputs = lax.dot_general(
        cots, full, (((1,), (1,)), ((), ())), preferred_element_type=F32
    ).astype(BF16).reshape(2 * tokens, chips, rows)
    near, far = inputs[:tokens], swapped(inputs[tokens:])
    low = jnp.where(core == 0, near, far)
    high = jnp.where(core == 0, far, near)
    grad_input = jnp.stack([low, high], 2).reshape(tokens, features)
    return (key_values, grad_input, grad_weight)


def solution(mesh):
    blocks, shards = mesh.shape["blk"], mesh.shape["shard"]
    split = Mesh(mesh.devices.reshape(blocks, shards // 2, 2), AXES)
    by_token = P(AXES, None)
    by_piece = P(("chip", "core"), "blk")
    return jax.shard_map(
        by_hops if (blocks, shards) == (4, 8) else by_collectives,
        mesh=split,
        in_specs=(by_token, by_token, by_piece),
        out_specs=(by_token, by_token, by_piece),
        check_vma=False,
    )
```

```python
import math

import jax
import jax.numpy as jnp
from jax import lax
from jax.experimental import pallas as pl
from jax.experimental.pallas import tpu as pltpu
from jax.sharding import Mesh, PartitionSpec as P

F32, BF16 = jnp.float32, jnp.bfloat16
AXES = ("blk", "chip", "core")
SHRINK = 1000
MIB = 2**20
GATE = 10**7
ONCE = pl.Buffered(1)


def hops(move):
    pairs = []
    for blk in range(4):
        for z in range(4):
            for core in range(2):
                to = move(blk, z, core)
                if to is not None:
                    pairs.append(((blk * 4 + z) * 2 + core, (to[0] * 4 + to[1]) * 2 + to[2]))
    return pairs


def middle(z):
    return z in (1, 2)


SWAP = hops(lambda b, z, c: (b, z, 1 - c))
FLIP_A = hops(lambda b, z, c: (b ^ (1 + c), z, c))
FLIP_B = hops(lambda b, z, c: (b ^ (2 - c), z, c))
PAIR = hops(lambda b, z, c: (b, z ^ 1, c))
MID = hops(lambda b, z, c: (b, z ^ 3, c) if middle(z) else None)
OUT = hops(lambda b, z, c: (b, z ^ 1, c) if middle(z) else None)
IN = hops(lambda b, z, c: (b, z ^ 1, c) if not middle(z) else None)


def after(array, *others):
    return lax.optimization_barrier((array, *others))[0]


def sent(array, pairs):
    return lax.ppermute(array, AXES, pairs)


def column_block(place, a, b):
    core = place[1]
    return place[2] ^ (a * (1 + core)) ^ (b * (2 - core))


def cost(flops, moved, shrink=SHRINK):
    return pl.CostEstimate(flops=flops // shrink, bytes_accessed=moved // shrink, transcendentals=0)


def gate(place, *arrays):
    def kernel(*refs):
        for i in range(3):
            refs[-1][i] = refs[0][i]

    return pl.pallas_call(
        kernel,
        in_specs=[pl.BlockSpec(memory_space=pltpu.SMEM)]
        + [pl.BlockSpec(memory_space=pl.ANY)] * len(arrays),
        out_specs=pl.BlockSpec(memory_space=pltpu.SMEM),
        out_shape=jax.ShapeDtypeStruct(place.shape, place.dtype),
        compiler_params=pltpu.CompilerParams(vmem_limit_bytes=MIB),
        cost_estimate=cost(0, GATE, 1),
        name="gate",
    )(place, *arrays)


def first_term_kernel(place, mine, other, cot_mine, cot_other, keep, send, cots, turned):
    tokens, cols = cot_mine.shape[0], cot_mine.shape[1] // 4

    @pl.when(pl.program_id(0) == 0)
    def _():
        for b in (0, 1):
            for a in (0, 1):
                at = pl.ds(pl.multiple_of(column_block(place, a, b) * cols, cols), cols)
                to = slice((2 * b + a) * cols, (2 * b + a + 1) * cols)
                for array, half in ((cot_mine, slice(0, tokens)), (cot_other, slice(tokens, None))):
                    piece = array[:, at]
                    cots[half, to] = piece
                    turned[to, half] = piece.T

    tall = jnp.concatenate([mine[...], other[...]], 0)
    for b, out in ((1, send), (0, keep)):
        part = turned[2 * b * cols : (2 * b + 2) * cols]
        out[...] = jnp.dot(part, tall, preferred_element_type=F32).astype(BF16).reshape(out.shape)


def first_terms(place, activations, other, cot_mine, cot_other, rows):
    tokens, columns = cot_mine.shape
    part, cols = rows // 2, columns // 4
    mine = pl.BlockSpec((tokens, part), lambda r, s: (0, 2 * (2 * (s[0] ^ 3) + s[1]) + r))
    piece = pl.BlockSpec((2, cols, part), lambda r, s: (0, 0, r))

    held = pl.BlockSpec((tokens, columns), lambda r, s: (0, 0), pipeline_mode=ONCE)

    def whole(*shape):
        return pl.BlockSpec(shape, lambda r, s: (0, 0))

    return pl.pallas_call(
        first_term_kernel,
        grid_spec=pltpu.PrefetchScalarGridSpec(
            num_scalar_prefetch=1,
            grid=(2,),
            in_specs=[mine, mine, held, held],
            out_specs=[piece, piece, whole(2 * tokens, columns), whole(columns, 2 * tokens)],
        ),
        out_shape=[jax.ShapeDtypeStruct((2, cols, rows), BF16)] * 2
        + [
            jax.ShapeDtypeStruct((2 * tokens, columns), BF16),
            jax.ShapeDtypeStruct((columns, 2 * tokens), BF16),
        ],
        compiler_params=pltpu.CompilerParams(vmem_limit_bytes=22 * MIB),
        cost_estimate=cost(4 * tokens * rows * columns, 4 * tokens * rows + 4 * rows * columns),
        name="terms",
    )(place, activations, other, cot_mine, cot_other)


def term_kernel(place, mine, other, turned, *outs):
    rows = turned.shape[0] // 2
    for i in range(3):

        @pl.when(pl.program_id(0) == i)
        def _():
            tall = jnp.concatenate([mine[...], other[...]], 0)
            for b in (1, 0):
                out = outs[3 * b + i]
                part = turned[b * rows : (b + 1) * rows]
                out[...] = (
                    jnp.dot(part, tall, preferred_element_type=F32).astype(BF16).reshape(out.shape)
                )


def terms(place, activations, other, turned, rows):
    columns, tokens = turned.shape[0], activations.shape[0]
    part, cols = rows // 2, columns // 4
    mine = pl.BlockSpec((tokens, part), lambda i, r, s: (0, 2 * (2 * (s[0] ^ (2 - i)) + s[1]) + r))
    pieces = [
        pl.BlockSpec((2, cols, part), lambda i, r, s, n=n: (0, 0, jnp.clip(2 * (i - n) + r, 0, 1)))
        for n in range(3)
    ]
    return pl.pallas_call(
        term_kernel,
        grid_spec=pltpu.PrefetchScalarGridSpec(
            num_scalar_prefetch=1,
            grid=(3, 2),
            in_specs=[
                mine,
                mine,
                pl.BlockSpec(turned.shape, lambda i, r, s: (0, 0), pipeline_mode=ONCE),
            ],
            out_specs=pieces * 2,
        ),
        out_shape=[jax.ShapeDtypeStruct((2, cols, rows), BF16)] * 6,
        compiler_params=pltpu.CompilerParams(vmem_limit_bytes=18 * MIB),
        cost_estimate=cost(12 * tokens * rows * columns, 12 * tokens * rows + 12 * rows * columns),
        name="terms",
    )(place, activations, other, turned)


def project_kernel(place, acts, other, cots, here, there, *refs, first, last):
    near, far, *keys = refs[0 if first else 2 : -1]
    acc = refs[-1]
    tokens, cols = acts.shape[0], here.shape[2]
    step = pl.program_id(0)

    weight = jnp.concatenate([here[0], here[1], there[0], there[1]], 1)
    total = lax.dot_general(
        cots[...], weight, (((1,), (1,)), ((), ())), preferred_element_type=F32
    ).astype(BF16)
    near[...] = total[:tokens]
    far[...] = total[tokens:]
    tall = jnp.concatenate([acts[...], other[...]], 0)
    sums = jnp.dot(tall, weight, preferred_element_type=F32)

    @pl.when(step == 0)
    def _():
        acc[...] = sums if first else refs[0][...] + sums

    @pl.when(step == 1)
    def _():
        if last:
            for b in (0, 1):
                for a in (0, 1):
                    at = pl.ds(pl.multiple_of(column_block(place, a, b) * cols, cols), cols)
                    to = slice((2 * b + a) * cols, (2 * b + a + 1) * cols)
                    keys[0][:, at] = acc[:tokens, to] + sums[:tokens, to]
                    keys[1][:, at] = acc[tokens:, to] + sums[tokens:, to]
        else:
            keys[0][...] = acc[...] + sums


def projected(place, k, activations, other, cots, here, there, so_far=None):
    tokens, columns = activations.shape[0], cots.shape[1]
    _, rows, cols = here.shape
    part = rows // 2
    first, last = k == 0, k == 3

    def whole(*shape):
        return pl.BlockSpec(shape, lambda r, s: (0, 0))

    held = pl.BlockSpec((2 * tokens, columns), lambda r, s: (0, 0), pipeline_mode=ONCE)

    mine = pl.BlockSpec(
        (tokens, part), lambda r, s: (0, 2 * (2 * (s[0] ^ k) + s[1]) + r)
    )
    piece = pl.BlockSpec((2, part, cols), lambda r, s: (0, r, 0))
    one = jax.ShapeDtypeStruct((tokens, columns), F32)
    return pl.pallas_call(
        lambda *refs: project_kernel(*refs, first=first, last=last),
        grid_spec=pltpu.PrefetchScalarGridSpec(
            num_scalar_prefetch=1,
            grid=(2,),
            in_specs=[mine, mine, held, piece, piece]
            + ([] if first else [held, pl.BlockSpec(memory_space=pl.ANY)]),
            out_specs=[mine, pl.BlockSpec((tokens, part), lambda r, s: (0, r))]
            + ([whole(tokens, columns)] * 2 if last else [whole(2 * tokens, columns)]),
            scratch_shapes=[pltpu.VMEM((2 * tokens, columns), F32)],
        ),
        out_shape=[
            jax.ShapeDtypeStruct(activations.shape, BF16),
            jax.ShapeDtypeStruct((tokens, rows), BF16),
        ]
        + ([one, one] if last else [jax.ShapeDtypeStruct((2 * tokens, columns), F32)]),
        input_output_aliases={} if first else {7: 0},
        compiler_params=pltpu.CompilerParams(vmem_limit_bytes=28 * MIB),
        cost_estimate=cost(
            8 * tokens * rows * columns,
            8 * tokens * rows + 2 * rows * columns + 8 * tokens * columns,
        ),
        name="project",
    )(
        place, activations, other, cots, here, there,
        *([] if first else [so_far[2], so_far[0]]),
    )


def lay_kernel(place, *refs):
    for k in range(3):

        @pl.when(pl.program_id(0) == k)
        def _():
            refs[-1][...] = refs[k][...]


def laid(place, whole, parts):
    tokens, rows = parts[0].shape
    return pl.pallas_call(
        lay_kernel,
        grid_spec=pltpu.PrefetchScalarGridSpec(
            num_scalar_prefetch=1,
            grid=(3,),
            in_specs=[pl.BlockSpec((tokens, rows), lambda i, s: (0, 0), pipeline_mode=ONCE)] * 3
            + [pl.BlockSpec(memory_space=pl.ANY)],
            out_specs=pl.BlockSpec((tokens, rows), lambda i, s: (0, 2 * (s[0] ^ i) + 1 - s[1])),
        ),
        out_shape=jax.ShapeDtypeStruct(whole.shape, BF16),
        input_output_aliases={4: 0},
        compiler_params=pltpu.CompilerParams(vmem_limit_bytes=8 * MIB),
        cost_estimate=cost(0, 12 * tokens * rows),
        name="lay",
    )(place, *parts, whole)


def finish_kernel(place, got, near, far, last, arrived, whole, out, keys, weight, *, scale):
    out[...] = got[...]
    keys[...] = (near[...] + far[...]).astype(BF16)
    weight[...] = ((last[...] + arrived[...].astype(F32)) * scale).T.astype(BF16)


def finished(place, whole, got, keys_near, keys_far, last, arrived, scale):
    tokens, rows = got.shape
    cols, columns = last.shape[0], keys_near.shape[1]
    part, some = rows // 2, columns // 2
    wide = pl.BlockSpec((tokens, some), lambda r, s: (0, r))
    flat = pl.BlockSpec((cols, part), lambda r, s: (0, r))
    return pl.pallas_call(
        lambda *refs: finish_kernel(*refs, scale=scale),
        grid_spec=pltpu.PrefetchScalarGridSpec(
            num_scalar_prefetch=1,
            grid=(2,),
            in_specs=[
                pl.BlockSpec((tokens, part), lambda r, s: (0, r)),
                wide,
                wide,
                flat,
                flat,
                pl.BlockSpec(memory_space=pl.ANY),
            ],
            out_specs=[
                pl.BlockSpec((tokens, part), lambda r, s: (0, 2 * (2 * (s[0] ^ 3) + 1 - s[1]) + r)),
                wide,
                pl.BlockSpec((part, cols), lambda r, s: (r, 0)),
            ],
        ),
        out_shape=[
            jax.ShapeDtypeStruct(whole.shape, BF16),
            jax.ShapeDtypeStruct((tokens, columns), BF16),
            jax.ShapeDtypeStruct((rows, cols), BF16),
        ],
        input_output_aliases={6: 0},
        compiler_params=pltpu.CompilerParams(vmem_limit_bytes=12 * MIB),
        cost_estimate=cost(0, 4 * tokens * rows + 10 * tokens * columns),
        name="finish",
    )(place, got, keys_near, keys_far, last, arrived, whole)


def added(*arrays):
    total = arrays[0].astype(F32)
    for array in arrays[1:]:
        total = total + array.astype(F32)
    return total.astype(BF16)


def by_hops(activations, cotangent, kv_weight):
    rows = kv_weight.shape[0]
    tokens = activations.shape[0]
    place = jnp.stack([lax.axis_index(name) for name in ("chip", "core", "blk")]).astype(jnp.int32)

    other, cot_other = sent(activations, SWAP), sent(cotangent, SWAP)
    base = jnp.stack([kv_weight, sent(kv_weight, FLIP_A)])
    one, mid = sent(base, PAIR), sent(base, MID)
    base_b = sent(base, FLIP_B)

    keep3, send3, cots, turned = first_terms(
        place, activations, other, cotangent, cot_other, rows
    )
    got3 = sent(send3, FLIP_B)
    keep2, keep1, keep0, send2, send1, send0 = terms(place, activations, other, turned, rows)
    first = gate(place, after(one, keep0), mid, base_b)

    sum3 = added(after(keep3, first), got3)
    far = sent(sum3, IN)
    two_mid = sent(after(one, first, sum3), MID)
    two_end = sent(after(mid, sum3), OUT)
    got2 = sent(send2, FLIP_B)
    sum2 = added(keep2, got2)
    one_b = sent(after(one, sum3), FLIP_B)
    got1 = sent(after(send1, sum2), FLIP_B)
    whole, out0, keys = projected(
        first, 0, after(activations, keep0, sum3, sum2), other, cots, base, base_b
    )

    sum2_far = added(after(sum2, out0), far)
    mid_far = sent(sum2_far, MID)
    near = sent(after(sum2, sum2_far, two_mid, two_end, one_b), IN)
    three_end = sent(after(two_mid, sum2_far), OUT)
    two = after(two_mid, sum2_far) + two_end
    two_b = sent(two, FLIP_B)
    sum1 = added(keep1, got1)
    got0 = sent(after(send0, sum1), FLIP_B)
    whole, out1, keys = projected(
        place, 1, after(activations, sum2_far, sum1), other, cots, one, one_b, (whole, None, keys)
    )

    sum3_near = added(sum3, near)
    sum_mid = sent(sum3_near, MID)
    sum1_far = added(after(sum1, sum3_near, out1), mid_far)
    sum_one = sent(after(sum1_far, three_end, two_b), PAIR)
    three = after(mid, sum1_far) + three_end
    three_b = sent(three, FLIP_B)
    sum0 = added(keep0, got0)
    whole, out2, keys = projected(
        place,
        2,
        after(activations, sum1_far, sum0),
        other,
        cots,
        two,
        two_b,
        (whole, None, keys),
    )
    got_out0 = sent(out0, SWAP)
    whole, out3, keys, keys_far = projected(
        place, 3, after(activations, out2, got_out0), other, cots, three, three_b, (whole, None, keys)
    )
    sum_one = after(sum_one, out3)
    last = [
        sum0[a].astype(F32) + sum_mid[a].astype(F32) + sum_one[a].astype(F32) for a in (0, 1)
    ]
    over = last[1].astype(BF16)
    whole = laid(
        place,
        whole,
        (got_out0, sent(out1, SWAP), sent(out2, SWAP)),
    )
    grad_input, key_values, grad_weight = finished(
        place,
        whole,
        sent(out3, SWAP),
        keys,
        sent(keys_far, SWAP),
        last[0],
        sent(over, FLIP_A),
        1.0 / math.sqrt(32 * tokens),
    )
    return (key_values, grad_input, grad_weight)


def swapped(array):
    return lax.ppermute(array, "core", [(0, 1), (1, 0)])


def by_collectives(activations, cotangent, kv_weight):
    blocks, chips = lax.axis_size("blk"), lax.axis_size("chip")
    core = lax.axis_index("core")
    tokens, features = activations.shape
    rows, cols = kv_weight.shape
    columns = cotangent.shape[1]
    by_core = activations.reshape(tokens, chips, 2, rows)
    mine = lax.dynamic_index_in_dim(by_core, core, 2, keepdims=False)
    other = lax.dynamic_index_in_dim(by_core, 1 - core, 2, keepdims=False)
    acts = jnp.concatenate([mine, swapped(other)], 0)
    cots = jnp.concatenate([cotangent, swapped(cotangent)], 0)
    weight = lax.all_gather(kv_weight, ("blk", "chip"), axis=0, tiled=False)
    weight = weight.reshape(blocks, chips, rows, cols)
    parts = jnp.einsum(
        "tzr,tbc->bzrc", acts, cots.reshape(2 * tokens, blocks, cols), preferred_element_type=F32
    ).astype(BF16).reshape(blocks * chips, rows, cols)
    total = lax.psum_scatter(parts, ("blk", "chip"), scatter_dimension=0, tiled=False)
    count = tokens * blocks * chips * 2
    grad_weight = (total.astype(F32) * (1.0 / math.sqrt(count))).astype(BF16)
    full = weight.transpose(1, 2, 0, 3).reshape(chips * rows, columns)
    keys = jnp.dot(acts.reshape(2 * tokens, chips * rows), full, preferred_element_type=F32)
    key_values = (keys[:tokens] + swapped(keys[tokens:])).astype(BF16)
    inputs = lax.dot_general(
        cots, full, (((1,), (1,)), ((), ())), preferred_element_type=F32
    ).astype(BF16).reshape(2 * tokens, chips, rows)
    near, far = inputs[:tokens], swapped(inputs[tokens:])
    low = jnp.where(core == 0, near, far)
    high = jnp.where(core == 0, far, near)
    grad_input = jnp.stack([low, high], 2).reshape(tokens, features)
    return (key_values, grad_input, grad_weight)


def solution(mesh):
    blocks, shards = mesh.shape["blk"], mesh.shape["shard"]
    split = Mesh(mesh.devices.reshape(blocks, shards // 2, 2), AXES)
    by_token = P(AXES, None)
    by_piece = P(("chip", "core"), "blk")
    return jax.shard_map(
        by_hops if (blocks, shards) == (4, 8) else by_collectives,
        mesh=split,
        in_specs=(by_token, by_token, by_piece),
        out_specs=(by_token, by_token, by_piece),
        check_vma=False,
    )
```

```python
import math

import jax
import jax.numpy as jnp
from jax import lax
from jax.experimental import pallas as pl
from jax.experimental.pallas import tpu as pltpu
from jax.sharding import Mesh, PartitionSpec as P

F32, BF16 = jnp.float32, jnp.bfloat16
AXES = ("blk", "chip", "core")
SHRINK = 1000
MIB = 2**20
GATE = 10**7
ONCE = pl.Buffered(1)


def hops(move):
    pairs = []
    for blk in range(4):
        for z in range(4):
            for core in range(2):
                to = move(blk, z, core)
                if to is not None:
                    pairs.append(((blk * 4 + z) * 2 + core, (to[0] * 4 + to[1]) * 2 + to[2]))
    return pairs


def middle(z):
    return z in (1, 2)


SWAP = hops(lambda b, z, c: (b, z, 1 - c))
FLIP_A = hops(lambda b, z, c: (b ^ (1 + c), z, c))
FLIP_B = hops(lambda b, z, c: (b ^ (2 - c), z, c))
PAIR = hops(lambda b, z, c: (b, z ^ 1, c))
MID = hops(lambda b, z, c: (b, z ^ 3, c) if middle(z) else None)
OUT = hops(lambda b, z, c: (b, z ^ 1, c) if middle(z) else None)
IN = hops(lambda b, z, c: (b, z ^ 1, c) if not middle(z) else None)


def after(array, *others):
    return lax.optimization_barrier((array, *others))[0]


def sent(array, pairs):
    return lax.ppermute(array, AXES, pairs)


def column_block(place, a, b):
    core = place[1]
    return place[2] ^ (a * (1 + core)) ^ (b * (2 - core))


def cost(flops, moved, shrink=SHRINK):
    return pl.CostEstimate(flops=flops // shrink, bytes_accessed=moved // shrink, transcendentals=0)


def gate(place, *arrays):
    def kernel(*refs):
        for i in range(3):
            refs[-1][i] = refs[0][i]

    return pl.pallas_call(
        kernel,
        in_specs=[pl.BlockSpec(memory_space=pltpu.SMEM)]
        + [pl.BlockSpec(memory_space=pl.ANY)] * len(arrays),
        out_specs=pl.BlockSpec(memory_space=pltpu.SMEM),
        out_shape=jax.ShapeDtypeStruct(place.shape, place.dtype),
        compiler_params=pltpu.CompilerParams(vmem_limit_bytes=MIB),
        cost_estimate=cost(0, GATE, 1),
        name="gate",
    )(place, *arrays)


def first_term_kernel(place, mine, other, cot_mine, cot_other, keep, send, cots, turned):
    tokens, cols = cot_mine.shape[0], cot_mine.shape[1] // 4

    @pl.when(pl.program_id(0) == 0)
    def _():
        for b in (0, 1):
            for a in (0, 1):
                at = pl.ds(pl.multiple_of(column_block(place, a, b) * cols, cols), cols)
                to = slice((2 * b + a) * cols, (2 * b + a + 1) * cols)
                for array, half in ((cot_mine, slice(0, tokens)), (cot_other, slice(tokens, None))):
                    piece = array[:, at]
                    cots[half, to] = piece
                    turned[to, half] = piece.T

    tall = jnp.concatenate([mine[...], other[...]], 0)
    for b, out in ((1, send), (0, keep)):
        part = turned[2 * b * cols : (2 * b + 2) * cols]
        out[...] = jnp.dot(part, tall, preferred_element_type=F32).astype(BF16).reshape(out.shape)


def first_terms(place, activations, other, cot_mine, cot_other, rows):
    tokens, columns = cot_mine.shape
    part, cols = rows // 2, columns // 4
    mine = pl.BlockSpec((tokens, part), lambda r, s: (0, 2 * (2 * (s[0] ^ 3) + s[1]) + r))
    piece = pl.BlockSpec((2, cols, part), lambda r, s: (0, 0, r))

    held = pl.BlockSpec((tokens, columns), lambda r, s: (0, 0), pipeline_mode=ONCE)

    def whole(*shape):
        return pl.BlockSpec(shape, lambda r, s: (0, 0))

    return pl.pallas_call(
        first_term_kernel,
        grid_spec=pltpu.PrefetchScalarGridSpec(
            num_scalar_prefetch=1,
            grid=(2,),
            in_specs=[mine, mine, held, held],
            out_specs=[piece, piece, whole(2 * tokens, columns), whole(columns, 2 * tokens)],
        ),
        out_shape=[jax.ShapeDtypeStruct((2, cols, rows), BF16)] * 2
        + [
            jax.ShapeDtypeStruct((2 * tokens, columns), BF16),
            jax.ShapeDtypeStruct((columns, 2 * tokens), BF16),
        ],
        compiler_params=pltpu.CompilerParams(vmem_limit_bytes=22 * MIB),
        cost_estimate=cost(4 * tokens * rows * columns, 4 * tokens * rows + 4 * rows * columns),
        name="terms",
    )(place, activations, other, cot_mine, cot_other)


def term_kernel(place, mine, other, turned, *outs):
    rows = turned.shape[0] // 2
    for i in range(3):

        @pl.when(pl.program_id(0) == i)
        def _():
            tall = jnp.concatenate([mine[...], other[...]], 0)
            for b in (1, 0):
                out = outs[3 * b + i]
                part = turned[b * rows : (b + 1) * rows]
                out[...] = (
                    jnp.dot(part, tall, preferred_element_type=F32).astype(BF16).reshape(out.shape)
                )


def terms(place, activations, other, turned, rows):
    columns, tokens = turned.shape[0], activations.shape[0]
    part, cols = rows // 2, columns // 4
    mine = pl.BlockSpec((tokens, part), lambda i, r, s: (0, 2 * (2 * (s[0] ^ (2 - i)) + s[1]) + r))
    pieces = [
        pl.BlockSpec((2, cols, part), lambda i, r, s, n=n: (0, 0, jnp.clip(2 * (i - n) + r, 0, 1)))
        for n in range(3)
    ]
    return pl.pallas_call(
        term_kernel,
        grid_spec=pltpu.PrefetchScalarGridSpec(
            num_scalar_prefetch=1,
            grid=(3, 2),
            in_specs=[
                mine,
                mine,
                pl.BlockSpec(turned.shape, lambda i, r, s: (0, 0), pipeline_mode=ONCE),
            ],
            out_specs=pieces * 2,
        ),
        out_shape=[jax.ShapeDtypeStruct((2, cols, rows), BF16)] * 6,
        compiler_params=pltpu.CompilerParams(vmem_limit_bytes=18 * MIB),
        cost_estimate=cost(12 * tokens * rows * columns, 12 * tokens * rows + 12 * rows * columns),
        name="terms",
    )(place, activations, other, turned)


def project_kernel(place, acts, other, cots, here, there, *refs, first, last):
    near, far, *keys = refs[0 if first else 2 : -1]
    acc = refs[-1]
    tokens, cols = acts.shape[0], here.shape[2]
    step = pl.program_id(0)

    weight = jnp.concatenate([here[0], here[1], there[0], there[1]], 1)
    total = lax.dot_general(
        cots[...], weight, (((1,), (1,)), ((), ())), preferred_element_type=F32
    ).astype(BF16)
    near[...] = total[:tokens]
    far[...] = total[tokens:]
    tall = jnp.concatenate([acts[...], other[...]], 0)
    sums = jnp.dot(tall, weight, preferred_element_type=F32)

    @pl.when(step == 0)
    def _():
        acc[...] = sums if first else refs[0][...] + sums

    @pl.when(step == 1)
    def _():
        if last:
            for b in (0, 1):
                for a in (0, 1):
                    at = pl.ds(pl.multiple_of(column_block(place, a, b) * cols, cols), cols)
                    to = slice((2 * b + a) * cols, (2 * b + a + 1) * cols)
                    keys[0][:, at] = acc[:tokens, to] + sums[:tokens, to]
                    keys[1][:, at] = acc[tokens:, to] + sums[tokens:, to]
        else:
            keys[0][...] = acc[...] + sums


def projected(place, k, activations, other, cots, here, there, so_far=None):
    tokens, columns = activations.shape[0], cots.shape[1]
    _, rows, cols = here.shape
    part = rows // 2
    first, last = k == 0, k == 3

    def whole(*shape):
        return pl.BlockSpec(shape, lambda r, s: (0, 0))

    held = pl.BlockSpec((2 * tokens, columns), lambda r, s: (0, 0), pipeline_mode=ONCE)

    mine = pl.BlockSpec(
        (tokens, part), lambda r, s: (0, 2 * (2 * (s[0] ^ k) + s[1]) + r)
    )
    piece = pl.BlockSpec((2, part, cols), lambda r, s: (0, r, 0))
    one = jax.ShapeDtypeStruct((tokens, columns), F32)
    return pl.pallas_call(
        lambda *refs: project_kernel(*refs, first=first, last=last),
        grid_spec=pltpu.PrefetchScalarGridSpec(
            num_scalar_prefetch=1,
            grid=(2,),
            in_specs=[mine, mine, held, piece, piece]
            + ([] if first else [held, pl.BlockSpec(memory_space=pl.ANY)]),
            out_specs=[mine, pl.BlockSpec((tokens, part), lambda r, s: (0, r))]
            + ([whole(tokens, columns)] * 2 if last else [whole(2 * tokens, columns)]),
            scratch_shapes=[pltpu.VMEM((2 * tokens, columns), F32)],
        ),
        out_shape=[
            jax.ShapeDtypeStruct(activations.shape, BF16),
            jax.ShapeDtypeStruct((tokens, rows), BF16),
        ]
        + ([one, one] if last else [jax.ShapeDtypeStruct((2 * tokens, columns), F32)]),
        input_output_aliases={} if first else {7: 0},
        compiler_params=pltpu.CompilerParams(vmem_limit_bytes=28 * MIB),
        cost_estimate=cost(
            8 * tokens * rows * columns,
            8 * tokens * rows + 2 * rows * columns + 8 * tokens * columns,
        ),
        name="project",
    )(
        place, activations, other, cots, here, there,
        *([] if first else [so_far[2], so_far[0]]),
    )


def lay_kernel(place, *refs):
    for k in range(3):

        @pl.when(pl.program_id(0) == k)
        def _():
            refs[-1][...] = refs[k][...]


def laid(place, whole, parts):
    tokens, rows = parts[0].shape
    return pl.pallas_call(
        lay_kernel,
        grid_spec=pltpu.PrefetchScalarGridSpec(
            num_scalar_prefetch=1,
            grid=(3,),
            in_specs=[pl.BlockSpec((tokens, rows), lambda i, s: (0, 0), pipeline_mode=ONCE)] * 3
            + [pl.BlockSpec(memory_space=pl.ANY)],
            out_specs=pl.BlockSpec((tokens, rows), lambda i, s: (0, 2 * (s[0] ^ i) + 1 - s[1])),
        ),
        out_shape=jax.ShapeDtypeStruct(whole.shape, BF16),
        input_output_aliases={4: 0},
        compiler_params=pltpu.CompilerParams(vmem_limit_bytes=8 * MIB),
        cost_estimate=cost(0, 12 * tokens * rows),
        name="lay",
    )(place, *parts, whole)


def finish_kernel(place, got, near, far, last, arrived, whole, out, keys, weight, *, scale):
    out[...] = got[...]
    keys[...] = (near[...] + far[...]).astype(BF16)
    weight[...] = ((last[...] + arrived[...].astype(F32)) * scale).T.astype(BF16)


def finished(place, whole, got, keys_near, keys_far, last, arrived, scale):
    tokens, rows = got.shape
    cols, columns = last.shape[0], keys_near.shape[1]
    part, some = rows // 2, columns // 2
    wide = pl.BlockSpec((tokens, some), lambda r, s: (0, r))
    flat = pl.BlockSpec((cols, part), lambda r, s: (0, r))
    return pl.pallas_call(
        lambda *refs: finish_kernel(*refs, scale=scale),
        grid_spec=pltpu.PrefetchScalarGridSpec(
            num_scalar_prefetch=1,
            grid=(2,),
            in_specs=[
                pl.BlockSpec((tokens, part), lambda r, s: (0, r)),
                wide,
                wide,
                flat,
                flat,
                pl.BlockSpec(memory_space=pl.ANY),
            ],
            out_specs=[
                pl.BlockSpec((tokens, part), lambda r, s: (0, 2 * (2 * (s[0] ^ 3) + 1 - s[1]) + r)),
                wide,
                pl.BlockSpec((part, cols), lambda r, s: (r, 0)),
            ],
        ),
        out_shape=[
            jax.ShapeDtypeStruct(whole.shape, BF16),
            jax.ShapeDtypeStruct((tokens, columns), BF16),
            jax.ShapeDtypeStruct((rows, cols), BF16),
        ],
        input_output_aliases={6: 0},
        compiler_params=pltpu.CompilerParams(vmem_limit_bytes=12 * MIB),
        cost_estimate=cost(0, 4 * tokens * rows + 10 * tokens * columns),
        name="finish",
    )(place, got, keys_near, keys_far, last, arrived, whole)


def added(*arrays):
    total = arrays[0].astype(F32)
    for array in arrays[1:]:
        total = total + array.astype(F32)
    return total.astype(BF16)


def by_hops(activations, cotangent, kv_weight):
    rows = kv_weight.shape[0]
    tokens = activations.shape[0]
    place = jnp.stack([lax.axis_index(name) for name in ("chip", "core", "blk")]).astype(jnp.int32)

    other, cot_other = sent(activations, SWAP), sent(cotangent, SWAP)
    base = jnp.stack([kv_weight, sent(kv_weight, FLIP_A)])
    one, mid = sent(base, PAIR), sent(base, MID)
    base_b = sent(base, FLIP_B)

    keep3, send3, cots, turned = first_terms(
        place, activations, other, cotangent, cot_other, rows
    )
    got3 = sent(send3, FLIP_B)
    keep2, keep1, keep0, send2, send1, send0 = terms(place, activations, other, turned, rows)
    first = gate(place, after(mid, keep0), one, base_b)

    sum3 = added(after(keep3, first), got3)
    far = sent(sum3, IN)
    two_mid = sent(after(one, first, sum3), MID)
    two_end = sent(after(mid, sum3), OUT)
    got2 = sent(send2, FLIP_B)
    sum2 = added(keep2, got2)
    one_b = sent(after(one, sum3), FLIP_B)
    got1 = sent(after(send1, sum2), FLIP_B)
    whole, out0, keys = projected(
        first, 0, after(activations, keep0, sum3, sum2), other, cots, base, base_b
    )

    sum2_far = added(after(sum2, out0), far)
    mid_far = sent(sum2_far, MID)
    near = sent(after(sum2, sum2_far, two_mid, two_end, one_b), IN)
    three_end = sent(after(two_mid, sum2_far), OUT)
    two = after(two_mid, sum2_far) + two_end
    two_b = sent(two, FLIP_B)
    sum1 = added(keep1, got1)
    got0 = sent(after(send0, sum1), FLIP_B)
    whole, out1, keys = projected(
        place, 1, after(activations, sum2_far, sum1), other, cots, one, one_b, (whole, None, keys)
    )

    sum3_near = added(sum3, near)
    sum_mid = sent(sum3_near, MID)
    sum1_far = added(after(sum1, sum3_near, out1), mid_far)
    sum_one = sent(after(sum1_far, three_end, two_b), PAIR)
    three = after(mid, sum1_far) + three_end
    three_b = sent(three, FLIP_B)
    sum0 = added(keep0, got0)
    whole, out2, keys = projected(
        place,
        2,
        after(activations, sum1_far, sum0),
        other,
        cots,
        two,
        two_b,
        (whole, None, keys),
    )
    whole, out3, keys, keys_far = projected(
        place, 3, after(activations, out2), other, cots, three, three_b, (whole, None, keys)
    )
    sum_one = after(sum_one, out3)
    last = [
        sum0[a].astype(F32) + sum_mid[a].astype(F32) + sum_one[a].astype(F32) for a in (0, 1)
    ]
    over = last[1].astype(BF16)
    whole = laid(
        place,
        whole,
        (sent(out0, SWAP), sent(out1, SWAP), sent(out2, SWAP)),
    )
    grad_input, key_values, grad_weight = finished(
        place,
        whole,
        sent(out3, SWAP),
        keys,
        sent(keys_far, SWAP),
        last[0],
        sent(over, FLIP_A),
        1.0 / math.sqrt(32 * tokens),
    )
    return (key_values, grad_input, grad_weight)


def swapped(array):
    return lax.ppermute(array, "core", [(0, 1), (1, 0)])


def by_collectives(activations, cotangent, kv_weight):
    blocks, chips = lax.axis_size("blk"), lax.axis_size("chip")
    core = lax.axis_index("core")
    tokens, features = activations.shape
    rows, cols = kv_weight.shape
    columns = cotangent.shape[1]
    by_core = activations.reshape(tokens, chips, 2, rows)
    mine = lax.dynamic_index_in_dim(by_core, core, 2, keepdims=False)
    other = lax.dynamic_index_in_dim(by_core, 1 - core, 2, keepdims=False)
    acts = jnp.concatenate([mine, swapped(other)], 0)
    cots = jnp.concatenate([cotangent, swapped(cotangent)], 0)
    weight = lax.all_gather(kv_weight, ("blk", "chip"), axis=0, tiled=False)
    weight = weight.reshape(blocks, chips, rows, cols)
    parts = jnp.einsum(
        "tzr,tbc->bzrc", acts, cots.reshape(2 * tokens, blocks, cols), preferred_element_type=F32
    ).astype(BF16).reshape(blocks * chips, rows, cols)
    total = lax.psum_scatter(parts, ("blk", "chip"), scatter_dimension=0, tiled=False)
    count = tokens * blocks * chips * 2
    grad_weight = (total.astype(F32) * (1.0 / math.sqrt(count))).astype(BF16)
    full = weight.transpose(1, 2, 0, 3).reshape(chips * rows, columns)
    keys = jnp.dot(acts.reshape(2 * tokens, chips * rows), full, preferred_element_type=F32)
    key_values = (keys[:tokens] + swapped(keys[tokens:])).astype(BF16)
    inputs = lax.dot_general(
        cots, full, (((1,), (1,)), ((), ())), preferred_element_type=F32
    ).astype(BF16).reshape(2 * tokens, chips, rows)
    near, far = inputs[:tokens], swapped(inputs[tokens:])
    low = jnp.where(core == 0, near, far)
    high = jnp.where(core == 0, far, near)
    grad_input = jnp.stack([low, high], 2).reshape(tokens, features)
    return (key_values, grad_input, grad_weight)


def solution(mesh):
    blocks, shards = mesh.shape["blk"], mesh.shape["shard"]
    split = Mesh(mesh.devices.reshape(blocks, shards // 2, 2), AXES)
    by_token = P(AXES, None)
    by_piece = P(("chip", "core"), "blk")
    return jax.shard_map(
        by_hops if (blocks, shards) == (4, 8) else by_collectives,
        mesh=split,
        in_specs=(by_token, by_token, by_piece),
        out_specs=(by_token, by_token, by_piece),
        check_vma=False,
    )
```
